128 devices in a mesh: seq: 32 (over z, y, x_hi), tp: 4 (over x_lo, core).
Axes of the slice: x: 4 (x_hi: 2, x_lo: 2; x = x_hi * 2 + x_lo), y: 4, z: 4, core: 2. Of those that a mesh axis runs over, the one named last changes fastest.
Arguments:
- residual: bfloat16 [16384, 4096], P(('seq', 'tp')), may hold values from -6 to 6
- norm_gain: float32 [4096], replicated, may hold values from 0.1 to 1.9
- query_weight: bfloat16 [4096, 2048], P('seq', 'tp'), may hold values from -0.109375 to 0.109375
- keyval_weight: bfloat16 [896, 2, 2048], P('seq', None, 'tp'), may hold values from -0.2338536 to 0.2338536
- output_weight: bfloat16 [4096, 2048], P('seq', 'tp'), may hold values from -0.125 to 0.125
- neighbours: bfloat16 [512, 128, 896], P(('seq', 'tp')), may hold values from -6 to 6
- cotangent: bfloat16 [16384, 4096], P(('seq', 'tp')), may hold values from -6 to 6
Outputs:
- layer_output: bfloat16 [16384, 4096], P(('seq', 'tp'))
- residual_grad: bfloat16 [16384, 4096], P(('seq', 'tp'))
- neighbour_grad: bfloat16 [512, 128, 896], P(('seq', 'tp'))
- gain_grad: float32 [4096], replicated
- query_grad: float32 [4096, 2048], P('seq', 'tp')
- keyval_grad: float32 [896, 2, 2048], P('seq', None, 'tp')
- output_grad: float32 [4096, 2048], P('seq', 'tp')
The draws below stay inside these ranges and needn't reach their ends.
All inputs are finite; a program needn't handle non-finite values.
Results may differ from the reference program's by a relative error of at most 0.03.
Values may be sent and summed in bfloat16 or wider, within the bound.
No kernel may reach another device: no remote copies, remote signals or barrier semaphores. Data moves between devices by JAX's collectives and lax.ppermute only.
A program may use at most 192 MiB of HBM per device.

```python
import math
import jax
import jax.numpy as jnp
from jax import lax

D = 4096
HEADS = 16
HEAD_DIM = 128
EW = 896
SPAN = 64
K_NB = 2
R = 128
LENGTH = 2048
TOK_DEV = 512
TOKENS = 16384
SPANS = 256
NEIGH = 512
HD = 2048
HD_TP = 512
NB_GROUP = 16
N_SEQ = 32
N_TP = 4


def draw_residual(key, part):
    own_key = jax.random.fold_in(key, 11)
    values = jax.random.truncated_normal(own_key, -6.0, 6.0, (TOKENS, D), jnp.float32)
    return values.astype(jnp.bfloat16)


def draw_query_weight(key, part):
    own_key = jax.random.fold_in(key, 12)
    values = jax.random.truncated_normal(own_key, -6.0, 6.0, (D, HD), jnp.float32) * D ** (-0.5)
    return values.astype(jnp.bfloat16)


def draw_keyval_weight(key, part):
    own_key = jax.random.fold_in(key, 13)
    values = jax.random.truncated_normal(own_key, -6.0, 6.0, (EW, 2, HD), jnp.float32) * EW ** (-0.5)
    return values.astype(jnp.bfloat16)


def draw_neighbours(key, part):
    own_key = jax.random.fold_in(key, 14)
    values = jax.random.truncated_normal(own_key, -6.0, 6.0, (NEIGH, R, EW), jnp.float32)
    return values.astype(jnp.bfloat16)


def level_of(rng, shape, cuts, low, high):
    def one(axis_at, shards_of):
        draws = jax.random.uniform(jax.random.fold_in(jax.random.fold_in(rng, 6), axis_at), (shards_of,), jnp.float32, low / len(cuts), high / len(cuts))
        return jnp.repeat(jnp.exp(draws), shape[axis_at] // shards_of).reshape((-1,) + (1,) * (len(shape) - axis_at - 1))

    loudness = one(*cuts[0])
    for cut in cuts[1:]:
        loudness = loudness * one(*cut)
    return loudness


def scatter_about(rng, shape, width, most, split=(), dtype=jnp.bfloat16):
    drawn = width * jax.random.normal(rng, shape, jnp.float32)
    if split:
        drawn = drawn * level_of(rng, shape, split, -0.22, 0.18)
    return jnp.clip(drawn, -most, most).astype(dtype)


def setup_inputs(seed: int = 0) -> dict:
    key_list = jax.random.split(jax.random.key(seed), 8)
    return {
        "residual": draw_residual(jax.random.fold_in(key_list[7], 71), 0),
        "norm_gain": jnp.clip(1.0 + 0.18 * jax.random.normal(key_list[1], (D,), jnp.float32), 0.1, 1.9),
        "query_weight": draw_query_weight(jax.random.fold_in(key_list[7], 71), 0),
        "keyval_weight": draw_keyval_weight(jax.random.fold_in(key_list[7], 71), 0),
        "output_weight": scatter_about(key_list[4], (D, HD), HD ** -0.5, 0.125, ((0, 32), (1, 4))),
        "neighbours": draw_neighbours(jax.random.fold_in(key_list[7], 71), 0),
        "cotangent": scatter_about(key_list[6], (TOKENS, D), 1.0, 6.0, ((0, 128),)),
    }


EPSILON = 1e-06

def span_forward(query, keys_prev, keys_cur, values_prev, values_cur, prev_rows, usable):
    factor = 1.0 / math.sqrt(query.shape[-1])
    prev_mask = prev_rows[None, None, :, None]
    score_prev = jnp.einsum('cqhd,ckhd->chqk', query, keys_prev, preferred_element_type=jnp.float32)
    score_cur = jnp.einsum('cqhd,ckhd->chqk', query, keys_cur, preferred_element_type=jnp.float32)
    scores = jnp.where(prev_mask, score_prev, score_cur) * factor
    row_peak = lax.optimization_barrier(jnp.max(scores, axis=-1, keepdims=True))
    exponent = jnp.exp(scores - row_peak)
    probabilities = exponent / lax.optimization_barrier(jnp.sum(exponent, axis=-1, keepdims=True))
    weights = probabilities.astype(jnp.bfloat16)
    zero_weight = jnp.zeros_like(weights)
    weights_prev = jnp.where(prev_mask, weights, zero_weight)
    weights_cur = jnp.where(prev_mask, zero_weight, weights)
    attended = jnp.einsum('chqk,ckhd->cqhd', weights_prev, values_prev, preferred_element_type=jnp.float32)
    attended = attended + jnp.einsum('chqk,ckhd->cqhd', weights_cur, values_cur, preferred_element_type=jnp.float32)
    attended = attended * usable[:, :, None, None]
    return (attended, probabilities, weights_prev, weights_cur)

def span_backward(upstream, query, keys_prev, keys_cur, values_prev, values_cur, prev_rows, usable, probabilities, weights_prev, weights_cur):
    factor = 1.0 / math.sqrt(query.shape[-1])
    prev_mask = prev_rows[None, None, :, None]
    masked_grad = jnp.where(usable[:, :, None, None] > 0, upstream, jnp.zeros_like(upstream))
    grad_prev = jnp.einsum('cqhd,ckhd->chqk', masked_grad, values_prev, preferred_element_type=jnp.float32)
    grad_cur = jnp.einsum('cqhd,ckhd->chqk', masked_grad, values_cur, preferred_element_type=jnp.float32)
    weight_grad = jnp.where(prev_mask, grad_prev, grad_cur)
    inner = lax.optimization_barrier(jnp.sum(weight_grad * probabilities, axis=-1, keepdims=True))
    score_grad = (probabilities * (weight_grad - inner) * factor).astype(jnp.bfloat16)
    zero_score = jnp.zeros_like(score_grad)
    score_prev_grad = jnp.where(prev_mask, score_grad, zero_score)
    score_cur_grad = jnp.where(prev_mask, zero_score, score_grad)
    query_grad = jnp.einsum('chqk,ckhd->cqhd', score_prev_grad, keys_prev, preferred_element_type=jnp.float32)
    query_grad = query_grad + jnp.einsum('chqk,ckhd->cqhd', score_cur_grad, keys_cur, preferred_element_type=jnp.float32)
    keys_prev_grad = jnp.einsum('chqk,cqhd->ckhd', score_prev_grad, query, preferred_element_type=jnp.float32)
    keys_cur_grad = jnp.einsum('chqk,cqhd->ckhd', score_cur_grad, query, preferred_element_type=jnp.float32)
    values_prev_grad = jnp.einsum('chqk,cqhd->ckhd', weights_prev, masked_grad, preferred_element_type=jnp.float32)
    values_cur_grad = jnp.einsum('chqk,cqhd->ckhd', weights_cur, masked_grad, preferred_element_type=jnp.float32)
    return (query_grad, keys_prev_grad, keys_cur_grad, values_prev_grad, values_cur_grad)

def round_trip(values):
    return lax.optimization_barrier(values.astype(jnp.bfloat16)).astype(jnp.float32)

def reference(residual, norm_gain, query_weight, keyval_weight, output_weight, neighbours, cotangent):
    residual_wide = residual.astype(jnp.float32)
    mean_square = lax.optimization_barrier(jnp.mean(residual_wide * residual_wide, axis=-1, keepdims=True))
    inverse_rms = lax.rsqrt(mean_square + EPSILON)
    scaled = residual_wide * inverse_rms
    normed = (scaled * norm_gain).astype(jnp.bfloat16)
    query = jnp.dot(normed, query_weight, preferred_element_type=jnp.float32).astype(jnp.bfloat16)
    keyvals = jnp.einsum('nre,etc->nrtc', neighbours, keyval_weight, preferred_element_type=jnp.float32).astype(jnp.bfloat16)
    span_query = query.reshape(SPANS, SPAN, HEADS, HEAD_DIM)
    span_keyvals = keyvals.reshape(SPANS, K_NB * R, 2, HEADS, HEAD_DIM)
    prev_keyvals = jnp.concatenate([jnp.zeros_like(span_keyvals[:1]), span_keyvals[:-1]], axis=0)
    prev_rows = jnp.arange(SPAN) < SPAN - 1
    positions = jnp.arange(TOKENS)
    usable = (positions % LENGTH >= SPAN - 1).astype(jnp.float32).reshape(SPANS, SPAN)
    attended_wide, probabilities, weights_prev, weights_cur = span_forward(span_query, prev_keyvals[:, :, 0], span_keyvals[:, :, 0], prev_keyvals[:, :, 1], span_keyvals[:, :, 1], prev_rows, usable)
    attended = attended_wide.astype(jnp.bfloat16).reshape(TOKENS, HD)
    mixed = jnp.zeros((TOKENS, D), jnp.float32)
    for column_block in range(N_TP):
        lower = column_block * HD_TP
        upper = lower + HD_TP
        mixed = mixed + round_trip(jnp.dot(attended[:, lower:upper], output_weight[:, lower:upper].T, preferred_element_type=jnp.float32))
    layer_output = (residual_wide + mixed).astype(jnp.bfloat16)
    attended_grad = jnp.dot(cotangent, output_weight, preferred_element_type=jnp.float32).astype(jnp.bfloat16)
    query_grad_wide, keys_prev_grad, keys_cur_grad, values_prev_grad, values_cur_grad = span_backward(attended_grad.reshape(SPANS, SPAN, HEADS, HEAD_DIM), span_query, prev_keyvals[:, :, 0], span_keyvals[:, :, 0], prev_keyvals[:, :, 1], span_keyvals[:, :, 1], prev_rows, usable, probabilities, weights_prev, weights_cur)
    current_grad = jnp.stack([keys_cur_grad, values_cur_grad], axis=2)
    previous_grad = jnp.stack([keys_prev_grad, values_prev_grad], axis=2)
    keyval_total = current_grad + jnp.concatenate([previous_grad[1:], jnp.zeros_like(previous_grad[:1])], axis=0)
    keyval_back = keyval_total.astype(jnp.bfloat16).reshape(NEIGH, R, 2, HD)
    query_back = query_grad_wide.astype(jnp.bfloat16).reshape(TOKENS, HD)
    feature_grad = jnp.zeros((TOKENS, D), jnp.float32)
    neighbour_total = jnp.zeros((NEIGH, R, EW), jnp.float32)
    for column_block in range(N_TP):
        lower = column_block * HD_TP
        upper = lower + HD_TP
        feature_grad = feature_grad + round_trip(jnp.dot(query_back[:, lower:upper], query_weight[:, lower:upper].T, preferred_element_type=jnp.float32))
        neighbour_total = neighbour_total + round_trip(jnp.einsum('nrtc,etc->nre', keyval_back[:, :, :, lower:upper], keyval_weight[:, :, lower:upper], preferred_element_type=jnp.float32))
    neighbour_grad = neighbour_total.astype(jnp.bfloat16)
    gained = feature_grad * norm_gain
    residual_grad = (inverse_rms * (gained - scaled * lax.optimization_barrier(jnp.mean(gained * scaled, axis=-1, keepdims=True))) + cotangent.astype(jnp.float32)).astype(jnp.bfloat16)
    gain_grad = lax.optimization_barrier(jnp.sum(feature_grad * scaled, axis=0))

    def add_group(carry, pieces):
        normed_part, query_part, cotangent_part, attended_part, neighbour_part, keyval_part = pieces
        query_term = jnp.einsum('td,th->dh', normed_part, query_part, preferred_element_type=jnp.float32)
        output_term = jnp.einsum('td,th->dh', cotangent_part, attended_part, preferred_element_type=jnp.float32)
        keyval_term = jnp.einsum('nre,nrtc->etc', neighbour_part, keyval_part, preferred_element_type=jnp.float32)
        return ((carry[0] + round_trip(query_term), carry[1] + round_trip(output_term), carry[2] + round_trip(keyval_term)), None)
    initial = (jnp.zeros((D, HD), jnp.float32), jnp.zeros((D, HD), jnp.float32), jnp.zeros((EW, 2, HD), jnp.float32))
    pieces = (normed.reshape(N_SEQ, TOK_DEV, D), query_back.reshape(N_SEQ, TOK_DEV, HD), cotangent.reshape(N_SEQ, TOK_DEV, D), attended.reshape(N_SEQ, TOK_DEV, HD), neighbours.reshape(N_SEQ, NB_GROUP, R, EW), keyval_back.reshape(N_SEQ, NB_GROUP, R, 2, HD))
    totals, unused_stack = lax.scan(add_group, initial, pieces)
    query_grad, output_grad, keyval_grad = totals
    return (layer_output, residual_grad, neighbour_grad, gain_grad, query_grad, keyval_grad, output_grad)
```

```python
import functools
import math

import jax
import jax.numpy as jnp
from jax import lax
from jax.experimental import pallas as pl
from jax.experimental.pallas import tpu as pltpu
from jax.sharding import PartitionSpec as P

HEAD_DIM = 128
SPAN = 64
K_NB = 2
R = 128
LENGTH = 2048
EPSILON = 1e-06
LANES = 128

Z_NEAR, Z_WRAP = 8, 24
Y_NEAR, Y_WRAP = 2, 6
X_HIGH = 1
X_LOW, CORE = 2, 1


def seq_swap(value, mask):
    count = lax.axis_size("seq")
    return lax.ppermute(value, "seq", [(i, i ^ mask) for i in range(count)])


def tp_swap(value, mask):
    count = lax.axis_size("tp")
    return lax.ppermute(value, "tp", [(i, i ^ mask) for i in range(count)])


def f32_sum(*terms):
    total = terms[0].astype(jnp.float32)
    for term in terms[1:]:
        total = total + term.astype(jnp.float32)
    return total


def ring_gather(block, near, wrap):
    half = block.shape[0] // 2
    from_near, from_wrap = seq_swap(block, near), seq_swap(block, wrap)
    low, high = seq_swap(from_wrap[:half], near), seq_swap(from_near[half:], wrap)
    return jnp.concatenate([block, from_near, low, high, from_wrap], axis=0)


def ring_scatter(parts, near, wrap):
    rows = parts.shape[0] // 4
    half = rows // 2
    own, to_near, far, to_wrap = [parts[i * rows : (i + 1) * rows] for i in range(4)]
    low, high = seq_swap(far[:half], wrap), seq_swap(far[half:], near)
    to_near = jnp.concatenate(
        [f32_sum(to_near[:half], low).astype(jnp.bfloat16), to_near[half:]], axis=0
    )
    to_wrap = jnp.concatenate(
        [to_wrap[:half], f32_sum(to_wrap[half:], high).astype(jnp.bfloat16)], axis=0
    )
    return f32_sum(own, seq_swap(to_near, near), seq_swap(to_wrap, wrap)).astype(jnp.bfloat16)


def gather_seq(shard, y_outer):
    block = jnp.concatenate([shard, seq_swap(shard, X_HIGH)], axis=0)
    if y_outer:
        return ring_gather(ring_gather(block, Z_NEAR, Z_WRAP), Y_NEAR, Y_WRAP)
    return ring_gather(ring_gather(block, Y_NEAR, Y_WRAP), Z_NEAR, Z_WRAP)


def scatter_seq(parts, y_outer):
    if y_outer:
        parts = ring_scatter(ring_scatter(parts, Y_NEAR, Y_WRAP), Z_NEAR, Z_WRAP)
    else:
        parts = ring_scatter(ring_scatter(parts, Z_NEAR, Z_WRAP), Y_NEAR, Y_WRAP)
    rows = parts.shape[0] // 2
    return f32_sum(parts[:rows], seq_swap(parts[rows:], X_HIGH))


def gather_tp(shard):
    across = tp_swap(shard, X_LOW)
    return jnp.concatenate([shard, across, tp_swap(shard, CORE), tp_swap(across, CORE)], axis=0)


def scatter_tp(parts):
    half = parts.shape[0] // 2
    quarter = half // 2
    beside = tp_swap(parts[half:], CORE)
    sent = f32_sum(parts[quarter:half], beside[quarter:]).astype(jnp.bfloat16)
    kept = f32_sum(parts[:quarter], beside[:quarter]).astype(jnp.bfloat16)
    return kept, tp_swap(sent, X_LOW)


def mask_of(place, y_outer):
    if not y_outer:
        return place
    y, z, x = place // 8, (place // 2) % 4, place % 2
    return z * 8 + y * 2 + x


def norm_kernel(seq_ref, residual_ref, gain_ref, cotangent_ref, normed_ref, turned_ref):
    me = seq_ref[0]
    width = residual_ref.shape[1]
    total = jnp.zeros((residual_ref.shape[0], LANES), jnp.float32)
    for place in range(width // LANES):
        piece = residual_ref[:, place * LANES : (place + 1) * LANES].astype(jnp.float32)
        total = total + piece * piece
    inverse_rms = lax.rsqrt(jnp.sum(total, axis=-1, keepdims=True) / width + EPSILON)
    for place in range(width // LANES):
        here = slice(place * LANES, (place + 1) * LANES)
        there = pl.ds(pl.multiple_of((me ^ mask_of(place, True)) * LANES, LANES), LANES)
        scaled = residual_ref[:, there].astype(jnp.float32) * inverse_rms
        normed_ref[:, here] = (scaled * gain_ref[:, there]).astype(jnp.bfloat16)
        there = pl.ds(pl.multiple_of((me ^ mask_of(place, False)) * LANES, LANES), LANES)
        turned_ref[:, here] = cotangent_ref[:, there]


def output_kernel(seq_ref, residual_ref, kept_ref, across_ref, out_ref):
    me = seq_ref[0]
    for place in range(residual_ref.shape[1] // LANES):
        here = slice(place * LANES, (place + 1) * LANES)
        there = pl.ds(pl.multiple_of((me ^ mask_of(place, False)) * LANES, LANES), LANES)
        mixed = kept_ref[:, here].astype(jnp.float32) + across_ref[:, here].astype(jnp.float32)
        out_ref[:, there] = (residual_ref[:, there].astype(jnp.float32) + mixed).astype(
            jnp.bfloat16
        )


def residual_kernel(
    seq_ref, residual_ref, gain_ref, cotangent_ref, kept_ref, across_ref, out_ref, gained_ref
):
    me = seq_ref[0]
    width = residual_ref.shape[1]
    rows = residual_ref.shape[0]
    square = jnp.zeros((rows, LANES), jnp.float32)
    cross = jnp.zeros((rows, LANES), jnp.float32)
    for place in range(width // LANES):
        here = slice(place * LANES, (place + 1) * LANES)
        there = pl.ds(pl.multiple_of((me ^ mask_of(place, True)) * LANES, LANES), LANES)
        feature = kept_ref[:, here].astype(jnp.float32) + across_ref[:, here].astype(jnp.float32)
        gained = feature * gain_ref[:, there]
        piece = residual_ref[:, there].astype(jnp.float32)
        square = square + piece * piece
        cross = cross + gained * piece
        gained_ref[:, there] = gained
    inverse_rms = lax.rsqrt(jnp.sum(square, axis=-1, keepdims=True) / width + EPSILON)
    mean = jnp.sum(cross, axis=-1, keepdims=True) * inverse_rms / width
    for place in range(width // LANES):
        here = slice(place * LANES, (place + 1) * LANES)
        scaled = residual_ref[:, here].astype(jnp.float32) * inverse_rms
        out_ref[:, here] = (
            inverse_rms * (gained_ref[:, here] - scaled * mean)
            + cotangent_ref[:, here].astype(jnp.float32)
        ).astype(jnp.bfloat16)


def whole(shape):
    return pl.BlockSpec(shape, lambda *_: (0,) * len(shape))


def row_call(kernel, seq_index, args, outs, scratch=()):
    return pl.pallas_call(
        kernel,
        grid_spec=pltpu.PrefetchScalarGridSpec(
            num_scalar_prefetch=1,
            grid=(1,),
            in_specs=[whole(arg.shape) for arg in args],
            out_specs=[whole(out.shape) for out in outs],
            scratch_shapes=list(scratch),
        ),
        out_shape=outs,
        compiler_params=pltpu.CompilerParams(vmem_limit_bytes=40 * 1024 * 1024),
    )(seq_index, *args)


def dot(left, right, left_dim, right_dim):
    return lax.dot_general(
        left, right, (((left_dim,), (right_dim,)), ((), ())), preferred_element_type=jnp.float32
    )


def attention_kernel(
    place_ref,
    query_ref,
    query_next_ref,
    up_ref,
    up_next_ref,
    keyval_ref,
    attended_ref,
    query_back_ref,
    keyval_back_ref,
    attended_end_ref,
    query_back_end_ref,
    attended_carry,
    query_carry,
):
    span = pl.program_id(0)
    last = pl.num_programs(0) - 1
    width = query_ref.shape[1]
    rows = lax.broadcasted_iota(jnp.int32, (SPAN, width), 0)
    here = pl.ds(pl.multiple_of(place_ref[span] * SPAN, SPAN), SPAN)
    after = pl.ds(pl.multiple_of(place_ref[span + 1] * SPAN, SPAN), SPAN)

    @pl.when(span == 0)
    def _():
        attended_carry[...] = jnp.zeros_like(attended_carry)
        query_carry[...] = jnp.zeros_like(query_carry)

    def shifted(ref, next_ref):
        first = ref[here, :].astype(jnp.float32)
        second = jnp.where(span == last, next_ref[...], ref[after, :]).astype(jnp.float32)
        joined = jnp.where(rows == SPAN - 1, first, second)
        return pltpu.roll(joined, 1, 0).astype(jnp.bfloat16)

    query = shifted(query_ref, query_next_ref)
    up = shifted(up_ref, up_next_ref)
    factor = 1.0 / math.sqrt(HEAD_DIM)
    attended_parts, query_parts = [], []
    for head in range(width // HEAD_DIM):
        own = slice(head * HEAD_DIM, (head + 1) * HEAD_DIM)
        value_own = slice(width + head * HEAD_DIM, width + (head + 1) * HEAD_DIM)
        q, u = query[:, own], up[:, own]
        keys, values = keyval_ref[:, own], keyval_ref[:, value_own]
        scores = dot(q, keys, 1, 1) * factor
        exponent = jnp.exp(scores - jnp.max(scores, axis=-1, keepdims=True))
        probabilities = exponent / jnp.sum(exponent, axis=-1, keepdims=True)
        weights = probabilities.astype(jnp.bfloat16)
        attended_parts.append(dot(weights, values, 1, 0))
        weight_grad = dot(u, values, 1, 1)
        inner = jnp.sum(weight_grad * probabilities, axis=-1, keepdims=True)
        score_grad = (probabilities * (weight_grad - inner) * factor).astype(jnp.bfloat16)
        query_parts.append(dot(score_grad, keys, 1, 0))
        keyval_back_ref[:, own] = dot(score_grad, q, 0, 0).astype(jnp.bfloat16)
        keyval_back_ref[:, value_own] = dot(weights, u, 0, 0).astype(jnp.bfloat16)
    for parts, carry, out_ref, end_ref in (
        (attended_parts, attended_carry, attended_ref, attended_end_ref),
        (query_parts, query_carry, query_back_ref, query_back_end_ref),
    ):
        turned = pltpu.roll(jnp.concatenate(parts, axis=1), SPAN - 1, 0)
        out_ref[...] = jnp.where(rows == SPAN - 1, turned, carry[...]).astype(jnp.bfloat16)
        carry[...] = turned
        end_ref[...] = jnp.where(rows == SPAN - 1, 0.0, turned).astype(jnp.bfloat16)


def attention(places, query, query_next, up, up_next, keyvals):
    tokens, width = query.shape
    spans = tokens // SPAN
    span_rows = keyvals.shape[0] // spans
    by_place = lambda i, places: (places[i], 0)
    like = lambda array: jax.ShapeDtypeStruct(array.shape, jnp.bfloat16)
    return pl.pallas_call(
        attention_kernel,
        grid_spec=pltpu.PrefetchScalarGridSpec(
            num_scalar_prefetch=1,
            grid=(spans,),
            in_specs=[
                whole(query.shape),
                whole(query_next.shape),
                whole(up.shape),
                whole(up_next.shape),
                pl.BlockSpec((span_rows, keyvals.shape[1]), by_place),
            ],
            out_specs=[
                pl.BlockSpec((SPAN, width), by_place),
                pl.BlockSpec((SPAN, width), by_place),
                pl.BlockSpec((span_rows, keyvals.shape[1]), by_place),
                whole(query_next.shape),
                whole(query_next.shape),
            ],
            scratch_shapes=[
                pltpu.VMEM((SPAN, width), jnp.float32),
                pltpu.VMEM((SPAN, width), jnp.float32),
            ],
        ),
        out_shape=[
            like(query),
            like(query),
            like(keyvals),
            like(query_next),
            like(query_next),
        ],
        compiler_params=pltpu.CompilerParams(vmem_limit_bytes=40 * 1024 * 1024),
    )(places, query, query_next, up, up_next, keyvals)


def per_device(
    residual, norm_gain, query_weight, keyval_weight, output_weight, neighbours, cotangent
):
    me, seq_count = lax.axis_index("seq"), lax.axis_size("seq")
    column, tp_count = lax.axis_index("tp"), lax.axis_size("tp")
    tokens_here, features = residual.shape
    local_width = query_weight.shape[1]
    neighbour_count, _, enc_width = neighbours.shape
    enc_rows = keyval_weight.shape[0]
    group_tokens = tokens_here * tp_count
    spans = group_tokens // SPAN
    seq_index = me.astype(jnp.int32).reshape(1)
    gain_row = norm_gain.reshape(1, features)
    token_shape = jax.ShapeDtypeStruct(residual.shape, jnp.bfloat16)

    flat_neighbours = neighbours.reshape(neighbour_count * R, enc_width)
    group_neighbours = gather_tp(flat_neighbours)
    full_keyval = lax.all_gather(
        keyval_weight.reshape(enc_rows, 2 * local_width), "seq", axis=0, tiled=False
    ).reshape(seq_count * enc_rows, 2 * local_width)
    normed, turned = row_call(
        norm_kernel, seq_index, (residual, gain_row, cotangent), [token_shape, token_shape]
    )
    group_normed = gather_tp(normed)
    group_cotangent = gather_tp(turned)
    full_query = gather_seq(query_weight, True)
    full_output = gather_seq(output_weight, False)

    keyvals = dot(group_neighbours, full_keyval, 1, 0).astype(jnp.bfloat16)
    query = dot(group_normed, full_query, 1, 0).astype(jnp.bfloat16)
    attended_grad = dot(group_cotangent, full_output, 1, 0).astype(jnp.bfloat16)

    block = jnp.arange(spans, dtype=jnp.int32)
    mask = (block // (spans // tp_count)) ^ column.astype(jnp.int32)
    place = ((mask % 2) * 2 + mask // 2) * (spans // tp_count) + block % (spans // tp_count)
    places = jnp.concatenate([place, place[:1]])
    groups = LENGTH // group_tokens
    inside = [i for i in range(seq_count) if i % groups]
    first_row = place[0] * SPAN

    def first_block(value):
        return lax.dynamic_slice(value, (first_row, 0), (SPAN, local_width))

    def from_next(value):
        return lax.ppermute(first_block(value), "seq", [(i, i - 1) for i in inside])

    attended, query_back, keyval_back, attended_end, query_back_end = attention(
        places, query, from_next(query), attended_grad, from_next(attended_grad), keyvals
    )

    def with_previous(value, end):
        arrived = lax.ppermute(end, "seq", [(i - 1, i) for i in inside])
        return lax.dynamic_update_slice(value, first_block(value) + arrived, (first_row, 0))

    attended = with_previous(attended, attended_end)
    query_back = with_previous(query_back, query_back_end)

    keyval_part = dot(group_neighbours, keyval_back, 0, 0).astype(jnp.bfloat16)
    keyval_grad = lax.psum_scatter(
        keyval_part.reshape(seq_count, enc_rows, 2 * local_width),
        "seq",
        scatter_dimension=0,
        tiled=False,
    )
    neighbour_kept, neighbour_across = scatter_tp(
        dot(keyval_back, full_keyval, 1, 1).astype(jnp.bfloat16)
    )
    output_part = dot(group_cotangent, attended, 0, 0).astype(jnp.bfloat16)
    query_part = dot(group_normed, query_back, 0, 0).astype(jnp.bfloat16)
    output_grad = scatter_seq(output_part, False)
    query_grad = scatter_seq(query_part, True)
    mixed_kept, mixed_across = scatter_tp(dot(attended, full_output, 1, 1).astype(jnp.bfloat16))
    feature_kept, feature_across = scatter_tp(
        dot(query_back, full_query, 1, 1).astype(jnp.bfloat16)
    )

    row_sums = jnp.sum(f32_sum(full_query) * f32_sum(query_part), axis=1)
    where_from = mask_of(jnp.arange(seq_count, dtype=jnp.int32) ^ me, True)
    gain_part = jnp.take(row_sums.reshape(seq_count, features // seq_count), where_from, axis=0)
    gain_grad = lax.psum(gain_part.reshape(features), ("seq", "tp")) / norm_gain

    (layer_output,) = row_call(
        output_kernel, seq_index, (residual, mixed_kept, mixed_across), [token_shape]
    )
    (residual_grad,) = row_call(
        residual_kernel,
        seq_index,
        (residual, gain_row, cotangent, feature_kept, feature_across),
        [token_shape],
        [pltpu.VMEM(residual.shape, jnp.float32)],
    )
    neighbour_grad = (
        f32_sum(neighbour_kept, neighbour_across).astype(jnp.bfloat16).reshape(neighbours.shape)
    )
    return (
        layer_output,
        residual_grad,
        neighbour_grad,
        gain_grad,
        query_grad,
        keyval_grad.astype(jnp.float32).reshape(enc_rows, 2, local_width),
        output_grad,
    )


def solution(mesh):
    in_specs = (
        P(("seq", "tp"), None),
        P(),
        P("seq", "tp"),
        P("seq", None, "tp"),
        P("seq", "tp"),
        P(("seq", "tp"), None, None),
        P(("seq", "tp"), None),
    )
    out_specs = (
        P(("seq", "tp"), None),
        P(("seq", "tp"), None),
        P(("seq", "tp"), None, None),
        P(),
        P("seq", "tp"),
        P("seq", None, "tp"),
        P("seq", "tp"),
    )
    return jax.shard_map(
        per_device, mesh=mesh, in_specs=in_specs, out_specs=out_specs, check_vma=False
    )
```

```python
import functools
import math

import jax
import jax.numpy as jnp
from jax import lax
from jax.experimental import pallas as pl
from jax.experimental.pallas import tpu as pltpu
from jax.sharding import PartitionSpec as P

HEAD_DIM = 128
SPAN = 64
K_NB = 2
R = 128
LENGTH = 2048
EPSILON = 1e-06
LANES = 128

Z_NEAR, Z_WRAP = 8, 24
Y_NEAR, Y_WRAP = 2, 6
X_HIGH = 1
X_LOW, CORE = 2, 1


def seq_swap(value, mask):
    count = lax.axis_size("seq")
    return lax.ppermute(value, "seq", [(i, i ^ mask) for i in range(count)])


def tp_swap(value, mask):
    count = lax.axis_size("tp")
    return lax.ppermute(value, "tp", [(i, i ^ mask) for i in range(count)])


def f32_sum(*terms):
    total = terms[0].astype(jnp.float32)
    for term in terms[1:]:
        total = total + term.astype(jnp.float32)
    return total


def fence(values, after):
    count = len(values)
    anywhere = pl.BlockSpec(memory_space=pl.ANY)
    return pl.pallas_call(
        lambda *refs: None,
        in_specs=[anywhere] * (count + len(after)),
        out_specs=[anywhere] * count,
        out_shape=[jax.ShapeDtypeStruct(value.shape, value.dtype) for value in values],
        input_output_aliases={i: i for i in range(count)},
    )(*values, *after)


def narrow_sum(*terms):
    return f32_sum(*terms).astype(jnp.bfloat16)


def halves(value):
    half = value.shape[0] // 2
    return value[:half], value[half:]


def quarters(value):
    rows = value.shape[0] // 4
    return [value[i * rows : (i + 1) * rows] for i in range(4)]


def gather_first(block, near, wrap):
    return seq_swap(block, near), seq_swap(block, wrap)


def gather_second(from_near, from_wrap, near, wrap):
    return seq_swap(from_wrap, near), seq_swap(from_near, wrap)


def scatter_first(far, near, wrap):
    low, high = halves(far)
    return seq_swap(low, wrap), seq_swap(high, near)


def scatter_sums(to_near, to_wrap, low, high):
    near_low, near_high = halves(to_near)
    wrap_low, wrap_high = halves(to_wrap)
    return (
        jnp.concatenate([narrow_sum(near_low, low), near_high], axis=0),
        jnp.concatenate([wrap_low, narrow_sum(wrap_high, high)], axis=0),
    )


def scatter_tp_first(parts):
    own, other = halves(parts)
    beside = tp_swap(other, CORE)
    kept, sent = halves(own)
    kept_beside, sent_beside = halves(beside)
    return narrow_sum(kept, kept_beside), narrow_sum(sent, sent_beside)


def mask_of(place, y_outer):
    if not y_outer:
        return place
    y, z, x = place // 8, (place // 2) % 4, place % 2
    return z * 8 + y * 2 + x


def norm_kernel(seq_ref, residual_ref, gain_ref, cotangent_ref, normed_ref, turned_ref):
    me = seq_ref[0]
    width = residual_ref.shape[1]
    total = jnp.zeros((residual_ref.shape[0], LANES), jnp.float32)
    for place in range(width // LANES):
        piece = residual_ref[:, place * LANES : (place + 1) * LANES].astype(jnp.float32)
        total = total + piece * piece
    inverse_rms = lax.rsqrt(jnp.sum(total, axis=-1, keepdims=True) / width + EPSILON)
    for place in range(width // LANES):
        here = slice(place * LANES, (place + 1) * LANES)
        there = pl.ds(pl.multiple_of((me ^ mask_of(place, True)) * LANES, LANES), LANES)
        scaled = residual_ref[:, there].astype(jnp.float32) * inverse_rms
        normed_ref[:, here] = (scaled * gain_ref[:, there]).astype(jnp.bfloat16)
        there = pl.ds(pl.multiple_of((me ^ mask_of(place, False)) * LANES, LANES), LANES)
        turned_ref[:, here] = cotangent_ref[:, there]


def output_kernel(seq_ref, residual_ref, kept_ref, across_ref, out_ref):
    me = seq_ref[0]
    for place in range(residual_ref.shape[1] // LANES):
        here = slice(place * LANES, (place + 1) * LANES)
        there = pl.ds(pl.multiple_of((me ^ mask_of(place, False)) * LANES, LANES), LANES)
        mixed = kept_ref[:, here].astype(jnp.float32) + across_ref[:, here].astype(jnp.float32)
        out_ref[:, there] = (residual_ref[:, there].astype(jnp.float32) + mixed).astype(
            jnp.bfloat16
        )


def residual_kernel(
    seq_ref, residual_ref, gain_ref, cotangent_ref, kept_ref, across_ref, out_ref, gained_ref
):
    me = seq_ref[0]
    width = residual_ref.shape[1]
    rows = residual_ref.shape[0]
    square = jnp.zeros((rows, LANES), jnp.float32)
    cross = jnp.zeros((rows, LANES), jnp.float32)
    for place in range(width // LANES):
        here = slice(place * LANES, (place + 1) * LANES)
        there = pl.ds(pl.multiple_of((me ^ mask_of(place, True)) * LANES, LANES), LANES)
        feature = kept_ref[:, here].astype(jnp.float32) + across_ref[:, here].astype(jnp.float32)
        gained = feature * gain_ref[:, there]
        piece = residual_ref[:, there].astype(jnp.float32)
        square = square + piece * piece
        cross = cross + gained * piece
        gained_ref[:, there] = gained
    inverse_rms = lax.rsqrt(jnp.sum(square, axis=-1, keepdims=True) / width + EPSILON)
    mean = jnp.sum(cross, axis=-1, keepdims=True) * inverse_rms / width
    for place in range(width // LANES):
        here = slice(place * LANES, (place + 1) * LANES)
        scaled = residual_ref[:, here].astype(jnp.float32) * inverse_rms
        out_ref[:, here] = (
            inverse_rms * (gained_ref[:, here] - scaled * mean)
            + cotangent_ref[:, here].astype(jnp.float32)
        ).astype(jnp.bfloat16)


def compact_kernel(seq_ref, keys_ref, values_ref, out_ref):
    me = seq_ref[0]
    count = keys_ref.shape[0]
    rows, width = out_ref.shape[0] // count, keys_ref.shape[2]
    for part in range(count):
        here = slice(part * rows, (part + 1) * rows)
        out_ref[here, :width] = keys_ref[mask_of(me ^ part, True), :rows, :]
        out_ref[here, width:] = values_ref[mask_of(me ^ part, False), :rows, :]


def spread_kernel(seq_ref, keyval_ref, keys_ref, values_ref):
    me = seq_ref[0]
    count, padded, width = keys_ref.shape
    rows = keyval_ref.shape[0] // count
    rest = jnp.zeros((padded - rows, width), jnp.bfloat16)
    for part in range(count):
        here = slice(part * rows, (part + 1) * rows)
        keys_ref[mask_of(me ^ part, True)] = jnp.concatenate([keyval_ref[here, :width], rest], axis=0)
        values_ref[mask_of(me ^ part, False)] = jnp.concatenate(
            [keyval_ref[here, width:], rest], axis=0
        )


def whole(shape):
    return pl.BlockSpec(shape, lambda *_: (0,) * len(shape))


def row_call(kernel, seq_index, args, outs, scratch=()):
    return pl.pallas_call(
        kernel,
        grid_spec=pltpu.PrefetchScalarGridSpec(
            num_scalar_prefetch=1,
            grid=(1,),
            in_specs=[whole(arg.shape) for arg in args],
            out_specs=[whole(out.shape) for out in outs],
            scratch_shapes=list(scratch),
        ),
        out_shape=outs,
        compiler_params=pltpu.CompilerParams(vmem_limit_bytes=40 * 1024 * 1024),
    )(seq_index, *args)


def dot(left, right, left_dim, right_dim):
    return lax.dot_general(
        left, right, (((left_dim,), (right_dim,)), ((), ())), preferred_element_type=jnp.float32
    )


def attention_kernel(
    place_ref,
    query_ref,
    query_next_ref,
    up_ref,
    up_next_ref,
    keyval_ref,
    attended_ref,
    query_back_ref,
    keyval_back_ref,
    attended_end_ref,
    query_back_end_ref,
    attended_carry,
    query_carry,
):
    span = pl.program_id(0)
    last = pl.num_programs(0) - 1
    width = query_ref.shape[1]
    rows = lax.broadcasted_iota(jnp.int32, (SPAN, width), 0)
    here = pl.ds(pl.multiple_of(place_ref[span] * SPAN, SPAN), SPAN)
    after = pl.ds(pl.multiple_of(place_ref[span + 1] * SPAN, SPAN), SPAN)

    @pl.when(span == 0)
    def _():
        attended_carry[...] = jnp.zeros_like(attended_carry)
        query_carry[...] = jnp.zeros_like(query_carry)

    def shifted(ref, next_ref):
        first = ref[here, :].astype(jnp.float32)
        second = jnp.where(span == last, next_ref[...], ref[after, :]).astype(jnp.float32)
        joined = jnp.where(rows == SPAN - 1, first, second)
        return pltpu.roll(joined, 1, 0).astype(jnp.bfloat16)

    query = shifted(query_ref, query_next_ref)
    up = shifted(up_ref, up_next_ref)
    factor = 1.0 / math.sqrt(HEAD_DIM)
    attended_parts, query_parts = [], []
    for head in range(width // HEAD_DIM):
        own = slice(head * HEAD_DIM, (head + 1) * HEAD_DIM)
        value_own = slice(width + head * HEAD_DIM, width + (head + 1) * HEAD_DIM)
        q, u = query[:, own], up[:, own]
        keys, values = keyval_ref[:, own], keyval_ref[:, value_own]
        scores = dot(q, keys, 1, 1) * factor
        exponent = jnp.exp(scores - jnp.max(scores, axis=-1, keepdims=True))
        probabilities = exponent / jnp.sum(exponent, axis=-1, keepdims=True)
        weights = probabilities.astype(jnp.bfloat16)
        attended_parts.append(dot(weights, values, 1, 0))
        weight_grad = dot(u, values, 1, 1)
        inner = jnp.sum(weight_grad * probabilities, axis=-1, keepdims=True)
        score_grad = (probabilities * (weight_grad - inner) * factor).astype(jnp.bfloat16)
        query_parts.append(dot(score_grad, keys, 1, 0))
        keyval_back_ref[:, own] = dot(score_grad, q, 0, 0).astype(jnp.bfloat16)
        keyval_back_ref[:, value_own] = dot(weights, u, 0, 0).astype(jnp.bfloat16)
    for parts, carry, out_ref, end_ref in (
        (attended_parts, attended_carry, attended_ref, attended_end_ref),
        (query_parts, query_carry, query_back_ref, query_back_end_ref),
    ):
        turned = pltpu.roll(jnp.concatenate(parts, axis=1), SPAN - 1, 0)
        out_ref[...] = jnp.where(rows == SPAN - 1, turned, carry[...]).astype(jnp.bfloat16)
        carry[...] = turned
        end_ref[...] = jnp.where(rows == SPAN - 1, 0.0, turned).astype(jnp.bfloat16)


def attention(places, query, query_next, up, up_next, keyvals):
    tokens, width = query.shape
    spans = tokens // SPAN
    span_rows = keyvals.shape[0] // spans
    by_place = lambda i, places: (places[i], 0)
    like = lambda array: jax.ShapeDtypeStruct(array.shape, jnp.bfloat16)
    return pl.pallas_call(
        attention_kernel,
        grid_spec=pltpu.PrefetchScalarGridSpec(
            num_scalar_prefetch=1,
            grid=(spans,),
            in_specs=[
                whole(query.shape),
                whole(query_next.shape),
                whole(up.shape),
                whole(up_next.shape),
                pl.BlockSpec((span_rows, keyvals.shape[1]), by_place),
            ],
            out_specs=[
                pl.BlockSpec((SPAN, width), by_place),
                pl.BlockSpec((SPAN, width), by_place),
                pl.BlockSpec((span_rows, keyvals.shape[1]), by_place),
                whole(query_next.shape),
                whole(query_next.shape),
            ],
            scratch_shapes=[
                pltpu.VMEM((SPAN, width), jnp.float32),
                pltpu.VMEM((SPAN, width), jnp.float32),
            ],
        ),
        out_shape=[
            like(query),
            like(query),
            like(keyvals),
            like(query_next),
            like(query_next),
        ],
        compiler_params=pltpu.CompilerParams(vmem_limit_bytes=40 * 1024 * 1024),
    )(places, query, query_next, up, up_next, keyvals)


def per_device(
    residual, norm_gain, query_weight, keyval_weight, output_weight, neighbours, cotangent
):
    me, seq_count = lax.axis_index("seq"), lax.axis_size("seq")
    column, tp_count = lax.axis_index("tp"), lax.axis_size("tp")
    tokens_here, features = residual.shape
    local_width = query_weight.shape[1]
    neighbour_count, _, enc_width = neighbours.shape
    enc_rows = keyval_weight.shape[0]
    group_tokens = tokens_here * tp_count
    spans = group_tokens // SPAN
    seq_index = me.astype(jnp.int32).reshape(1)
    gain_row = norm_gain.reshape(1, features)
    token_shape = jax.ShapeDtypeStruct(residual.shape, jnp.bfloat16)

    weight_rows = query_weight.shape[0]
    padded = -(-enc_rows // 16) * 16
    padding = ((0, padded - enc_rows), (0, 0))
    query_shard = jnp.concatenate([query_weight, jnp.pad(keyval_weight[:, 0], padding)])[None]
    output_shard = jnp.concatenate([output_weight, jnp.pad(keyval_weight[:, 1], padding)])[None]
    flat_neighbours = neighbours.reshape(neighbour_count * R, enc_width)
    normed, turned = row_call(
        norm_kernel, seq_index, (residual, gain_row, cotangent), [token_shape, token_shape]
    )

    neighbours_across = tp_swap(flat_neighbours, X_LOW)
    neighbours_beside = tp_swap(flat_neighbours, CORE)
    queries = jnp.concatenate([query_shard, seq_swap(query_shard, X_HIGH)])
    outputs = jnp.concatenate([output_shard, seq_swap(output_shard, X_HIGH)])
    queries_near, queries_wrap = gather_first(queries, Z_NEAR, Z_WRAP)
    outputs_near, outputs_wrap = gather_first(outputs, Y_NEAR, Y_WRAP)
    queries_far = gather_second(
        halves(queries_near)[1], halves(queries_wrap)[0], Z_NEAR, Z_WRAP
    )
    outputs_far = gather_second(
        halves(outputs_near)[1], halves(outputs_wrap)[0], Y_NEAR, Y_WRAP
    )
    queries = jnp.concatenate([queries, queries_near, *queries_far, queries_wrap])
    outputs = jnp.concatenate([outputs, outputs_near, *outputs_far, outputs_wrap])

    queries, outputs, normed = fence([queries, outputs, normed], [neighbours_across])
    neighbours_both = tp_swap(neighbours_across, CORE)
    normed_across, normed_beside = tp_swap(normed, X_LOW), tp_swap(normed, CORE)
    queries_near, queries_wrap = gather_first(queries, Y_NEAR, Y_WRAP)
    outputs_near, outputs_wrap = gather_first(outputs, Z_NEAR, Z_WRAP)

    queries_near, queries_wrap, outputs_near, outputs_wrap, turned = fence(
        [queries_near, queries_wrap, outputs_near, outputs_wrap, turned], [normed_across]
    )
    turned_across, turned_beside = tp_swap(turned, X_LOW), tp_swap(turned, CORE)
    normed_both = tp_swap(normed_across, CORE)
    queries_far = gather_second(
        halves(queries_near)[1], halves(queries_wrap)[0], Y_NEAR, Y_WRAP
    )
    outputs_far = gather_second(
        halves(outputs_near)[1], halves(outputs_wrap)[0], Z_NEAR, Z_WRAP
    )
    turned_both = tp_swap(turned_across, CORE)

    def joined(pieces, rows):
        return jnp.concatenate([piece[:, rows] for piece in pieces])

    query_pieces = [queries, queries_near, *queries_far, queries_wrap]
    output_pieces = [outputs, outputs_near, *outputs_far, outputs_wrap]
    main, extra = slice(None, weight_rows), slice(weight_rows, None)
    full_query = joined(query_pieces, main).reshape(features, local_width)
    full_output = joined(output_pieces, main).reshape(features, local_width)
    (full_keyval,) = row_call(
        compact_kernel,
        seq_index,
        (joined(query_pieces, extra), joined(output_pieces, extra)),
        [jax.ShapeDtypeStruct((enc_width, 2 * local_width), jnp.bfloat16)],
    )
    group_neighbours = jnp.concatenate(
        [flat_neighbours, neighbours_across, neighbours_beside, neighbours_both]
    )
    group_normed = jnp.concatenate([normed, normed_across, normed_beside, normed_both])
    group_cotangent = jnp.concatenate([turned, turned_across, turned_beside, turned_both])

    keyvals = dot(group_neighbours, full_keyval, 1, 0).astype(jnp.bfloat16)
    query = dot(group_normed, full_query, 1, 0).astype(jnp.bfloat16)
    attended_grad = dot(group_cotangent, full_output, 1, 0).astype(jnp.bfloat16)

    block = jnp.arange(spans, dtype=jnp.int32)
    mask = (block // (spans // tp_count)) ^ column.astype(jnp.int32)
    place = ((mask % 2) * 2 + mask // 2) * (spans // tp_count) + block % (spans // tp_count)
    places = jnp.concatenate([place, place[:1]])
    groups = LENGTH // group_tokens
    inside = [i for i in range(seq_count) if i % groups]
    first_row = place[0] * SPAN

    def first_block(value):
        return lax.dynamic_slice(value, (first_row, 0), (SPAN, local_width))

    def from_next(value):
        return lax.ppermute(first_block(value), "seq", [(i, i - 1) for i in inside])

    attended, query_back, keyval_back, attended_end, query_back_end = attention(
        places, query, from_next(query), attended_grad, from_next(attended_grad), keyvals
    )

    def with_previous(value, end):
        arrived = lax.ppermute(end, "seq", [(i - 1, i) for i in inside])
        return lax.dynamic_update_slice(value, first_block(value) + arrived, (first_row, 0))

    attended = with_previous(attended, attended_end)
    query_back = with_previous(query_back, query_back_end)

    neighbour_kept, neighbour_sent = scatter_tp_first(
        dot(keyval_back, full_keyval, 1, 1).astype(jnp.bfloat16)
    )
    keyval_part = dot(group_neighbours, keyval_back, 0, 0).astype(jnp.bfloat16)
    extra_shape = jax.ShapeDtypeStruct((seq_count, padded, local_width), jnp.bfloat16)
    key_part, value_part = row_call(
        spread_kernel, seq_index, (keyval_part,), [extra_shape, extra_shape]
    )
    attended, query_back, neighbour_sent = fence(
        [attended, query_back, neighbour_sent], [key_part]
    )
    neighbour_across = tp_swap(neighbour_sent, X_LOW)

    def parts(product, more):
        product = product.reshape(seq_count, weight_rows, local_width)
        return [
            jnp.concatenate(pair, axis=1) for pair in zip(quarters(product), quarters(more))
        ]

    output_part = dot(group_cotangent, attended, 0, 0).astype(jnp.bfloat16)
    query_part = dot(group_normed, query_back, 0, 0).astype(jnp.bfloat16)
    output_own, output_near, output_far, output_wrap = parts(output_part, value_part)
    query_own, query_near, query_far, query_wrap = parts(query_part, key_part)
    output_far = scatter_first(output_far, Z_NEAR, Z_WRAP)
    query_far = scatter_first(query_far, Y_NEAR, Y_WRAP)
    mixed_kept, mixed_sent = scatter_tp_first(
        dot(attended, full_output, 1, 1).astype(jnp.bfloat16)
    )
    output_near, output_wrap = scatter_sums(output_near, output_wrap, *output_far)
    query_near, query_wrap = scatter_sums(query_near, query_wrap, *query_far)

    output_near, output_wrap, query_near, query_wrap, mixed_sent, query_back = fence(
        [output_near, output_wrap, query_near, query_wrap, mixed_sent, query_back],
        [neighbour_across],
    )
    mixed_across = tp_swap(mixed_sent, X_LOW)
    feature_kept, feature_sent = scatter_tp_first(
        dot(query_back, full_query, 1, 1).astype(jnp.bfloat16)
    )
    outputs = narrow_sum(
        output_own, seq_swap(output_near, Z_NEAR), seq_swap(output_wrap, Z_WRAP)
    )
    queries = narrow_sum(query_own, seq_swap(query_near, Y_NEAR), seq_swap(query_wrap, Y_WRAP))

    outputs, queries, feature_sent = fence([outputs, queries, feature_sent], [mixed_across])
    feature_across = tp_swap(feature_sent, X_LOW)
    output_own, output_near, output_far, output_wrap = quarters(outputs)
    query_own, query_near, query_far, query_wrap = quarters(queries)
    output_far = scatter_first(output_far, Y_NEAR, Y_WRAP)
    query_far = scatter_first(query_far, Z_NEAR, Z_WRAP)
    output_near, output_wrap = scatter_sums(output_near, output_wrap, *output_far)
    query_near, query_wrap = scatter_sums(query_near, query_wrap, *query_far)
    outputs = narrow_sum(
        output_own, seq_swap(output_near, Y_NEAR), seq_swap(output_wrap, Y_WRAP)
    )
    queries = narrow_sum(query_own, seq_swap(query_near, Z_NEAR), seq_swap(query_wrap, Z_WRAP))
    outputs, queries = fence([outputs, queries], [feature_across])
    output_total = f32_sum(outputs[0], seq_swap(outputs[1], X_HIGH))
    query_total = f32_sum(queries[0], seq_swap(queries[1], X_HIGH))
    output_grad, query_grad = output_total[:weight_rows], query_total[:weight_rows]
    keyval_grad = jnp.stack(
        [
            query_total[weight_rows : weight_rows + enc_rows],
            output_total[weight_rows : weight_rows + enc_rows],
        ],
        axis=1,
    )

    row_sums = jnp.sum(f32_sum(full_query) * f32_sum(query_part), axis=1)
    where_from = mask_of(jnp.arange(seq_count, dtype=jnp.int32) ^ me, True)
    gain_total = jnp.take(row_sums.reshape(seq_count, features // seq_count), where_from, axis=0)
    for swap, mask in (
        (tp_swap, CORE),
        (tp_swap, X_LOW),
        (seq_swap, X_HIGH),
        (seq_swap, Y_NEAR),
        (seq_swap, Y_WRAP),
        (seq_swap, Z_NEAR),
        (seq_swap, Z_WRAP),
    ):
        gain_total = gain_total + swap(gain_total, mask)
    gain_grad = gain_total.reshape(features) / norm_gain

    (layer_output,) = row_call(
        output_kernel, seq_index, (residual, mixed_kept, mixed_across), [token_shape]
    )
    (residual_grad,) = row_call(
        residual_kernel,
        seq_index,
        (residual, gain_row, cotangent, feature_kept, feature_across),
        [token_shape],
        [pltpu.VMEM(residual.shape, jnp.float32)],
    )
    neighbour_grad = (
        f32_sum(neighbour_kept, neighbour_across).astype(jnp.bfloat16).reshape(neighbours.shape)
    )
    return (
        layer_output,
        residual_grad,
        neighbour_grad,
        gain_grad,
        query_grad,
        keyval_grad,
        output_grad,
    )


def solution(mesh):
    in_specs = (
        P(("seq", "tp"), None),
        P(),
        P("seq", "tp"),
        P("seq", None, "tp"),
        P("seq", "tp"),
        P(("seq", "tp"), None, None),
        P(("seq", "tp"), None),
    )
    out_specs = (
        P(("seq", "tp"), None),
        P(("seq", "tp"), None),
        P(("seq", "tp"), None, None),
        P(),
        P("seq", "tp"),
        P("seq", None, "tp"),
        P("seq", "tp"),
    )
    return jax.shard_map(
        per_device, mesh=mesh, in_specs=in_specs, out_specs=out_specs, check_vma=False
    )
```

```python
import functools
import math

import jax
import jax.numpy as jnp
from jax import lax
from jax.experimental import pallas as pl
from jax.experimental.pallas import tpu as pltpu
from jax.sharding import PartitionSpec as P

HEAD_DIM = 128
SPAN = 64
K_NB = 2
R = 128
LENGTH = 2048
EPSILON = 1e-06
LANES = 128
VMEM_BYTES = 40 * 1024 * 1024
MOST_VMEM_BYTES = 56 * 1024 * 1024

Z_NEAR, Z_WRAP = 8, 24
Y_NEAR, Y_WRAP = 2, 6
X_HIGH = 1
X_LOW, CORE = 2, 1


def seq_swap(value, mask):
    count = lax.axis_size("seq")
    return lax.ppermute(value, "seq", [(i, i ^ mask) for i in range(count)])


def tp_swap(value, mask):
    count = lax.axis_size("tp")
    return lax.ppermute(value, "tp", [(i, i ^ mask) for i in range(count)])


def f32_sum(*terms):
    total = terms[0].astype(jnp.float32)
    for term in terms[1:]:
        total = total + term.astype(jnp.float32)
    return total


def fence(values, after):
    count = len(values)
    anywhere = pl.BlockSpec(memory_space=pl.ANY)
    return pl.pallas_call(
        lambda *refs: None,
        in_specs=[anywhere] * (count + len(after)),
        out_specs=[anywhere] * count,
        out_shape=[jax.ShapeDtypeStruct(value.shape, value.dtype) for value in values],
        input_output_aliases={i: i for i in range(count)},
    )(*values, *after)


def block_steps(count, copies, sums, held, after):
    anywhere = pl.BlockSpec(memory_space=pl.ANY)

    def spec(array, first):
        return pl.BlockSpec((1, *array.shape[1:]), lambda i: (i + first, 0, 0))

    copied, summed = len(copies), len(sums)

    def body(*refs):
        for source, out in zip(refs[:copied], refs[-copied - summed - len(held) :]):
            out[...] = source[...]
        sources = refs[copied : copied + 2 * summed]
        for i in range(summed):
            out = refs[len(refs) - summed - len(held) + i]
            out[...] = narrow_sum(sources[2 * i][...], sources[2 * i + 1][...])

    args = [array for array, _ in copies]
    in_specs = [spec(array, first) for array, first in copies]
    out_specs = [spec(array, 0) for array, _ in copies]
    out_shape = [
        jax.ShapeDtypeStruct((count, *array.shape[1:]), array.dtype) for array, _ in copies
    ]
    aliases = {}
    for array, incoming, first in sums:
        aliases[len(args)] = len(out_shape)
        args += [array, incoming]
        in_specs += [spec(array, first), spec(incoming, 0)]
        out_specs.append(spec(array, first))
        out_shape.append(jax.ShapeDtypeStruct(array.shape, array.dtype))
    for array in held:
        aliases[len(args)] = len(out_shape)
        args.append(array)
        in_specs.append(anywhere)
        out_specs.append(anywhere)
        out_shape.append(jax.ShapeDtypeStruct(array.shape, array.dtype))
    return pl.pallas_call(
        body,
        grid=(count,),
        in_specs=in_specs + [anywhere] * len(after),
        out_specs=out_specs,
        out_shape=out_shape,
        input_output_aliases=aliases,
        compiler_params=pltpu.CompilerParams(vmem_limit_bytes=VMEM_BYTES),
    )(*args, *after)


def piece_specs(sizes, block, shape):
    specs, first = [], 0
    for size in sizes:
        steps = size // block
        specs.append(
            pl.BlockSpec(
                (block, *shape), lambda i, f=first, n=steps: (jnp.clip(i - f, 0, n - 1), 0, 0)
            )
        )
        first += steps
    return specs


def store_piece(sizes, block, refs, step, value):
    first = 0
    for size, ref in zip(sizes, refs):
        end = first + size // block

        @pl.when((step >= first) & (step < end))
        def _(ref=ref):
            ref[...] = value

        first = end


def sum_and_split(groups, sizes, held, after):
    anywhere = pl.BlockSpec(memory_space=pl.ANY)
    terms, pieces = len(groups[0]), len(sizes)
    shape = groups[0][0].shape
    flat = [array for group in groups for array in group]

    def body(*refs):
        step = pl.program_id(0)
        outs = refs[len(flat) + len(held) + len(after) :]
        for i in range(len(groups)):
            total = narrow_sum(*[ref[...] for ref in refs[i * terms : (i + 1) * terms]])
            store_piece(sizes, 1, outs[i * pieces : (i + 1) * pieces], step, total)

    one = pl.BlockSpec((1, *shape[1:]), lambda i: (i, 0, 0))
    results = pl.pallas_call(
        body,
        grid=(shape[0],),
        in_specs=[one] * len(flat) + [anywhere] * (len(held) + len(after)),
        out_specs=piece_specs(sizes, 1, shape[1:]) * len(groups) + [anywhere] * len(held),
        out_shape=[
            jax.ShapeDtypeStruct((size, *shape[1:]), jnp.bfloat16)
            for _ in groups
            for size in sizes
        ]
        + [jax.ShapeDtypeStruct(array.shape, array.dtype) for array in held],
        input_output_aliases={len(flat) + i: len(groups) * pieces + i for i in range(len(held))},
        compiler_params=pltpu.CompilerParams(vmem_limit_bytes=VMEM_BYTES),
    )(*flat, *held, *after)
    cut = [results[i * pieces : (i + 1) * pieces] for i in range(len(groups))]
    return *cut, list(results[len(groups) * pieces :])


def narrow_sum(*terms):
    return f32_sum(*terms).astype(jnp.bfloat16)


def halves(value):
    half = value.shape[0] // 2
    return value[:half], value[half:]


def quarters(value):
    rows = value.shape[0] // 4
    return [value[i * rows : (i + 1) * rows] for i in range(4)]


def gather_first(block, near, wrap):
    return seq_swap(block, near), seq_swap(block, wrap)


def gather_second(from_near, from_wrap, near, wrap):
    return seq_swap(from_wrap, near), seq_swap(from_near, wrap)


def scatter_first(far, near, wrap):
    low, high = halves(far)
    return seq_swap(low, wrap), seq_swap(high, near)


def scatter_sums(to_near, to_wrap, low, high):
    near_low, near_high = halves(to_near)
    wrap_low, wrap_high = halves(to_wrap)
    return (
        jnp.concatenate([narrow_sum(near_low, low), near_high], axis=0),
        jnp.concatenate([wrap_low, narrow_sum(wrap_high, high)], axis=0),
    )


def swap_half(parts):
    own, other = halves(parts)
    return own, tp_swap(other, CORE)


def half_sums(own, beside):
    kept, sent = halves(own)
    kept_beside, sent_beside = halves(beside)
    return narrow_sum(kept, kept_beside), narrow_sum(sent, sent_beside)


def mask_of(place, y_outer):
    if not y_outer:
        return place
    y, z, x = place // 8, (place // 2) % 4, place % 2
    return z * 8 + y * 2 + x


def norm_kernel(seq_ref, residual_ref, gain_ref, cotangent_ref, normed_ref, turned_ref):
    me = seq_ref[0]
    width = residual_ref.shape[1]
    total = jnp.zeros((residual_ref.shape[0], LANES), jnp.float32)
    for place in range(width // LANES):
        piece = residual_ref[:, place * LANES : (place + 1) * LANES].astype(jnp.float32)
        total = total + piece * piece
    inverse_rms = lax.rsqrt(jnp.sum(total, axis=-1, keepdims=True) / width + EPSILON)
    for place in range(width // LANES):
        here = slice(place * LANES, (place + 1) * LANES)
        there = pl.ds(pl.multiple_of((me ^ mask_of(place, True)) * LANES, LANES), LANES)
        scaled = residual_ref[:, there].astype(jnp.float32) * inverse_rms
        normed_ref[:, here] = (scaled * gain_ref[:, there]).astype(jnp.bfloat16)
        there = pl.ds(pl.multiple_of((me ^ mask_of(place, False)) * LANES, LANES), LANES)
        turned_ref[:, here] = cotangent_ref[:, there]


def output_kernel(seq_ref, residual_ref, kept_ref, across_ref, out_ref):
    me = seq_ref[0]
    for place in range(residual_ref.shape[1] // LANES):
        here = slice(place * LANES, (place + 1) * LANES)
        there = pl.ds(pl.multiple_of((me ^ mask_of(place, False)) * LANES, LANES), LANES)
        mixed = kept_ref[:, here].astype(jnp.float32) + across_ref[:, here].astype(jnp.float32)
        out_ref[:, there] = (residual_ref[:, there].astype(jnp.float32) + mixed).astype(
            jnp.bfloat16
        )


def residual_kernel(
    seq_ref, residual_ref, gain_ref, cotangent_ref, kept_ref, across_ref, out_ref, gained_ref
):
    me = seq_ref[0]
    width = residual_ref.shape[1]
    rows = residual_ref.shape[0]
    square = jnp.zeros((rows, LANES), jnp.float32)
    cross = jnp.zeros((rows, LANES), jnp.float32)
    for place in range(width // LANES):
        here = slice(place * LANES, (place + 1) * LANES)
        there = pl.ds(pl.multiple_of((me ^ mask_of(place, True)) * LANES, LANES), LANES)
        feature = kept_ref[:, here].astype(jnp.float32) + across_ref[:, here].astype(jnp.float32)
        gained = feature * gain_ref[:, there]
        piece = residual_ref[:, there].astype(jnp.float32)
        square = square + piece * piece
        cross = cross + gained * piece
        gained_ref[:, there] = gained
    inverse_rms = lax.rsqrt(jnp.sum(square, axis=-1, keepdims=True) / width + EPSILON)
    mean = jnp.sum(cross, axis=-1, keepdims=True) * inverse_rms / width
    for place in range(width // LANES):
        here = slice(place * LANES, (place + 1) * LANES)
        scaled = residual_ref[:, here].astype(jnp.float32) * inverse_rms
        out_ref[:, here] = (
            inverse_rms * (gained_ref[:, here] - scaled * mean)
            + cotangent_ref[:, here].astype(jnp.float32)
        ).astype(jnp.bfloat16)


def compact_kernel(seq_ref, *refs):
    me = seq_ref[0]
    out_ref, keys, values = refs[-3:]
    count, _, width = keys.shape
    pieces = (len(refs) - 3) // 2
    for joined, sources in ((keys, refs[:pieces]), (values, refs[pieces : 2 * pieces])):
        first = 0
        for source in sources:
            joined[first : first + source.shape[0]] = source[...]
            first += source.shape[0]
    rows = out_ref.shape[0] // count
    for part in range(count):
        here = slice(part * rows, (part + 1) * rows)
        out_ref[here, :width] = keys[mask_of(me ^ part, True), :rows, :]
        out_ref[here, width:] = values[mask_of(me ^ part, False), :rows, :]


def compact(seq_index, query_pieces, output_pieces, first_row, rows):
    pieces = [*query_pieces, *output_pieces]
    _, all_rows, width = pieces[0].shape
    padded = all_rows - first_row
    count = sum(piece.shape[0] for piece in query_pieces)
    extra = lambda *_: (0, first_row // padded, 0)
    return pl.pallas_call(
        compact_kernel,
        grid_spec=pltpu.PrefetchScalarGridSpec(
            num_scalar_prefetch=1,
            grid=(1,),
            in_specs=[pl.BlockSpec((piece.shape[0], padded, width), extra) for piece in pieces],
            out_specs=whole((count * rows, 2 * width)),
            scratch_shapes=[pltpu.VMEM((count, padded, width), jnp.bfloat16)] * 2,
        ),
        out_shape=jax.ShapeDtypeStruct((count * rows, 2 * width), jnp.bfloat16),
        compiler_params=pltpu.CompilerParams(vmem_limit_bytes=MOST_VMEM_BYTES),
    )(seq_index, *pieces)


def spread_kernel(seq_ref, keyval_ref, keys_ref, values_ref):
    me = seq_ref[0]
    count, padded, width = keys_ref.shape
    rows = keyval_ref.shape[0] // count
    rest = jnp.zeros((padded - rows, width), jnp.bfloat16)
    for part in range(count):
        here = slice(part * rows, (part + 1) * rows)
        keys_ref[mask_of(me ^ part, True)] = jnp.concatenate([keyval_ref[here, :width], rest], axis=0)
        values_ref[mask_of(me ^ part, False)] = jnp.concatenate(
            [keyval_ref[here, width:], rest], axis=0
        )


def whole(shape):
    return pl.BlockSpec(shape, lambda *_: (0,) * len(shape))


def row_call(kernel, seq_index, args, outs, scratch=()):
    return pl.pallas_call(
        kernel,
        grid_spec=pltpu.PrefetchScalarGridSpec(
            num_scalar_prefetch=1,
            grid=(1,),
            in_specs=[whole(arg.shape) for arg in args],
            out_specs=[whole(out.shape) for out in outs],
            scratch_shapes=list(scratch),
        ),
        out_shape=outs,
        compiler_params=pltpu.CompilerParams(vmem_limit_bytes=VMEM_BYTES),
    )(seq_index, *args)


def dot(left, right, left_dim, right_dim):
    return lax.dot_general(
        left, right, (((left_dim,), (right_dim,)), ((), ())), preferred_element_type=jnp.float32
    )


def weight_kernel(starts, parts, *refs):
    tokens, pieces = refs[:parts], refs[parts:-3]
    product_ref, full_ref, total = refs[-3:]
    step = pl.program_id(0)
    count = pieces[0].shape[0]
    rows, width = full_ref.shape[0] // count, full_ref.shape[1]
    for piece, first, end in zip(pieces, starts, starts[1:]):

        @pl.when((step >= first) & (step < end))
        def _(piece=piece):
            full_ref[...] = piece[...].reshape(count * rows, width)

    @pl.when(step == 0)
    def _():
        total[...] = jnp.zeros_like(total)

    total[...] += dot(jnp.concatenate([ref[...] for ref in tokens]), full_ref[...], 1, 0)

    @pl.when(step == pl.num_programs(0) - 1)
    def _():
        product_ref[...] = total[...].astype(jnp.bfloat16)


def weight_call(tokens, pieces, rows):
    shards = min(piece.shape[0] for piece in pieces)
    width = pieces[0].shape[2]
    starts = [0]
    for piece in pieces:
        starts.append(starts[-1] + piece.shape[0] // shards)
    steps = starts[-1]
    token_rows = tokens[0].shape[0]
    all_tokens = token_rows * len(tokens)
    return pl.pallas_call(
        functools.partial(weight_kernel, tuple(starts), len(tokens)),
        grid=(steps,),
        in_specs=[pl.BlockSpec((token_rows, shards * rows), lambda i: (0, i))] * len(tokens)
        + piece_specs([piece.shape[0] for piece in pieces], shards, (rows, width)),
        out_specs=[
            whole((all_tokens, width)),
            pl.BlockSpec((shards * rows, width), lambda i: (i, 0)),
        ],
        out_shape=[
            jax.ShapeDtypeStruct((all_tokens, width), jnp.bfloat16),
            jax.ShapeDtypeStruct((steps * shards * rows, width), jnp.bfloat16),
        ],
        scratch_shapes=[pltpu.VMEM((all_tokens, width), jnp.float32)],
        compiler_params=pltpu.CompilerParams(vmem_limit_bytes=MOST_VMEM_BYTES),
    )(*tokens, *pieces)


def grad_kernel(sizes, parts, *refs):
    tokens, (back_ref, extra_ref), pieces = refs[:parts], refs[parts : parts + 2], refs[parts + 2 :]
    joined = jnp.concatenate([ref[...] for ref in tokens])
    product = dot(joined, back_ref[...], 0, 0)
    count, _, width = extra_ref.shape
    shards = product.astype(jnp.bfloat16).reshape(count, product.shape[0] // count, width)
    value = jnp.concatenate([shards, extra_ref[...]], axis=1)
    store_piece(sizes, count, pieces, pl.program_id(0), value)


def grad_call(tokens, back, extra, sizes):
    shards = min(sizes)
    count, padded, width = extra.shape
    features = tokens[0].shape[1]
    columns = features // count * shards
    rows = features // count + padded
    return pl.pallas_call(
        functools.partial(grad_kernel, tuple(sizes), len(tokens)),
        grid=(count // shards,),
        in_specs=[pl.BlockSpec((tokens[0].shape[0], columns), lambda i: (0, i))] * len(tokens)
        + [whole(back.shape), pl.BlockSpec((shards, padded, width), lambda i: (i, 0, 0))],
        out_specs=piece_specs(sizes, shards, (rows, width)),
        out_shape=[jax.ShapeDtypeStruct((size, rows, width), jnp.bfloat16) for size in sizes],
        cost_estimate=pl.CostEstimate(
            flops=2 * back.shape[0] * features * width,
            bytes_accessed=8 * features * width,
            transcendentals=0,
        ),
        compiler_params=pltpu.CompilerParams(vmem_limit_bytes=MOST_VMEM_BYTES),
    )(*tokens, back, extra)


def column_kernel(parts, *refs):
    tokens, feature_ref, out_ref = refs[:parts], refs[parts], refs[parts + 1]
    joined = jnp.concatenate([ref[...] for ref in tokens]).astype(jnp.float32)
    product = joined * feature_ref[...].astype(jnp.float32)
    rows, columns = product.shape
    out_ref[...] = jnp.sum(product.reshape(rows // 8, 8, columns), axis=0)


def column_sums(tokens, feature):
    rows, features = feature.shape
    columns = features // 8
    return pl.pallas_call(
        functools.partial(column_kernel, len(tokens)),
        grid=(8,),
        in_specs=[pl.BlockSpec((tokens[0].shape[0], columns), lambda i: (0, i))] * len(tokens)
        + [pl.BlockSpec((rows, columns), lambda i: (0, i))],
        out_specs=pl.BlockSpec((8, columns), lambda i: (0, i)),
        out_shape=jax.ShapeDtypeStruct((8, features), jnp.float32),
        compiler_params=pltpu.CompilerParams(vmem_limit_bytes=VMEM_BYTES),
    )(*tokens, feature)


def attention_kernel(
    place_ref,
    query_ref,
    up_ref,
    next_ref,
    keyval_ref,
    attended_ref,
    query_back_ref,
    keyval_back_ref,
    end_ref,
    attended_carry,
    query_carry,
):
    span = pl.program_id(0)
    last = pl.num_programs(0) - 1
    width = query_ref.shape[1]
    rows = lax.broadcasted_iota(jnp.int32, (SPAN, width), 0)
    here = pl.ds(pl.multiple_of(place_ref[span] * SPAN, SPAN), SPAN)
    after = pl.ds(pl.multiple_of(place_ref[span + 1] * SPAN, SPAN), SPAN)

    @pl.when(span == 0)
    def _():
        attended_carry[...] = jnp.zeros_like(attended_carry)
        query_carry[...] = jnp.zeros_like(query_carry)

    def shifted(ref, part):
        first = ref[here, :].astype(jnp.float32)
        following = next_ref[part * SPAN : (part + 1) * SPAN, :]
        second = jnp.where(span == last, following, ref[after, :]).astype(jnp.float32)
        joined = jnp.where(rows == SPAN - 1, first, second)
        return pltpu.roll(joined, 1, 0).astype(jnp.bfloat16)

    query = shifted(query_ref, 0)
    up = shifted(up_ref, 1)
    factor = 1.0 / math.sqrt(HEAD_DIM)
    attended_parts, query_parts = [], []
    for head in range(width // HEAD_DIM):
        own = slice(head * HEAD_DIM, (head + 1) * HEAD_DIM)
        value_own = slice(width + head * HEAD_DIM, width + (head + 1) * HEAD_DIM)
        q, u = query[:, own], up[:, own]
        keys, values = keyval_ref[:, own], keyval_ref[:, value_own]
        scores = dot(q, keys, 1, 1) * factor
        exponent = jnp.exp(scores - jnp.max(scores, axis=-1, keepdims=True))
        probabilities = exponent / jnp.sum(exponent, axis=-1, keepdims=True)
        weights = probabilities.astype(jnp.bfloat16)
        attended_parts.append(dot(weights, values, 1, 0))
        weight_grad = dot(u, values, 1, 1)
        inner = jnp.sum(weight_grad * probabilities, axis=-1, keepdims=True)
        score_grad = (probabilities * (weight_grad - inner) * factor).astype(jnp.bfloat16)
        query_parts.append(dot(score_grad, keys, 1, 0))
        keyval_back_ref[:, own] = dot(score_grad, q, 0, 0).astype(jnp.bfloat16)
        keyval_back_ref[:, value_own] = dot(weights, u, 0, 0).astype(jnp.bfloat16)
    for part, (parts, carry, out_ref) in enumerate(
        (
            (attended_parts, attended_carry, attended_ref),
            (query_parts, query_carry, query_back_ref),
        )
    ):
        turned = pltpu.roll(jnp.concatenate(parts, axis=1), SPAN - 1, 0)
        out_ref[...] = jnp.where(rows == SPAN - 1, turned, carry[...]).astype(jnp.bfloat16)
        carry[...] = turned
        end_ref[part * SPAN : (part + 1) * SPAN, :] = jnp.where(
            rows == SPAN - 1, 0.0, turned
        ).astype(jnp.bfloat16)


def attention(places, query, up, following, keyvals):
    tokens, width = query.shape
    spans = tokens // SPAN
    span_rows = keyvals.shape[0] // spans
    by_place = lambda i, places: (places[i], 0)
    like = lambda array: jax.ShapeDtypeStruct(array.shape, jnp.bfloat16)
    return pl.pallas_call(
        attention_kernel,
        grid_spec=pltpu.PrefetchScalarGridSpec(
            num_scalar_prefetch=1,
            grid=(spans,),
            in_specs=[
                whole(query.shape),
                whole(up.shape),
                whole(following.shape),
                pl.BlockSpec((span_rows, keyvals.shape[1]), by_place),
            ],
            out_specs=[
                pl.BlockSpec((SPAN, width), by_place),
                pl.BlockSpec((SPAN, width), by_place),
                pl.BlockSpec((span_rows, keyvals.shape[1]), by_place),
                whole(following.shape),
            ],
            scratch_shapes=[
                pltpu.VMEM((SPAN, width), jnp.float32),
                pltpu.VMEM((SPAN, width), jnp.float32),
            ],
        ),
        out_shape=[
            like(query),
            like(query),
            like(keyvals),
            like(following),
        ],
        compiler_params=pltpu.CompilerParams(vmem_limit_bytes=VMEM_BYTES),
    )(places, query, up, following, keyvals)


def per_device(
    residual, norm_gain, query_weight, keyval_weight, output_weight, neighbours, cotangent
):
    me, seq_count = lax.axis_index("seq"), lax.axis_size("seq")
    column, tp_count = lax.axis_index("tp"), lax.axis_size("tp")
    tokens_here, features = residual.shape
    local_width = query_weight.shape[1]
    neighbour_count, _, enc_width = neighbours.shape
    enc_rows = keyval_weight.shape[0]
    group_tokens = tokens_here * tp_count
    spans = group_tokens // SPAN
    seq_index = me.astype(jnp.int32).reshape(1)
    gain_row = norm_gain.reshape(1, features)
    token_shape = jax.ShapeDtypeStruct(residual.shape, jnp.bfloat16)

    weight_rows = query_weight.shape[0]
    padded = -(-enc_rows // 16) * 16
    padding = ((0, padded - enc_rows), (0, 0))
    query_shard = jnp.concatenate([query_weight, jnp.pad(keyval_weight[:, 0], padding)])[None]
    output_shard = jnp.concatenate([output_weight, jnp.pad(keyval_weight[:, 1], padding)])[None]
    flat_neighbours = neighbours.reshape(neighbour_count * R, enc_width)
    normed, turned = row_call(
        norm_kernel, seq_index, (residual, gain_row, cotangent), [token_shape, token_shape]
    )

    neighbours_beside = tp_swap(flat_neighbours, CORE)
    normed_beside, turned_beside = tp_swap(normed, CORE), tp_swap(turned, CORE)
    queries = jnp.concatenate([query_shard, seq_swap(query_shard, X_HIGH)])
    outputs = jnp.concatenate([output_shard, seq_swap(output_shard, X_HIGH)])
    queries, outputs, flat_neighbours = fence(
        [queries, outputs, flat_neighbours], [neighbours_beside, normed_beside, turned_beside]
    )
    neighbours_across = tp_swap(flat_neighbours, X_LOW)
    queries_near, queries_wrap = gather_first(queries, Z_NEAR, Z_WRAP)
    outputs_near, outputs_wrap = gather_first(outputs, Y_NEAR, Y_WRAP)
    queries_far = gather_second(
        halves(queries_near)[1], halves(queries_wrap)[0], Z_NEAR, Z_WRAP
    )
    outputs_far = gather_second(
        halves(outputs_near)[1], halves(outputs_wrap)[0], Y_NEAR, Y_WRAP
    )
    queries = jnp.concatenate([queries, queries_near, *queries_far, queries_wrap])
    outputs = jnp.concatenate([outputs, outputs_near, *outputs_far, outputs_wrap])

    neighbours_both = tp_swap(neighbours_across, CORE)
    queries, outputs, normed = fence([queries, outputs, normed], [neighbours_both])
    normed_across = tp_swap(normed, X_LOW)
    queries_near, queries_wrap = gather_first(queries, Y_NEAR, Y_WRAP)
    outputs_near, outputs_wrap = gather_first(outputs, Z_NEAR, Z_WRAP)

    group_neighbours = jnp.concatenate(
        [flat_neighbours, neighbours_across, neighbours_beside, neighbours_both]
    )
    half = queries.shape[0] // 2
    *far, turned = block_steps(
        half,
        [(queries_wrap, 0), (queries_near, half), (outputs_wrap, 0), (outputs_near, half)],
        [],
        [turned],
        [normed_across, group_neighbours],
    )
    turned_across = tp_swap(turned, X_LOW)
    query_pieces = [
        queries,
        queries_near,
        seq_swap(far[0], Y_NEAR),
        seq_swap(far[1], Y_WRAP),
        queries_wrap,
    ]
    output_pieces = [
        outputs,
        outputs_near,
        seq_swap(far[2], Z_NEAR),
        seq_swap(far[3], Z_WRAP),
        outputs_wrap,
    ]
    (normed_across,) = fence([normed_across], [*query_pieces[2:4], *output_pieces[2:4]])
    normed_both = tp_swap(normed_across, CORE)
    turned_both = tp_swap(turned_across, CORE)
    group_normed = [normed, normed_across, normed_beside, normed_both]
    group_cotangent = [turned, turned_across, turned_beside, turned_both]
    full_keyval = compact(seq_index, query_pieces, output_pieces, weight_rows, enc_rows)
    keyvals = dot(group_neighbours, full_keyval, 1, 0).astype(jnp.bfloat16)
    query, full_query = weight_call(group_normed, query_pieces, weight_rows)
    attended_grad, full_output = weight_call(group_cotangent, output_pieces, weight_rows)

    block = jnp.arange(spans, dtype=jnp.int32)
    mask = (block // (spans // tp_count)) ^ column.astype(jnp.int32)
    place = ((mask % 2) * 2 + mask // 2) * (spans // tp_count) + block % (spans // tp_count)
    places = jnp.concatenate([place, place[:1]])
    groups = LENGTH // group_tokens
    inside = [i for i in range(seq_count) if i % groups]
    first_row = place[0] * SPAN

    def first_block(value):
        return lax.dynamic_slice(value, (first_row, 0), (SPAN, local_width))

    following = lax.ppermute(
        jnp.concatenate([first_block(query), first_block(attended_grad)]),
        "seq",
        [(i, i - 1) for i in inside],
    )
    attended, query_back, keyval_back, ends = attention(
        places, query, attended_grad, following, keyvals
    )
    arrived = lax.ppermute(ends, "seq", [(i - 1, i) for i in inside])

    def with_previous(value, part):
        block = first_block(value) + arrived[part * SPAN : (part + 1) * SPAN]
        return lax.dynamic_update_slice(value, block, (first_row, 0))

    attended, query_back = with_previous(attended, 0), with_previous(query_back, 1)

    feature_part = dot(query_back, full_query, 1, 1).astype(jnp.bfloat16)
    feature_own, feature_beside = swap_half(feature_part)
    where_from = mask_of(jnp.arange(seq_count, dtype=jnp.int32) ^ me, True)
    gain_total = jnp.sum(column_sums(group_normed, feature_part), axis=0)
    gain_total = jnp.take(
        gain_total.reshape(seq_count, features // seq_count), where_from, axis=0
    )

    keyval_part = dot(group_neighbours, keyval_back, 0, 0).astype(jnp.bfloat16)
    mixed_part = dot(attended, full_output, 1, 1).astype(jnp.bfloat16)
    mixed_own, mixed_beside = swap_half(mixed_part)
    neighbour_part = dot(keyval_back, full_keyval, 1, 1).astype(jnp.bfloat16)
    neighbour_kept, neighbour_sent = half_sums(*swap_half(neighbour_part))
    extra_shape = jax.ShapeDtypeStruct((seq_count, padded, local_width), jnp.bfloat16)
    key_part, value_part = row_call(
        spread_kernel, seq_index, (keyval_part,), [extra_shape, extra_shape]
    )

    eighth = seq_count // 8
    sizes = [2 * eighth, 2 * eighth, eighth, eighth, 2 * eighth]
    query_own, query_near, query_low, query_high, query_wrap = grad_call(
        group_normed, query_back, key_part, sizes
    )
    output_own, output_near, output_low, output_high, output_wrap = grad_call(
        group_cotangent, attended, value_part, sizes
    )
    for swap, mask in (
        (tp_swap, CORE),
        (tp_swap, X_LOW),
        (seq_swap, X_HIGH),
        (seq_swap, Y_NEAR),
        (seq_swap, Y_WRAP),
        (seq_swap, Z_NEAR),
        (seq_swap, Z_WRAP),
    ):
        gain_total = gain_total + swap(gain_total, mask)
    gain_grad = gain_total.reshape(features) / norm_gain

    query_low, query_high, output_low, output_high, neighbour_sent = fence(
        [query_low, query_high, output_low, output_high, neighbour_sent],
        [gain_grad, mixed_beside, feature_beside],
    )
    mixed_kept, mixed_sent = half_sums(mixed_own, mixed_beside)
    feature_kept, feature_sent = half_sums(feature_own, feature_beside)
    query_low, query_high = seq_swap(query_low, Y_WRAP), seq_swap(query_high, Y_NEAR)
    output_low, output_high = seq_swap(output_low, Z_WRAP), seq_swap(output_high, Z_NEAR)
    neighbour_across = tp_swap(neighbour_sent, X_LOW)
    query_near, query_wrap, output_near, output_wrap, mixed_sent = block_steps(
        eighth,
        [],
        [
            (query_near, query_low, 0),
            (query_wrap, query_high, eighth),
            (output_near, output_low, 0),
            (output_wrap, output_high, eighth),
        ],
        [mixed_sent],
        [neighbour_across],
    )
    mixed_across = tp_swap(mixed_sent, X_LOW)
    feature_first, feature_last = halves(feature_sent)
    query_cut, output_cut, (feature_first, feature_last) = sum_and_split(
        [
            [query_own, seq_swap(query_near, Y_NEAR), seq_swap(query_wrap, Y_WRAP)],
            [output_own, seq_swap(output_near, Z_NEAR), seq_swap(output_wrap, Z_WRAP)],
        ],
        [2, 2, 2, 2],
        [feature_first, feature_last],
        [mixed_across],
    )
    query_own, query_near, query_far, query_wrap = query_cut
    output_own, output_near, output_far, output_wrap = output_cut
    feature_first = tp_swap(feature_first, X_LOW)
    query_wrap, output_wrap, feature_last = block_steps(
        2,
        [],
        [
            (query_wrap, seq_swap(query_far, Z_NEAR), 0),
            (output_wrap, seq_swap(output_far, Y_NEAR), 0),
        ],
        [feature_last],
        [feature_first],
    )
    feature_last = tp_swap(feature_last, X_LOW)
    feature_across = jnp.concatenate([feature_first, feature_last])
    queries = narrow_sum(query_own, seq_swap(query_near, Z_NEAR), seq_swap(query_wrap, Z_WRAP))
    outputs = narrow_sum(
        output_own, seq_swap(output_near, Y_NEAR), seq_swap(output_wrap, Y_WRAP)
    )
    outputs, queries = fence([outputs, queries], [feature_last])
    output_total = f32_sum(outputs[0], seq_swap(outputs[1], X_HIGH))
    query_total = f32_sum(queries[0], seq_swap(queries[1], X_HIGH))
    output_grad, query_grad = output_total[:weight_rows], query_total[:weight_rows]
    keyval_grad = jnp.stack(
        [
            query_total[weight_rows : weight_rows + enc_rows],
            output_total[weight_rows : weight_rows + enc_rows],
        ],
        axis=1,
    )

    (layer_output,) = row_call(
        output_kernel, seq_index, (residual, mixed_kept, mixed_across), [token_shape]
    )
    (residual_grad,) = row_call(
        residual_kernel,
        seq_index,
        (residual, gain_row, cotangent, feature_kept, feature_across),
        [token_shape],
        [pltpu.VMEM(residual.shape, jnp.float32)],
    )
    neighbour_grad = (
        f32_sum(neighbour_kept, neighbour_across).astype(jnp.bfloat16).reshape(neighbours.shape)
    )
    return (
        layer_output,
        residual_grad,
        neighbour_grad,
        gain_grad,
        query_grad,
        keyval_grad,
        output_grad,
    )


def solution(mesh):
    in_specs = (
        P(("seq", "tp"), None),
        P(),
        P("seq", "tp"),
        P("seq", None, "tp"),
        P("seq", "tp"),
        P(("seq", "tp"), None, None),
        P(("seq", "tp"), None),
    )
    out_specs = (
        P(("seq", "tp"), None),
        P(("seq", "tp"), None),
        P(("seq", "tp"), None, None),
        P(),
        P("seq", "tp"),
        P("seq", None, "tp"),
        P("seq", "tp"),
    )
    return jax.shard_map(
        per_device, mesh=mesh, in_specs=in_specs, out_specs=out_specs, check_vma=False
    )
```

```python
import functools
import math

import jax
import jax.numpy as jnp
from jax import lax
from jax.experimental import pallas as pl
from jax.experimental.pallas import tpu as pltpu
from jax.sharding import PartitionSpec as P

HEAD_DIM = 128
SPAN = 64
K_NB = 2
R = 128
LENGTH = 2048
EPSILON = 1e-06
LANES = 128
VMEM_BYTES = 40 * 1024 * 1024
MOST_VMEM_BYTES = 56 * 1024 * 1024

Z_NEAR, Z_WRAP = 8, 24
Y_NEAR, Y_WRAP = 2, 6
X_HIGH = 1
X_LOW, CORE = 2, 1


def seq_swap(value, mask):
    count = lax.axis_size("seq")
    return lax.ppermute(value, "seq", [(i, i ^ mask) for i in range(count)])


def tp_swap(value, mask):
    count = lax.axis_size("tp")
    return lax.ppermute(value, "tp", [(i, i ^ mask) for i in range(count)])


def sum_over_x(value):
    count = lax.axis_size("tp")
    devices = range(count * lax.axis_size("seq"))
    near, far, beyond = [
        lax.ppermute(value, ("seq", "tp"), [(i, i ^ mask) for i in devices])
        for mask in (X_LOW, X_HIGH * count, X_HIGH * count + X_LOW)
    ]
    return (value + near) + (far + beyond)


def f32_sum(*terms):
    total = terms[0].astype(jnp.float32)
    for term in terms[1:]:
        total = total + term.astype(jnp.float32)
    return total


def fence(values, after):
    count = len(values)
    anywhere = pl.BlockSpec(memory_space=pl.ANY)
    return pl.pallas_call(
        lambda *refs: None,
        in_specs=[anywhere] * (count + len(after)),
        out_specs=[anywhere] * count,
        out_shape=[jax.ShapeDtypeStruct(value.shape, value.dtype) for value in values],
        input_output_aliases={i: i for i in range(count)},
    )(*values, *after)


def block_steps(count, copies, sums, held, after):
    anywhere = pl.BlockSpec(memory_space=pl.ANY)

    def spec(array, first):
        return pl.BlockSpec((1, *array.shape[1:]), lambda i: (i + first, 0, 0))

    copied, summed = len(copies), len(sums)

    def body(*refs):
        for source, out in zip(refs[:copied], refs[-copied - summed - len(held) :]):
            out[...] = source[...]
        sources = refs[copied : copied + 2 * summed]
        for i in range(summed):
            out = refs[len(refs) - summed - len(held) + i]
            out[...] = narrow_sum(sources[2 * i][...], sources[2 * i + 1][...])

    args = [array for array, _ in copies]
    in_specs = [spec(array, first) for array, first in copies]
    out_specs = [spec(array, 0) for array, _ in copies]
    out_shape = [
        jax.ShapeDtypeStruct((count, *array.shape[1:]), array.dtype) for array, _ in copies
    ]
    aliases = {}
    for array, incoming, first in sums:
        aliases[len(args)] = len(out_shape)
        args += [array, incoming]
        in_specs += [spec(array, first), spec(incoming, 0)]
        out_specs.append(spec(array, first))
        out_shape.append(jax.ShapeDtypeStruct(array.shape, array.dtype))
    for array in held:
        aliases[len(args)] = len(out_shape)
        args.append(array)
        in_specs.append(anywhere)
        out_specs.append(anywhere)
        out_shape.append(jax.ShapeDtypeStruct(array.shape, array.dtype))
    return pl.pallas_call(
        body,
        grid=(count,),
        in_specs=in_specs + [anywhere] * len(after),
        out_specs=out_specs,
        out_shape=out_shape,
        input_output_aliases=aliases,
        compiler_params=pltpu.CompilerParams(vmem_limit_bytes=VMEM_BYTES),
    )(*args, *after)


def piece_specs(sizes, block, shape):
    specs, first = [], 0
    for size in sizes:
        steps = size // block
        specs.append(
            pl.BlockSpec(
                (block, *shape), lambda i, f=first, n=steps: (jnp.clip(i - f, 0, n - 1), 0, 0)
            )
        )
        first += steps
    return specs


def store_piece(sizes, block, refs, step, value):
    first = 0
    for size, ref in zip(sizes, refs):
        end = first + size // block

        @pl.when((step >= first) & (step < end))
        def _(ref=ref):
            ref[...] = value

        first = end


def sum_and_split(groups, sizes, held, after):
    anywhere = pl.BlockSpec(memory_space=pl.ANY)
    terms, pieces = len(groups[0]), len(sizes)
    shape = groups[0][0].shape
    flat = [array for group in groups for array in group]

    def body(*refs):
        step = pl.program_id(0)
        outs = refs[len(flat) + len(held) + len(after) :]
        for i in range(len(groups)):
            total = narrow_sum(*[ref[...] for ref in refs[i * terms : (i + 1) * terms]])
            store_piece(sizes, 1, outs[i * pieces : (i + 1) * pieces], step, total)

    one = pl.BlockSpec((1, *shape[1:]), lambda i: (i, 0, 0))
    results = pl.pallas_call(
        body,
        grid=(shape[0],),
        in_specs=[one] * len(flat) + [anywhere] * (len(held) + len(after)),
        out_specs=piece_specs(sizes, 1, shape[1:]) * len(groups) + [anywhere] * len(held),
        out_shape=[
            jax.ShapeDtypeStruct((size, *shape[1:]), jnp.bfloat16)
            for _ in groups
            for size in sizes
        ]
        + [jax.ShapeDtypeStruct(array.shape, array.dtype) for array in held],
        input_output_aliases={len(flat) + i: len(groups) * pieces + i for i in range(len(held))},
        compiler_params=pltpu.CompilerParams(vmem_limit_bytes=VMEM_BYTES),
    )(*flat, *held, *after)
    cut = [results[i * pieces : (i + 1) * pieces] for i in range(len(groups))]
    return *cut, list(results[len(groups) * pieces :])


def narrow_sum(*terms):
    return f32_sum(*terms).astype(jnp.bfloat16)


def halves(value):
    half = value.shape[0] // 2
    return value[:half], value[half:]


def quarters(value):
    rows = value.shape[0] // 4
    return [value[i * rows : (i + 1) * rows] for i in range(4)]


def gather_first(block, near, wrap):
    return seq_swap(block, near), seq_swap(block, wrap)


def gather_second(from_near, from_wrap, near, wrap):
    return seq_swap(from_wrap, near), seq_swap(from_near, wrap)


def scatter_first(far, near, wrap):
    low, high = halves(far)
    return seq_swap(low, wrap), seq_swap(high, near)


def scatter_sums(to_near, to_wrap, low, high):
    near_low, near_high = halves(to_near)
    wrap_low, wrap_high = halves(to_wrap)
    return (
        jnp.concatenate([narrow_sum(near_low, low), near_high], axis=0),
        jnp.concatenate([wrap_low, narrow_sum(wrap_high, high)], axis=0),
    )


def swap_half(parts):
    own, other = halves(parts)
    return own, tp_swap(other, CORE)


def half_sums(own, beside):
    kept, sent = halves(own)
    kept_beside, sent_beside = halves(beside)
    return narrow_sum(kept, kept_beside), narrow_sum(sent, sent_beside)


def mask_of(place, y_outer):
    if not y_outer:
        return place
    y, z, x = place // 8, (place // 2) % 4, place % 2
    return z * 8 + y * 2 + x


def norm_kernel(seq_ref, residual_ref, gain_ref, cotangent_ref, normed_ref, turned_ref):
    me = seq_ref[0]
    width = residual_ref.shape[1]
    total = jnp.zeros((residual_ref.shape[0], LANES), jnp.float32)
    for place in range(width // LANES):
        piece = residual_ref[:, place * LANES : (place + 1) * LANES].astype(jnp.float32)
        total = total + piece * piece
    inverse_rms = lax.rsqrt(jnp.sum(total, axis=-1, keepdims=True) / width + EPSILON)
    for place in range(width // LANES):
        here = slice(place * LANES, (place + 1) * LANES)
        there = pl.ds(pl.multiple_of((me ^ mask_of(place, True)) * LANES, LANES), LANES)
        scaled = residual_ref[:, there].astype(jnp.float32) * inverse_rms
        normed_ref[:, here] = (scaled * gain_ref[:, there]).astype(jnp.bfloat16)
        there = pl.ds(pl.multiple_of((me ^ mask_of(place, False)) * LANES, LANES), LANES)
        turned_ref[:, here] = cotangent_ref[:, there]


def output_kernel(seq_ref, residual_ref, kept_ref, across_ref, out_ref):
    me = seq_ref[0]
    for place in range(residual_ref.shape[1] // LANES):
        here = slice(place * LANES, (place + 1) * LANES)
        there = pl.ds(pl.multiple_of((me ^ mask_of(place, False)) * LANES, LANES), LANES)
        mixed = kept_ref[:, here].astype(jnp.float32) + across_ref[:, here].astype(jnp.float32)
        out_ref[:, there] = (residual_ref[:, there].astype(jnp.float32) + mixed).astype(
            jnp.bfloat16
        )


def residual_kernel(
    seq_ref, residual_ref, gain_ref, cotangent_ref, kept_ref, across_ref, out_ref, gained_ref
):
    me = seq_ref[0]
    width = residual_ref.shape[1]
    rows = residual_ref.shape[0]
    square = jnp.zeros((rows, LANES), jnp.float32)
    cross = jnp.zeros((rows, LANES), jnp.float32)
    for place in range(width // LANES):
        here = slice(place * LANES, (place + 1) * LANES)
        there = pl.ds(pl.multiple_of((me ^ mask_of(place, True)) * LANES, LANES), LANES)
        feature = kept_ref[:, here].astype(jnp.float32) + across_ref[:, here].astype(jnp.float32)
        gained = feature * gain_ref[:, there]
        piece = residual_ref[:, there].astype(jnp.float32)
        square = square + piece * piece
        cross = cross + gained * piece
        gained_ref[:, there] = gained
    inverse_rms = lax.rsqrt(jnp.sum(square, axis=-1, keepdims=True) / width + EPSILON)
    mean = jnp.sum(cross, axis=-1, keepdims=True) * inverse_rms / width
    for place in range(width // LANES):
        here = slice(place * LANES, (place + 1) * LANES)
        scaled = residual_ref[:, here].astype(jnp.float32) * inverse_rms
        out_ref[:, here] = (
            inverse_rms * (gained_ref[:, here] - scaled * mean)
            + cotangent_ref[:, here].astype(jnp.float32)
        ).astype(jnp.bfloat16)


def compact_kernel(seq_ref, *refs):
    me = seq_ref[0]
    out_ref, keys, values = refs[-3:]
    count, _, width = keys.shape
    pieces = (len(refs) - 3) // 2
    for joined, sources in ((keys, refs[:pieces]), (values, refs[pieces : 2 * pieces])):
        first = 0
        for source in sources:
            joined[first : first + source.shape[0]] = source[...]
            first += source.shape[0]
    rows = out_ref.shape[0] // count
    for part in range(count):
        here = slice(part * rows, (part + 1) * rows)
        out_ref[here, :width] = keys[mask_of(me ^ part, True), :rows, :]
        out_ref[here, width:] = values[mask_of(me ^ part, False), :rows, :]


def compact(seq_index, query_pieces, output_pieces, first_row, rows):
    pieces = [*query_pieces, *output_pieces]
    _, all_rows, width = pieces[0].shape
    padded = all_rows - first_row
    count = sum(piece.shape[0] for piece in query_pieces)
    extra = lambda *_: (0, first_row // padded, 0)
    return pl.pallas_call(
        compact_kernel,
        grid_spec=pltpu.PrefetchScalarGridSpec(
            num_scalar_prefetch=1,
            grid=(1,),
            in_specs=[pl.BlockSpec((piece.shape[0], padded, width), extra) for piece in pieces],
            out_specs=whole((count * rows, 2 * width)),
            scratch_shapes=[pltpu.VMEM((count, padded, width), jnp.bfloat16)] * 2,
        ),
        out_shape=jax.ShapeDtypeStruct((count * rows, 2 * width), jnp.bfloat16),
        compiler_params=pltpu.CompilerParams(vmem_limit_bytes=MOST_VMEM_BYTES),
    )(seq_index, *pieces)


def spread_kernel(seq_ref, keyval_ref, keys_ref, values_ref):
    me = seq_ref[0]
    count, padded, width = keys_ref.shape
    rows = keyval_ref.shape[0] // count
    rest = jnp.zeros((padded - rows, width), jnp.bfloat16)
    for part in range(count):
        here = slice(part * rows, (part + 1) * rows)
        keys_ref[mask_of(me ^ part, True)] = jnp.concatenate([keyval_ref[here, :width], rest], axis=0)
        values_ref[mask_of(me ^ part, False)] = jnp.concatenate(
            [keyval_ref[here, width:], rest], axis=0
        )


def whole(shape):
    return pl.BlockSpec(shape, lambda *_: (0,) * len(shape))


def row_call(kernel, seq_index, args, outs, scratch=()):
    return pl.pallas_call(
        kernel,
        grid_spec=pltpu.PrefetchScalarGridSpec(
            num_scalar_prefetch=1,
            grid=(1,),
            in_specs=[whole(arg.shape) for arg in args],
            out_specs=[whole(out.shape) for out in outs],
            scratch_shapes=list(scratch),
        ),
        out_shape=outs,
        compiler_params=pltpu.CompilerParams(vmem_limit_bytes=VMEM_BYTES),
    )(seq_index, *args)


def dot(left, right, left_dim, right_dim):
    return lax.dot_general(
        left, right, (((left_dim,), (right_dim,)), ((), ())), preferred_element_type=jnp.float32
    )


def weight_kernel(starts, parts, *refs):
    tokens, pieces = refs[:parts], refs[parts:-3]
    product_ref, full_ref, total = refs[-3:]
    step = pl.program_id(0)
    count = pieces[0].shape[0]
    rows, width = full_ref.shape[0] // count, full_ref.shape[1]
    for piece, first, end in zip(pieces, starts, starts[1:]):

        @pl.when((step >= first) & (step < end))
        def _(piece=piece):
            full_ref[...] = piece[...].reshape(count * rows, width)

    @pl.when(step == 0)
    def _():
        total[...] = jnp.zeros_like(total)

    total[...] += dot(jnp.concatenate([ref[...] for ref in tokens]), full_ref[...], 1, 0)

    @pl.when(step == pl.num_programs(0) - 1)
    def _():
        product_ref[...] = total[...].astype(jnp.bfloat16)


def weight_call(tokens, pieces, rows):
    shards = min(piece.shape[0] for piece in pieces)
    width = pieces[0].shape[2]
    starts = [0]
    for piece in pieces:
        starts.append(starts[-1] + piece.shape[0] // shards)
    steps = starts[-1]
    token_rows = tokens[0].shape[0]
    all_tokens = token_rows * len(tokens)
    return pl.pallas_call(
        functools.partial(weight_kernel, tuple(starts), len(tokens)),
        grid=(steps,),
        in_specs=[pl.BlockSpec((token_rows, shards * rows), lambda i: (0, i))] * len(tokens)
        + piece_specs([piece.shape[0] for piece in pieces], shards, (rows, width)),
        out_specs=[
            whole((all_tokens, width)),
            pl.BlockSpec((shards * rows, width), lambda i: (i, 0)),
        ],
        out_shape=[
            jax.ShapeDtypeStruct((all_tokens, width), jnp.bfloat16),
            jax.ShapeDtypeStruct((steps * shards * rows, width), jnp.bfloat16),
        ],
        scratch_shapes=[pltpu.VMEM((all_tokens, width), jnp.float32)],
        compiler_params=pltpu.CompilerParams(vmem_limit_bytes=MOST_VMEM_BYTES),
    )(*tokens, *pieces)


def grad_kernel(sizes, parts, *refs):
    tokens, (back_ref, extra_ref), pieces = refs[:parts], refs[parts : parts + 2], refs[parts + 2 :]
    joined = jnp.concatenate([ref[...] for ref in tokens])
    product = dot(joined, back_ref[...], 0, 0)
    count, _, width = extra_ref.shape
    shards = product.astype(jnp.bfloat16).reshape(count, product.shape[0] // count, width)
    value = jnp.concatenate([shards, extra_ref[...]], axis=1)
    store_piece(sizes, count, pieces, pl.program_id(0), value)


def grad_call(tokens, back, extra, sizes):
    shards = min(sizes)
    count, padded, width = extra.shape
    features = tokens[0].shape[1]
    columns = features // count * shards
    rows = features // count + padded
    return pl.pallas_call(
        functools.partial(grad_kernel, tuple(sizes), len(tokens)),
        grid=(count // shards,),
        in_specs=[pl.BlockSpec((tokens[0].shape[0], columns), lambda i: (0, i))] * len(tokens)
        + [whole(back.shape), pl.BlockSpec((shards, padded, width), lambda i: (i, 0, 0))],
        out_specs=piece_specs(sizes, shards, (rows, width)),
        out_shape=[jax.ShapeDtypeStruct((size, rows, width), jnp.bfloat16) for size in sizes],
        cost_estimate=pl.CostEstimate(
            flops=2 * back.shape[0] * features * width,
            bytes_accessed=8 * features * width,
            transcendentals=0,
        ),
        compiler_params=pltpu.CompilerParams(vmem_limit_bytes=MOST_VMEM_BYTES),
    )(*tokens, back, extra)


def column_kernel(parts, *refs):
    tokens, feature_ref, out_ref = refs[:parts], refs[parts], refs[parts + 1]
    joined = jnp.concatenate([ref[...] for ref in tokens]).astype(jnp.float32)
    product = joined * feature_ref[...].astype(jnp.float32)
    rows, columns = product.shape
    out_ref[...] = jnp.sum(product.reshape(rows // 8, 8, columns), axis=0)


def column_sums(tokens, feature):
    rows, features = feature.shape
    columns = features // 8
    return pl.pallas_call(
        functools.partial(column_kernel, len(tokens)),
        grid=(8,),
        in_specs=[pl.BlockSpec((tokens[0].shape[0], columns), lambda i: (0, i))] * len(tokens)
        + [pl.BlockSpec((rows, columns), lambda i: (0, i))],
        out_specs=pl.BlockSpec((8, columns), lambda i: (0, i)),
        out_shape=jax.ShapeDtypeStruct((8, features), jnp.float32),
        compiler_params=pltpu.CompilerParams(vmem_limit_bytes=VMEM_BYTES),
    )(*tokens, feature)


def attention_kernel(
    place_ref,
    query_ref,
    up_ref,
    next_ref,
    keyval_ref,
    attended_ref,
    query_back_ref,
    keyval_back_ref,
    end_ref,
    attended_carry,
    query_carry,
):
    span = pl.program_id(0)
    last = pl.num_programs(0) - 1
    width = query_ref.shape[1]
    rows = lax.broadcasted_iota(jnp.int32, (SPAN, width), 0)
    here = pl.ds(pl.multiple_of(place_ref[span] * SPAN, SPAN), SPAN)
    after = pl.ds(pl.multiple_of(place_ref[span + 1] * SPAN, SPAN), SPAN)

    @pl.when(span == 0)
    def _():
        attended_carry[...] = jnp.zeros_like(attended_carry)
        query_carry[...] = jnp.zeros_like(query_carry)

    def shifted(ref, part):
        first = ref[here, :].astype(jnp.float32)
        following = next_ref[part * SPAN : (part + 1) * SPAN, :]
        second = jnp.where(span == last, following, ref[after, :]).astype(jnp.float32)
        joined = jnp.where(rows == SPAN - 1, first, second)
        return pltpu.roll(joined, 1, 0).astype(jnp.bfloat16)

    query = shifted(query_ref, 0)
    up = shifted(up_ref, 1)
    factor = 1.0 / math.sqrt(HEAD_DIM)
    attended_parts, query_parts = [], []
    for head in range(width // HEAD_DIM):
        own = slice(head * HEAD_DIM, (head + 1) * HEAD_DIM)
        value_own = slice(width + head * HEAD_DIM, width + (head + 1) * HEAD_DIM)
        q, u = query[:, own], up[:, own]
        keys, values = keyval_ref[:, own], keyval_ref[:, value_own]
        scores = dot(q, keys, 1, 1) * factor
        exponent = jnp.exp(scores - jnp.max(scores, axis=-1, keepdims=True))
        probabilities = exponent / jnp.sum(exponent, axis=-1, keepdims=True)
        weights = probabilities.astype(jnp.bfloat16)
        attended_parts.append(dot(weights, values, 1, 0))
        weight_grad = dot(u, values, 1, 1)
        inner = jnp.sum(weight_grad * probabilities, axis=-1, keepdims=True)
        score_grad = (probabilities * (weight_grad - inner) * factor).astype(jnp.bfloat16)
        query_parts.append(dot(score_grad, keys, 1, 0))
        keyval_back_ref[:, own] = dot(score_grad, q, 0, 0).astype(jnp.bfloat16)
        keyval_back_ref[:, value_own] = dot(weights, u, 0, 0).astype(jnp.bfloat16)
    for part, (parts, carry, out_ref) in enumerate(
        (
            (attended_parts, attended_carry, attended_ref),
            (query_parts, query_carry, query_back_ref),
        )
    ):
        turned = pltpu.roll(jnp.concatenate(parts, axis=1), SPAN - 1, 0)
        out_ref[...] = jnp.where(rows == SPAN - 1, turned, carry[...]).astype(jnp.bfloat16)
        carry[...] = turned
        end_ref[part * SPAN : (part + 1) * SPAN, :] = jnp.where(
            rows == SPAN - 1, 0.0, turned
        ).astype(jnp.bfloat16)


def attention(places, query, up, following, keyvals):
    tokens, width = query.shape
    spans = tokens // SPAN
    span_rows = keyvals.shape[0] // spans
    by_place = lambda i, places: (places[i], 0)
    like = lambda array: jax.ShapeDtypeStruct(array.shape, jnp.bfloat16)
    return pl.pallas_call(
        attention_kernel,
        grid_spec=pltpu.PrefetchScalarGridSpec(
            num_scalar_prefetch=1,
            grid=(spans,),
            in_specs=[
                whole(query.shape),
                whole(up.shape),
                whole(following.shape),
                pl.BlockSpec((span_rows, keyvals.shape[1]), by_place),
            ],
            out_specs=[
                pl.BlockSpec((SPAN, width), by_place),
                pl.BlockSpec((SPAN, width), by_place),
                pl.BlockSpec((span_rows, keyvals.shape[1]), by_place),
                whole(following.shape),
            ],
            scratch_shapes=[
                pltpu.VMEM((SPAN, width), jnp.float32),
                pltpu.VMEM((SPAN, width), jnp.float32),
            ],
        ),
        out_shape=[
            like(query),
            like(query),
            like(keyvals),
            like(following),
        ],
        compiler_params=pltpu.CompilerParams(vmem_limit_bytes=VMEM_BYTES),
    )(places, query, up, following, keyvals)


def per_device(
    residual, norm_gain, query_weight, keyval_weight, output_weight, neighbours, cotangent
):
    me, seq_count = lax.axis_index("seq"), lax.axis_size("seq")
    column, tp_count = lax.axis_index("tp"), lax.axis_size("tp")
    tokens_here, features = residual.shape
    local_width = query_weight.shape[1]
    neighbour_count, _, enc_width = neighbours.shape
    enc_rows = keyval_weight.shape[0]
    group_tokens = tokens_here * tp_count
    spans = group_tokens // SPAN
    seq_index = me.astype(jnp.int32).reshape(1)
    gain_row = norm_gain.reshape(1, features)
    token_shape = jax.ShapeDtypeStruct(residual.shape, jnp.bfloat16)

    weight_rows = query_weight.shape[0]
    padded = -(-enc_rows // 16) * 16
    padding = ((0, padded - enc_rows), (0, 0))
    query_shard = jnp.concatenate([query_weight, jnp.pad(keyval_weight[:, 0], padding)])[None]
    output_shard = jnp.concatenate([output_weight, jnp.pad(keyval_weight[:, 1], padding)])[None]
    flat_neighbours = neighbours.reshape(neighbour_count * R, enc_width)
    normed, turned = row_call(
        norm_kernel, seq_index, (residual, gain_row, cotangent), [token_shape, token_shape]
    )

    neighbours_beside = tp_swap(flat_neighbours, CORE)
    normed_beside, turned_beside = tp_swap(normed, CORE), tp_swap(turned, CORE)
    queries = jnp.concatenate([query_shard, seq_swap(query_shard, X_HIGH)])
    outputs = jnp.concatenate([output_shard, seq_swap(output_shard, X_HIGH)])
    queries, outputs, flat_neighbours = fence(
        [queries, outputs, flat_neighbours], [neighbours_beside, normed_beside, turned_beside]
    )
    neighbours_across = tp_swap(flat_neighbours, X_LOW)
    queries_near, queries_wrap = gather_first(queries, Z_NEAR, Z_WRAP)
    outputs_near, outputs_wrap = gather_first(outputs, Y_NEAR, Y_WRAP)
    queries_far = gather_second(
        halves(queries_near)[1], halves(queries_wrap)[0], Z_NEAR, Z_WRAP
    )
    outputs_far = gather_second(
        halves(outputs_near)[1], halves(outputs_wrap)[0], Y_NEAR, Y_WRAP
    )
    queries = jnp.concatenate([queries, queries_near, *queries_far, queries_wrap])
    outputs = jnp.concatenate([outputs, outputs_near, *outputs_far, outputs_wrap])

    neighbours_both = tp_swap(neighbours_across, CORE)
    queries, outputs, normed = fence([queries, outputs, normed], [neighbours_both])
    normed_across = tp_swap(normed, X_LOW)
    queries_near, queries_wrap = gather_first(queries, Y_NEAR, Y_WRAP)
    outputs_near, outputs_wrap = gather_first(outputs, Z_NEAR, Z_WRAP)

    group_neighbours = jnp.concatenate(
        [flat_neighbours, neighbours_across, neighbours_beside, neighbours_both]
    )
    half = queries.shape[0] // 2
    *far, turned = block_steps(
        half,
        [(queries_wrap, 0), (queries_near, half), (outputs_wrap, 0), (outputs_near, half)],
        [],
        [turned],
        [normed_across, group_neighbours],
    )
    turned_across = tp_swap(turned, X_LOW)
    query_pieces = [
        queries,
        queries_near,
        seq_swap(far[0], Y_NEAR),
        seq_swap(far[1], Y_WRAP),
        queries_wrap,
    ]
    output_pieces = [
        outputs,
        outputs_near,
        seq_swap(far[2], Z_NEAR),
        seq_swap(far[3], Z_WRAP),
        outputs_wrap,
    ]
    (normed_across,) = fence([normed_across], [*query_pieces[2:4], *output_pieces[2:4]])
    normed_both = tp_swap(normed_across, CORE)
    turned_both = tp_swap(turned_across, CORE)
    group_normed = [normed, normed_across, normed_beside, normed_both]
    group_cotangent = [turned, turned_across, turned_beside, turned_both]
    full_keyval = compact(seq_index, query_pieces, output_pieces, weight_rows, enc_rows)
    keyvals = dot(group_neighbours, full_keyval, 1, 0).astype(jnp.bfloat16)
    query, full_query = weight_call(group_normed, query_pieces, weight_rows)
    attended_grad, full_output = weight_call(group_cotangent, output_pieces, weight_rows)

    block = jnp.arange(spans, dtype=jnp.int32)
    mask = (block // (spans // tp_count)) ^ column.astype(jnp.int32)
    place = ((mask % 2) * 2 + mask // 2) * (spans // tp_count) + block % (spans // tp_count)
    places = jnp.concatenate([place, place[:1]])
    groups = LENGTH // group_tokens
    inside = [i for i in range(seq_count) if i % groups]
    first_row = place[0] * SPAN

    def first_block(value):
        return lax.dynamic_slice(value, (first_row, 0), (SPAN, local_width))

    following = lax.ppermute(
        jnp.concatenate([first_block(query), first_block(attended_grad)]),
        "seq",
        [(i, i - 1) for i in inside],
    )
    attended, query_back, keyval_back, ends = attention(
        places, query, attended_grad, following, keyvals
    )
    arrived = lax.ppermute(ends, "seq", [(i - 1, i) for i in inside])

    def with_previous(value, part):
        block = first_block(value) + arrived[part * SPAN : (part + 1) * SPAN]
        return lax.dynamic_update_slice(value, block, (first_row, 0))

    attended, query_back = with_previous(attended, 0), with_previous(query_back, 1)

    feature_part = dot(query_back, full_query, 1, 1).astype(jnp.bfloat16)
    feature_own, feature_beside = swap_half(feature_part)
    where_from = mask_of(jnp.arange(seq_count, dtype=jnp.int32) ^ me, True)
    gain_total = jnp.sum(column_sums(group_normed, feature_part), axis=0)
    gain_total = jnp.take(
        gain_total.reshape(seq_count, features // seq_count), where_from, axis=0
    )

    keyval_part = dot(group_neighbours, keyval_back, 0, 0).astype(jnp.bfloat16)
    mixed_part = dot(attended, full_output, 1, 1).astype(jnp.bfloat16)
    mixed_own, mixed_beside = swap_half(mixed_part)
    neighbour_part = dot(keyval_back, full_keyval, 1, 1).astype(jnp.bfloat16)
    neighbour_kept, neighbour_sent = half_sums(*swap_half(neighbour_part))
    extra_shape = jax.ShapeDtypeStruct((seq_count, padded, local_width), jnp.bfloat16)
    key_part, value_part = row_call(
        spread_kernel, seq_index, (keyval_part,), [extra_shape, extra_shape]
    )

    eighth = seq_count // 8
    sizes = [2 * eighth, 2 * eighth, eighth, eighth, 2 * eighth]
    query_own, query_near, query_low, query_high, query_wrap = grad_call(
        group_normed, query_back, key_part, sizes
    )
    output_own, output_near, output_low, output_high, output_wrap = grad_call(
        group_cotangent, attended, value_part, sizes
    )
    gain_total = sum_over_x(gain_total + tp_swap(gain_total, CORE))
    for swap, mask in (
        (seq_swap, Y_NEAR),
        (seq_swap, Y_WRAP),
        (seq_swap, Z_NEAR),
        (seq_swap, Z_WRAP),
    ):
        gain_total = gain_total + swap(gain_total, mask)
    gain_grad = gain_total.reshape(features) / norm_gain

    query_low, query_high, output_low, output_high, neighbour_sent = fence(
        [query_low, query_high, output_low, output_high, neighbour_sent],
        [gain_grad, mixed_beside, feature_beside],
    )
    mixed_kept, mixed_sent = half_sums(mixed_own, mixed_beside)
    feature_kept, feature_sent = half_sums(feature_own, feature_beside)
    query_low, query_high = seq_swap(query_low, Y_WRAP), seq_swap(query_high, Y_NEAR)
    output_low, output_high = seq_swap(output_low, Z_WRAP), seq_swap(output_high, Z_NEAR)
    neighbour_across = tp_swap(neighbour_sent, X_LOW)
    query_near, query_wrap, output_near, output_wrap = block_steps(
        eighth,
        [],
        [
            (query_near, query_low, 0),
            (query_wrap, query_high, eighth),
            (output_near, output_low, 0),
            (output_wrap, output_high, eighth),
        ],
        [],
        [],
    )
    (mixed_sent,) = fence([mixed_sent], [neighbour_across])
    mixed_across = tp_swap(mixed_sent, X_LOW)
    feature_first, feature_last = halves(feature_sent)
    query_cut, output_cut, (feature_first, feature_last) = sum_and_split(
        [
            [query_own, seq_swap(query_near, Y_NEAR), seq_swap(query_wrap, Y_WRAP)],
            [output_own, seq_swap(output_near, Z_NEAR), seq_swap(output_wrap, Z_WRAP)],
        ],
        [2, 2, 2, 2],
        [feature_first, feature_last],
        [mixed_across],
    )
    query_own, query_near, query_far, query_wrap = query_cut
    output_own, output_near, output_far, output_wrap = output_cut
    feature_first = tp_swap(feature_first, X_LOW)
    query_wrap, output_wrap, feature_last = block_steps(
        2,
        [],
        [
            (query_wrap, seq_swap(query_far, Z_NEAR), 0),
            (output_wrap, seq_swap(output_far, Y_NEAR), 0),
        ],
        [feature_last],
        [feature_first],
    )
    feature_last = tp_swap(feature_last, X_LOW)
    feature_across = jnp.concatenate([feature_first, feature_last])
    queries = narrow_sum(query_own, seq_swap(query_near, Z_NEAR), seq_swap(query_wrap, Z_WRAP))
    outputs = narrow_sum(
        output_own, seq_swap(output_near, Y_NEAR), seq_swap(output_wrap, Y_WRAP)
    )
    outputs, queries = fence([outputs, queries], [feature_last])
    output_total = f32_sum(outputs[0], seq_swap(outputs[1], X_HIGH))
    query_total = f32_sum(queries[0], seq_swap(queries[1], X_HIGH))
    output_grad, query_grad = output_total[:weight_rows], query_total[:weight_rows]
    keyval_grad = jnp.stack(
        [
            query_total[weight_rows : weight_rows + enc_rows],
            output_total[weight_rows : weight_rows + enc_rows],
        ],
        axis=1,
    )

    (layer_output,) = row_call(
        output_kernel, seq_index, (residual, mixed_kept, mixed_across), [token_shape]
    )
    (residual_grad,) = row_call(
        residual_kernel,
        seq_index,
        (residual, gain_row, cotangent, feature_kept, feature_across),
        [token_shape],
        [pltpu.VMEM(residual.shape, jnp.float32)],
    )
    neighbour_grad = (
        f32_sum(neighbour_kept, neighbour_across).astype(jnp.bfloat16).reshape(neighbours.shape)
    )
    return (
        layer_output,
        residual_grad,
        neighbour_grad,
        gain_grad,
        query_grad,
        keyval_grad,
        output_grad,
    )


def solution(mesh):
    in_specs = (
        P(("seq", "tp"), None),
        P(),
        P("seq", "tp"),
        P("seq", None, "tp"),
        P("seq", "tp"),
        P(("seq", "tp"), None, None),
        P(("seq", "tp"), None),
    )
    out_specs = (
        P(("seq", "tp"), None),
        P(("seq", "tp"), None),
        P(("seq", "tp"), None, None),
        P(),
        P("seq", "tp"),
        P("seq", None, "tp"),
        P("seq", "tp"),
    )
    return jax.shard_map(
        per_device, mesh=mesh, in_specs=in_specs, out_specs=out_specs, check_vma=False
    )
```

```python
import functools
import math

import jax
import jax.numpy as jnp
from jax import lax
from jax.experimental import pallas as pl
from jax.experimental.pallas import tpu as pltpu
from jax.sharding import PartitionSpec as P

HEAD_DIM = 128
SPAN = 64
K_NB = 2
R = 128
LENGTH = 2048
EPSILON = 1e-06
LANES = 128
VMEM_BYTES = 40 * 1024 * 1024
MOST_VMEM_BYTES = 56 * 1024 * 1024

Z_NEAR, Z_WRAP = 8, 24
Y_NEAR, Y_WRAP = 2, 6
X_HIGH = 1
X_LOW, CORE = 2, 1


def seq_swap(value, mask):
    count = lax.axis_size("seq")
    return lax.ppermute(value, "seq", [(i, i ^ mask) for i in range(count)])


def tp_swap(value, mask):
    count = lax.axis_size("tp")
    return lax.ppermute(value, "tp", [(i, i ^ mask) for i in range(count)])


def f32_sum(*terms):
    total = terms[0].astype(jnp.float32)
    for term in terms[1:]:
        total = total + term.astype(jnp.float32)
    return total


def fence(values, after):
    count = len(values)
    anywhere = pl.BlockSpec(memory_space=pl.ANY)
    return pl.pallas_call(
        lambda *refs: None,
        in_specs=[anywhere] * (count + len(after)),
        out_specs=[anywhere] * count,
        out_shape=[jax.ShapeDtypeStruct(value.shape, value.dtype) for value in values],
        input_output_aliases={i: i for i in range(count)},
    )(*values, *after)


def block_steps(count, copies, sums, held, after):
    anywhere = pl.BlockSpec(memory_space=pl.ANY)

    def spec(array, first):
        return pl.BlockSpec((1, *array.shape[1:]), lambda i: (i + first, 0, 0))

    copied, summed = len(copies), len(sums)

    def body(*refs):
        for source, out in zip(refs[:copied], refs[-copied - summed - len(held) :]):
            out[...] = source[...]
        sources = refs[copied : copied + 2 * summed]
        for i in range(summed):
            out = refs[len(refs) - summed - len(held) + i]
            out[...] = narrow_sum(sources[2 * i][...], sources[2 * i + 1][...])

    args = [array for array, _ in copies]
    in_specs = [spec(array, first) for array, first in copies]
    out_specs = [spec(array, 0) for array, _ in copies]
    out_shape = [
        jax.ShapeDtypeStruct((count, *array.shape[1:]), array.dtype) for array, _ in copies
    ]
    aliases = {}
    for array, incoming, first in sums:
        aliases[len(args)] = len(out_shape)
        args += [array, incoming]
        in_specs += [spec(array, first), spec(incoming, 0)]
        out_specs.append(spec(array, first))
        out_shape.append(jax.ShapeDtypeStruct(array.shape, array.dtype))
    for array in held:
        aliases[len(args)] = len(out_shape)
        args.append(array)
        in_specs.append(anywhere)
        out_specs.append(anywhere)
        out_shape.append(jax.ShapeDtypeStruct(array.shape, array.dtype))
    return pl.pallas_call(
        body,
        grid=(count,),
        in_specs=in_specs + [anywhere] * len(after),
        out_specs=out_specs,
        out_shape=out_shape,
        input_output_aliases=aliases,
        compiler_params=pltpu.CompilerParams(vmem_limit_bytes=VMEM_BYTES),
    )(*args, *after)


def piece_specs(sizes, block, shape):
    specs, first = [], 0
    for size in sizes:
        steps = size // block
        specs.append(
            pl.BlockSpec(
                (block, *shape), lambda i, f=first, n=steps: (jnp.clip(i - f, 0, n - 1), 0, 0)
            )
        )
        first += steps
    return specs


def store_piece(sizes, block, refs, step, value):
    first = 0
    for size, ref in zip(sizes, refs):
        end = first + size // block

        @pl.when((step >= first) & (step < end))
        def _(ref=ref):
            ref[...] = value

        first = end


def sum_and_split(groups, sizes, held, after):
    anywhere = pl.BlockSpec(memory_space=pl.ANY)
    terms, pieces = len(groups[0]), len(sizes)
    shape = groups[0][0].shape
    flat = [array for group in groups for array in group]

    def body(*refs):
        step = pl.program_id(0)
        outs = refs[len(flat) + len(held) + len(after) :]
        for i in range(len(groups)):
            total = narrow_sum(*[ref[...] for ref in refs[i * terms : (i + 1) * terms]])
            store_piece(sizes, 1, outs[i * pieces : (i + 1) * pieces], step, total)

    one = pl.BlockSpec((1, *shape[1:]), lambda i: (i, 0, 0))
    results = pl.pallas_call(
        body,
        grid=(shape[0],),
        in_specs=[one] * len(flat) + [anywhere] * (len(held) + len(after)),
        out_specs=piece_specs(sizes, 1, shape[1:]) * len(groups) + [anywhere] * len(held),
        out_shape=[
            jax.ShapeDtypeStruct((size, *shape[1:]), jnp.bfloat16)
            for _ in groups
            for size in sizes
        ]
        + [jax.ShapeDtypeStruct(array.shape, array.dtype) for array in held],
        input_output_aliases={len(flat) + i: len(groups) * pieces + i for i in range(len(held))},
        compiler_params=pltpu.CompilerParams(vmem_limit_bytes=VMEM_BYTES),
    )(*flat, *held, *after)
    cut = [results[i * pieces : (i + 1) * pieces] for i in range(len(groups))]
    return *cut, list(results[len(groups) * pieces :])


def narrow_sum(*terms):
    return f32_sum(*terms).astype(jnp.bfloat16)


def halves(value):
    half = value.shape[0] // 2
    return value[:half], value[half:]


def quarters(value):
    rows = value.shape[0] // 4
    return [value[i * rows : (i + 1) * rows] for i in range(4)]


def gather_first(block, near, wrap):
    return seq_swap(block, near), seq_swap(block, wrap)


def gather_second(from_near, from_wrap, near, wrap):
    return seq_swap(from_wrap, near), seq_swap(from_near, wrap)


def scatter_first(far, near, wrap):
    low, high = halves(far)
    return seq_swap(low, wrap), seq_swap(high, near)


def scatter_sums(to_near, to_wrap, low, high):
    near_low, near_high = halves(to_near)
    wrap_low, wrap_high = halves(to_wrap)
    return (
        jnp.concatenate([narrow_sum(near_low, low), near_high], axis=0),
        jnp.concatenate([wrap_low, narrow_sum(wrap_high, high)], axis=0),
    )


def swap_half(parts):
    own, other = halves(parts)
    return own, tp_swap(other, CORE)


def half_sums(own, beside):
    kept, sent = halves(own)
    kept_beside, sent_beside = halves(beside)
    return narrow_sum(kept, kept_beside), narrow_sum(sent, sent_beside)


def mask_of(place, y_outer):
    if not y_outer:
        return place
    y, z, x = place // 8, (place // 2) % 4, place % 2
    return z * 8 + y * 2 + x


def norm_kernel(seq_ref, residual_ref, gain_ref, cotangent_ref, normed_ref, turned_ref):
    me = seq_ref[0]
    width = residual_ref.shape[1]
    total = jnp.zeros((residual_ref.shape[0], LANES), jnp.float32)
    for place in range(width // LANES):
        piece = residual_ref[:, place * LANES : (place + 1) * LANES].astype(jnp.float32)
        total = total + piece * piece
    inverse_rms = lax.rsqrt(jnp.sum(total, axis=-1, keepdims=True) / width + EPSILON)
    for place in range(width // LANES):
        here = slice(place * LANES, (place + 1) * LANES)
        there = pl.ds(pl.multiple_of((me ^ mask_of(place, True)) * LANES, LANES), LANES)
        scaled = residual_ref[:, there].astype(jnp.float32) * inverse_rms
        normed_ref[:, here] = (scaled * gain_ref[:, there]).astype(jnp.bfloat16)
        there = pl.ds(pl.multiple_of((me ^ mask_of(place, False)) * LANES, LANES), LANES)
        turned_ref[:, here] = cotangent_ref[:, there]


def output_kernel(seq_ref, residual_ref, kept_ref, across_ref, out_ref):
    me = seq_ref[0]
    for place in range(residual_ref.shape[1] // LANES):
        here = slice(place * LANES, (place + 1) * LANES)
        there = pl.ds(pl.multiple_of((me ^ mask_of(place, False)) * LANES, LANES), LANES)
        mixed = kept_ref[:, here].astype(jnp.float32) + across_ref[:, here].astype(jnp.float32)
        out_ref[:, there] = (residual_ref[:, there].astype(jnp.float32) + mixed).astype(
            jnp.bfloat16
        )


def residual_kernel(
    seq_ref, residual_ref, gain_ref, cotangent_ref, kept_ref, across_ref, out_ref, gained_ref
):
    me = seq_ref[0]
    width = residual_ref.shape[1]
    rows = residual_ref.shape[0]
    square = jnp.zeros((rows, LANES), jnp.float32)
    cross = jnp.zeros((rows, LANES), jnp.float32)
    for place in range(width // LANES):
        here = slice(place * LANES, (place + 1) * LANES)
        there = pl.ds(pl.multiple_of((me ^ mask_of(place, True)) * LANES, LANES), LANES)
        feature = kept_ref[:, here].astype(jnp.float32) + across_ref[:, here].astype(jnp.float32)
        gained = feature * gain_ref[:, there]
        piece = residual_ref[:, there].astype(jnp.float32)
        square = square + piece * piece
        cross = cross + gained * piece
        gained_ref[:, there] = gained
    inverse_rms = lax.rsqrt(jnp.sum(square, axis=-1, keepdims=True) / width + EPSILON)
    mean = jnp.sum(cross, axis=-1, keepdims=True) * inverse_rms / width
    for place in range(width // LANES):
        here = slice(place * LANES, (place + 1) * LANES)
        scaled = residual_ref[:, here].astype(jnp.float32) * inverse_rms
        out_ref[:, here] = (
            inverse_rms * (gained_ref[:, here] - scaled * mean)
            + cotangent_ref[:, here].astype(jnp.float32)
        ).astype(jnp.bfloat16)


def compact_kernel(seq_ref, *refs):
    me = seq_ref[0]
    out_ref, keys, values = refs[-3:]
    count, _, width = keys.shape
    pieces = (len(refs) - 3) // 2
    for joined, sources in ((keys, refs[:pieces]), (values, refs[pieces : 2 * pieces])):
        first = 0
        for source in sources:
            joined[first : first + source.shape[0]] = source[...]
            first += source.shape[0]
    rows = out_ref.shape[0] // count
    for part in range(count):
        here = slice(part * rows, (part + 1) * rows)
        out_ref[here, :width] = keys[mask_of(me ^ part, True), :rows, :]
        out_ref[here, width:] = values[mask_of(me ^ part, False), :rows, :]


def compact(seq_index, query_pieces, output_pieces, first_row, rows):
    pieces = [*query_pieces, *output_pieces]
    _, all_rows, width = pieces[0].shape
    padded = all_rows - first_row
    count = sum(piece.shape[0] for piece in query_pieces)
    extra = lambda *_: (0, first_row // padded, 0)
    return pl.pallas_call(
        compact_kernel,
        grid_spec=pltpu.PrefetchScalarGridSpec(
            num_scalar_prefetch=1,
            grid=(1,),
            in_specs=[pl.BlockSpec((piece.shape[0], padded, width), extra) for piece in pieces],
            out_specs=whole((count * rows, 2 * width)),
            scratch_shapes=[pltpu.VMEM((count, padded, width), jnp.bfloat16)] * 2,
        ),
        out_shape=jax.ShapeDtypeStruct((count * rows, 2 * width), jnp.bfloat16),
        compiler_params=pltpu.CompilerParams(vmem_limit_bytes=MOST_VMEM_BYTES),
    )(seq_index, *pieces)


def spread_kernel(seq_ref, keyval_ref, keys_ref, values_ref):
    me = seq_ref[0]
    count, padded, width = keys_ref.shape
    rows = keyval_ref.shape[0] // count
    rest = jnp.zeros((padded - rows, width), jnp.bfloat16)
    for part in range(count):
        here = slice(part * rows, (part + 1) * rows)
        keys_ref[mask_of(me ^ part, True)] = jnp.concatenate([keyval_ref[here, :width], rest], axis=0)
        values_ref[mask_of(me ^ part, False)] = jnp.concatenate(
            [keyval_ref[here, width:], rest], axis=0
        )


def whole(shape):
    return pl.BlockSpec(shape, lambda *_: (0,) * len(shape))


def row_call(kernel, seq_index, args, outs, scratch=()):
    return pl.pallas_call(
        kernel,
        grid_spec=pltpu.PrefetchScalarGridSpec(
            num_scalar_prefetch=1,
            grid=(1,),
            in_specs=[whole(arg.shape) for arg in args],
            out_specs=[whole(out.shape) for out in outs],
            scratch_shapes=list(scratch),
        ),
        out_shape=outs,
        compiler_params=pltpu.CompilerParams(vmem_limit_bytes=VMEM_BYTES),
    )(seq_index, *args)


def dot(left, right, left_dim, right_dim):
    return lax.dot_general(
        left, right, (((left_dim,), (right_dim,)), ((), ())), preferred_element_type=jnp.float32
    )


def weight_kernel(starts, parts, *refs):
    tokens, pieces = refs[:parts], refs[parts:-3]
    product_ref, full_ref, total = refs[-3:]
    step = pl.program_id(0)
    count = pieces[0].shape[0]
    rows, width = full_ref.shape[0] // count, full_ref.shape[1]
    for piece, first, end in zip(pieces, starts, starts[1:]):

        @pl.when((step >= first) & (step < end))
        def _(piece=piece):
            full_ref[...] = piece[...].reshape(count * rows, width)

    @pl.when(step == 0)
    def _():
        total[...] = jnp.zeros_like(total)

    total[...] += dot(jnp.concatenate([ref[...] for ref in tokens]), full_ref[...], 1, 0)

    @pl.when(step == pl.num_programs(0) - 1)
    def _():
        product_ref[...] = total[...].astype(jnp.bfloat16)


def weight_call(tokens, pieces, rows):
    shards = min(piece.shape[0] for piece in pieces)
    width = pieces[0].shape[2]
    starts = [0]
    for piece in pieces:
        starts.append(starts[-1] + piece.shape[0] // shards)
    steps = starts[-1]
    token_rows = tokens[0].shape[0]
    all_tokens = token_rows * len(tokens)
    return pl.pallas_call(
        functools.partial(weight_kernel, tuple(starts), len(tokens)),
        grid=(steps,),
        in_specs=[pl.BlockSpec((token_rows, shards * rows), lambda i: (0, i))] * len(tokens)
        + piece_specs([piece.shape[0] for piece in pieces], shards, (rows, width)),
        out_specs=[
            whole((all_tokens, width)),
            pl.BlockSpec((shards * rows, width), lambda i: (i, 0)),
        ],
        out_shape=[
            jax.ShapeDtypeStruct((all_tokens, width), jnp.bfloat16),
            jax.ShapeDtypeStruct((steps * shards * rows, width), jnp.bfloat16),
        ],
        scratch_shapes=[pltpu.VMEM((all_tokens, width), jnp.float32)],
        compiler_params=pltpu.CompilerParams(vmem_limit_bytes=MOST_VMEM_BYTES),
    )(*tokens, *pieces)


def grad_kernel(sizes, parts, *refs):
    tokens, (back_ref, extra_ref), pieces = refs[:parts], refs[parts : parts + 2], refs[parts + 2 :]
    joined = jnp.concatenate([ref[...] for ref in tokens])
    product = dot(joined, back_ref[...], 0, 0)
    count, _, width = extra_ref.shape
    shards = product.astype(jnp.bfloat16).reshape(count, product.shape[0] // count, width)
    value = jnp.concatenate([shards, extra_ref[...]], axis=1)
    store_piece(sizes, count, pieces, pl.program_id(0), value)


def grad_call(tokens, back, extra, sizes):
    shards = min(sizes)
    count, padded, width = extra.shape
    features = tokens[0].shape[1]
    columns = features // count * shards
    rows = features // count + padded
    return pl.pallas_call(
        functools.partial(grad_kernel, tuple(sizes), len(tokens)),
        grid=(count // shards,),
        in_specs=[pl.BlockSpec((tokens[0].shape[0], columns), lambda i: (0, i))] * len(tokens)
        + [whole(back.shape), pl.BlockSpec((shards, padded, width), lambda i: (i, 0, 0))],
        out_specs=piece_specs(sizes, shards, (rows, width)),
        out_shape=[jax.ShapeDtypeStruct((size, rows, width), jnp.bfloat16) for size in sizes],
        cost_estimate=pl.CostEstimate(
            flops=2 * back.shape[0] * features * width,
            bytes_accessed=8 * features * width,
            transcendentals=0,
        ),
        compiler_params=pltpu.CompilerParams(vmem_limit_bytes=MOST_VMEM_BYTES),
    )(*tokens, back, extra)


def column_kernel(parts, *refs):
    tokens, feature_ref, out_ref = refs[:parts], refs[parts], refs[parts + 1]
    joined = jnp.concatenate([ref[...] for ref in tokens]).astype(jnp.float32)
    product = joined * feature_ref[...].astype(jnp.float32)
    rows, columns = product.shape
    out_ref[...] = jnp.sum(product.reshape(rows // 8, 8, columns), axis=0)


def column_sums(tokens, feature):
    rows, features = feature.shape
    columns = features // 8
    return pl.pallas_call(
        functools.partial(column_kernel, len(tokens)),
        grid=(8,),
        in_specs=[pl.BlockSpec((tokens[0].shape[0], columns), lambda i: (0, i))] * len(tokens)
        + [pl.BlockSpec((rows, columns), lambda i: (0, i))],
        out_specs=pl.BlockSpec((8, columns), lambda i: (0, i)),
        out_shape=jax.ShapeDtypeStruct((8, features), jnp.float32),
        compiler_params=pltpu.CompilerParams(vmem_limit_bytes=VMEM_BYTES),
    )(*tokens, feature)


def attention_kernel(
    place_ref,
    query_ref,
    up_ref,
    next_ref,
    keyval_ref,
    attended_ref,
    query_back_ref,
    keyval_back_ref,
    end_ref,
    attended_carry,
    query_carry,
):
    span = pl.program_id(0)
    last = pl.num_programs(0) - 1
    width = query_ref.shape[1]
    rows = lax.broadcasted_iota(jnp.int32, (SPAN, width), 0)
    here = pl.ds(pl.multiple_of(place_ref[span] * SPAN, SPAN), SPAN)
    after = pl.ds(pl.multiple_of(place_ref[span + 1] * SPAN, SPAN), SPAN)

    @pl.when(span == 0)
    def _():
        attended_carry[...] = jnp.zeros_like(attended_carry)
        query_carry[...] = jnp.zeros_like(query_carry)

    def shifted(ref, part):
        first = ref[here, :].astype(jnp.float32)
        following = next_ref[part * SPAN : (part + 1) * SPAN, :]
        second = jnp.where(span == last, following, ref[after, :]).astype(jnp.float32)
        joined = jnp.where(rows == SPAN - 1, first, second)
        return pltpu.roll(joined, 1, 0).astype(jnp.bfloat16)

    query = shifted(query_ref, 0)
    up = shifted(up_ref, 1)
    factor = 1.0 / math.sqrt(HEAD_DIM)
    heads = [slice(first, first + HEAD_DIM) for first in range(0, width, HEAD_DIM)]
    value_heads = [slice(width + head.start, width + head.stop) for head in heads]
    queries, ups = [query[:, head] for head in heads], [up[:, head] for head in heads]
    keys = [keyval_ref[:, head] for head in heads]
    values = [keyval_ref[:, head] for head in value_heads]
    scores = [dot(q, k, 1, 1) * factor for q, k in zip(queries, keys)]
    weight_grads = [dot(u, v, 1, 1) for u, v in zip(ups, values)]
    exponents = [jnp.exp(score - jnp.max(score, axis=-1, keepdims=True)) for score in scores]
    probabilities = [e * (1.0 / jnp.sum(e, axis=-1, keepdims=True)) for e in exponents]
    weights = [p.astype(jnp.bfloat16) for p in probabilities]
    inners = [
        jnp.sum(grad * p, axis=-1, keepdims=True) for grad, p in zip(weight_grads, probabilities)
    ]
    score_grads = [
        (p * (grad - inner) * factor).astype(jnp.bfloat16)
        for p, grad, inner in zip(probabilities, weight_grads, inners)
    ]
    attended_parts = [dot(w, v, 1, 0) for w, v in zip(weights, values)]
    query_parts = [dot(g, k, 1, 0) for g, k in zip(score_grads, keys)]
    key_grads = [dot(g, q, 0, 0).astype(jnp.bfloat16) for g, q in zip(score_grads, queries)]
    value_grads = [dot(w, u, 0, 0).astype(jnp.bfloat16) for w, u in zip(weights, ups)]
    for head, value_head, key_grad, value_grad in zip(heads, value_heads, key_grads, value_grads):
        keyval_back_ref[:, head] = key_grad
        keyval_back_ref[:, value_head] = value_grad
    for part, (parts, carry, out_ref) in enumerate(
        (
            (attended_parts, attended_carry, attended_ref),
            (query_parts, query_carry, query_back_ref),
        )
    ):
        turned = pltpu.roll(jnp.concatenate(parts, axis=1), SPAN - 1, 0)
        out_ref[...] = jnp.where(rows == SPAN - 1, turned, carry[...]).astype(jnp.bfloat16)
        carry[...] = turned
        end_ref[part * SPAN : (part + 1) * SPAN, :] = jnp.where(
            rows == SPAN - 1, 0.0, turned
        ).astype(jnp.bfloat16)


def attention(places, query, up, following, keyvals):
    tokens, width = query.shape
    spans = tokens // SPAN
    span_rows = keyvals.shape[0] // spans
    by_place = lambda i, places: (places[i], 0)
    like = lambda array: jax.ShapeDtypeStruct(array.shape, jnp.bfloat16)
    return pl.pallas_call(
        attention_kernel,
        grid_spec=pltpu.PrefetchScalarGridSpec(
            num_scalar_prefetch=1,
            grid=(spans,),
            in_specs=[
                whole(query.shape),
                whole(up.shape),
                whole(following.shape),
                pl.BlockSpec((span_rows, keyvals.shape[1]), by_place),
            ],
            out_specs=[
                pl.BlockSpec((SPAN, width), by_place),
                pl.BlockSpec((SPAN, width), by_place),
                pl.BlockSpec((span_rows, keyvals.shape[1]), by_place),
                whole(following.shape),
            ],
            scratch_shapes=[
                pltpu.VMEM((SPAN, width), jnp.float32),
                pltpu.VMEM((SPAN, width), jnp.float32),
            ],
        ),
        out_shape=[
            like(query),
            like(query),
            like(keyvals),
            like(following),
        ],
        compiler_params=pltpu.CompilerParams(vmem_limit_bytes=VMEM_BYTES),
    )(places, query, up, following, keyvals)


def per_device(
    residual, norm_gain, query_weight, keyval_weight, output_weight, neighbours, cotangent
):
    me, seq_count = lax.axis_index("seq"), lax.axis_size("seq")
    column, tp_count = lax.axis_index("tp"), lax.axis_size("tp")
    tokens_here, features = residual.shape
    local_width = query_weight.shape[1]
    neighbour_count, _, enc_width = neighbours.shape
    enc_rows = keyval_weight.shape[0]
    group_tokens = tokens_here * tp_count
    spans = group_tokens // SPAN
    seq_index = me.astype(jnp.int32).reshape(1)
    gain_row = norm_gain.reshape(1, features)
    token_shape = jax.ShapeDtypeStruct(residual.shape, jnp.bfloat16)

    weight_rows = query_weight.shape[0]
    padded = -(-enc_rows // 16) * 16
    padding = ((0, padded - enc_rows), (0, 0))
    query_shard = jnp.concatenate([query_weight, jnp.pad(keyval_weight[:, 0], padding)])[None]
    output_shard = jnp.concatenate([output_weight, jnp.pad(keyval_weight[:, 1], padding)])[None]
    flat_neighbours = neighbours.reshape(neighbour_count * R, enc_width)
    normed, turned = row_call(
        norm_kernel, seq_index, (residual, gain_row, cotangent), [token_shape, token_shape]
    )

    neighbours_beside = tp_swap(flat_neighbours, CORE)
    normed_beside, turned_beside = tp_swap(normed, CORE), tp_swap(turned, CORE)
    queries = jnp.concatenate([query_shard, seq_swap(query_shard, X_HIGH)])
    outputs = jnp.concatenate([output_shard, seq_swap(output_shard, X_HIGH)])
    queries, outputs, flat_neighbours = fence(
        [queries, outputs, flat_neighbours], [neighbours_beside, normed_beside, turned_beside]
    )
    neighbours_across = tp_swap(flat_neighbours, X_LOW)
    queries_near, queries_wrap = gather_first(queries, Z_NEAR, Z_WRAP)
    outputs_near, outputs_wrap = gather_first(outputs, Y_NEAR, Y_WRAP)
    queries_far = gather_second(
        halves(queries_near)[1], halves(queries_wrap)[0], Z_NEAR, Z_WRAP
    )
    outputs_far = gather_second(
        halves(outputs_near)[1], halves(outputs_wrap)[0], Y_NEAR, Y_WRAP
    )
    queries = jnp.concatenate([queries, queries_near, *queries_far, queries_wrap])
    outputs = jnp.concatenate([outputs, outputs_near, *outputs_far, outputs_wrap])

    neighbours_both = tp_swap(neighbours_across, CORE)
    queries, outputs, normed = fence([queries, outputs, normed], [neighbours_both])
    normed_across = tp_swap(normed, X_LOW)
    queries_near, queries_wrap = gather_first(queries, Y_NEAR, Y_WRAP)
    outputs_near, outputs_wrap = gather_first(outputs, Z_NEAR, Z_WRAP)

    group_neighbours = jnp.concatenate(
        [flat_neighbours, neighbours_across, neighbours_beside, neighbours_both]
    )
    half = queries.shape[0] // 2
    *far, turned = block_steps(
        half,
        [(queries_wrap, 0), (queries_near, half), (outputs_wrap, 0), (outputs_near, half)],
        [],
        [turned],
        [normed_across, group_neighbours],
    )
    turned_across = tp_swap(turned, X_LOW)
    query_pieces = [
        queries,
        queries_near,
        seq_swap(far[0], Y_NEAR),
        seq_swap(far[1], Y_WRAP),
        queries_wrap,
    ]
    output_pieces = [
        outputs,
        outputs_near,
        seq_swap(far[2], Z_NEAR),
        seq_swap(far[3], Z_WRAP),
        outputs_wrap,
    ]
    (normed_across,) = fence([normed_across], [*query_pieces[2:4], *output_pieces[2:4]])
    normed_both = tp_swap(normed_across, CORE)
    turned_both = tp_swap(turned_across, CORE)
    group_normed = [normed, normed_across, normed_beside, normed_both]
    group_cotangent = [turned, turned_across, turned_beside, turned_both]
    full_keyval = compact(seq_index, query_pieces, output_pieces, weight_rows, enc_rows)
    keyvals = dot(group_neighbours, full_keyval, 1, 0).astype(jnp.bfloat16)
    query, full_query = weight_call(group_normed, query_pieces, weight_rows)
    attended_grad, full_output = weight_call(group_cotangent, output_pieces, weight_rows)

    block = jnp.arange(spans, dtype=jnp.int32)
    mask = (block // (spans // tp_count)) ^ column.astype(jnp.int32)
    place = ((mask % 2) * 2 + mask // 2) * (spans // tp_count) + block % (spans // tp_count)
    places = jnp.concatenate([place, place[:1]])
    groups = LENGTH // group_tokens
    inside = [i for i in range(seq_count) if i % groups]
    first_row = place[0] * SPAN

    def first_block(value):
        return lax.dynamic_slice(value, (first_row, 0), (SPAN, local_width))

    following = lax.ppermute(
        jnp.concatenate([first_block(query), first_block(attended_grad)]),
        "seq",
        [(i, i - 1) for i in inside],
    )
    attended, query_back, keyval_back, ends = attention(
        places, query, attended_grad, following, keyvals
    )
    arrived = lax.ppermute(ends, "seq", [(i - 1, i) for i in inside])

    def with_previous(value, part):
        block = first_block(value) + arrived[part * SPAN : (part + 1) * SPAN]
        return lax.dynamic_update_slice(value, block, (first_row, 0))

    attended, query_back = with_previous(attended, 0), with_previous(query_back, 1)

    feature_part = dot(query_back, full_query, 1, 1).astype(jnp.bfloat16)
    feature_own, feature_beside = swap_half(feature_part)
    where_from = mask_of(jnp.arange(seq_count, dtype=jnp.int32) ^ me, True)
    gain_total = jnp.sum(column_sums(group_normed, feature_part), axis=0)
    gain_total = jnp.take(
        gain_total.reshape(seq_count, features // seq_count), where_from, axis=0
    )

    keyval_part = dot(group_neighbours, keyval_back, 0, 0).astype(jnp.bfloat16)
    mixed_part = dot(attended, full_output, 1, 1).astype(jnp.bfloat16)
    mixed_own, mixed_beside = swap_half(mixed_part)
    neighbour_part = dot(keyval_back, full_keyval, 1, 1).astype(jnp.bfloat16)
    neighbour_kept, neighbour_sent = half_sums(*swap_half(neighbour_part))
    extra_shape = jax.ShapeDtypeStruct((seq_count, padded, local_width), jnp.bfloat16)
    key_part, value_part = row_call(
        spread_kernel, seq_index, (keyval_part,), [extra_shape, extra_shape]
    )

    eighth = seq_count // 8
    sizes = [2 * eighth, 2 * eighth, eighth, eighth, 2 * eighth]
    query_own, query_near, query_low, query_high, query_wrap = grad_call(
        group_normed, query_back, key_part, sizes
    )
    output_own, output_near, output_low, output_high, output_wrap = grad_call(
        group_cotangent, attended, value_part, sizes
    )
    for swap, mask in (
        (tp_swap, CORE),
        (tp_swap, X_LOW),
        (seq_swap, X_HIGH),
        (seq_swap, Y_NEAR),
        (seq_swap, Y_WRAP),
        (seq_swap, Z_NEAR),
        (seq_swap, Z_WRAP),
    ):
        gain_total = gain_total + swap(gain_total, mask)
    gain_grad = gain_total.reshape(features) / norm_gain

    query_low, query_high, output_low, output_high, neighbour_sent = fence(
        [query_low, query_high, output_low, output_high, neighbour_sent],
        [gain_grad, mixed_beside, feature_beside],
    )
    mixed_kept, mixed_sent = half_sums(mixed_own, mixed_beside)
    feature_kept, feature_sent = half_sums(feature_own, feature_beside)
    query_low, query_high = seq_swap(query_low, Y_WRAP), seq_swap(query_high, Y_NEAR)
    output_low, output_high = seq_swap(output_low, Z_WRAP), seq_swap(output_high, Z_NEAR)
    neighbour_across = tp_swap(neighbour_sent, X_LOW)
    query_near, query_wrap, output_near, output_wrap, mixed_sent = block_steps(
        eighth,
        [],
        [
            (query_near, query_low, 0),
            (query_wrap, query_high, eighth),
            (output_near, output_low, 0),
            (output_wrap, output_high, eighth),
        ],
        [mixed_sent],
        [neighbour_across],
    )
    mixed_across = tp_swap(mixed_sent, X_LOW)
    feature_first, feature_last = halves(feature_sent)
    query_cut, output_cut, (feature_first, feature_last) = sum_and_split(
        [
            [query_own, seq_swap(query_near, Y_NEAR), seq_swap(query_wrap, Y_WRAP)],
            [output_own, seq_swap(output_near, Z_NEAR), seq_swap(output_wrap, Z_WRAP)],
        ],
        [2, 2, 2, 2],
        [feature_first, feature_last],
        [mixed_across],
    )
    query_own, query_near, query_far, query_wrap = query_cut
    output_own, output_near, output_far, output_wrap = output_cut
    feature_first = tp_swap(feature_first, X_LOW)
    query_wrap, output_wrap, feature_last = block_steps(
        2,
        [],
        [
            (query_wrap, seq_swap(query_far, Z_NEAR), 0),
            (output_wrap, seq_swap(output_far, Y_NEAR), 0),
        ],
        [feature_last],
        [feature_first],
    )
    feature_last = tp_swap(feature_last, X_LOW)
    feature_across = jnp.concatenate([feature_first, feature_last])
    queries = narrow_sum(query_own, seq_swap(query_near, Z_NEAR), seq_swap(query_wrap, Z_WRAP))
    outputs = narrow_sum(
        output_own, seq_swap(output_near, Y_NEAR), seq_swap(output_wrap, Y_WRAP)
    )
    outputs, queries = fence([outputs, queries], [feature_last])
    output_total = f32_sum(outputs[0], seq_swap(outputs[1], X_HIGH))
    query_total = f32_sum(queries[0], seq_swap(queries[1], X_HIGH))
    output_grad, query_grad = output_total[:weight_rows], query_total[:weight_rows]
    keyval_grad = jnp.stack(
        [
            query_total[weight_rows : weight_rows + enc_rows],
            output_total[weight_rows : weight_rows + enc_rows],
        ],
        axis=1,
    )

    (layer_output,) = row_call(
        output_kernel, seq_index, (residual, mixed_kept, mixed_across), [token_shape]
    )
    (residual_grad,) = row_call(
        residual_kernel,
        seq_index,
        (residual, gain_row, cotangent, feature_kept, feature_across),
        [token_shape],
        [pltpu.VMEM(residual.shape, jnp.float32)],
    )
    neighbour_grad = (
        f32_sum(neighbour_kept, neighbour_across).astype(jnp.bfloat16).reshape(neighbours.shape)
    )
    return (
        layer_output,
        residual_grad,
        neighbour_grad,
        gain_grad,
        query_grad,
        keyval_grad,
        output_grad,
    )


def solution(mesh):
    in_specs = (
        P(("seq", "tp"), None),
        P(),
        P("seq", "tp"),
        P("seq", None, "tp"),
        P("seq", "tp"),
        P(("seq", "tp"), None, None),
        P(("seq", "tp"), None),
    )
    out_specs = (
        P(("seq", "tp"), None),
        P(("seq", "tp"), None),
        P(("seq", "tp"), None, None),
        P(),
        P("seq", "tp"),
        P("seq", None, "tp"),
        P("seq", "tp"),
    )
    return jax.shard_map(
        per_device, mesh=mesh, in_specs=in_specs, out_specs=out_specs, check_vma=False
    )
```

```python
import functools
import math

import jax
import jax.numpy as jnp
from jax import lax
from jax.experimental import pallas as pl
from jax.experimental.pallas import tpu as pltpu
from jax.sharding import PartitionSpec as P

HEAD_DIM = 128
SPAN = 64
K_NB = 2
R = 128
LENGTH = 2048
EPSILON = 1e-06
LANES = 128
VMEM_BYTES = 40 * 1024 * 1024
MOST_VMEM_BYTES = 56 * 1024 * 1024

Z_NEAR, Z_WRAP = 8, 24
Y_NEAR, Y_WRAP = 2, 6
X_HIGH = 1
X_LOW, CORE = 2, 1


def seq_swap(value, mask):
    count = lax.axis_size("seq")
    return lax.ppermute(value, "seq", [(i, i ^ mask) for i in range(count)])


def tp_swap(value, mask):
    count = lax.axis_size("tp")
    return lax.ppermute(value, "tp", [(i, i ^ mask) for i in range(count)])


def f32_sum(*terms):
    total = terms[0].astype(jnp.float32)
    for term in terms[1:]:
        total = total + term.astype(jnp.float32)
    return total


def fence(values, after):
    count = len(values)
    anywhere = pl.BlockSpec(memory_space=pl.ANY)
    return pl.pallas_call(
        lambda *refs: None,
        in_specs=[anywhere] * (count + len(after)),
        out_specs=[anywhere] * count,
        out_shape=[jax.ShapeDtypeStruct(value.shape, value.dtype) for value in values],
        input_output_aliases={i: i for i in range(count)},
    )(*values, *after)


def block_steps(count, copies, sums, held, after):
    anywhere = pl.BlockSpec(memory_space=pl.ANY)

    def spec(array, first):
        return pl.BlockSpec((1, *array.shape[1:]), lambda i: (i + first, 0, 0))

    copied, summed = len(copies), len(sums)

    def body(*refs):
        for source, out in zip(refs[:copied], refs[-copied - summed - len(held) :]):
            out[...] = source[...]
        sources = refs[copied : copied + 2 * summed]
        for i in range(summed):
            out = refs[len(refs) - summed - len(held) + i]
            out[...] = narrow_sum(sources[2 * i][...], sources[2 * i + 1][...])

    args = [array for array, _ in copies]
    in_specs = [spec(array, first) for array, first in copies]
    out_specs = [spec(array, 0) for array, _ in copies]
    out_shape = [
        jax.ShapeDtypeStruct((count, *array.shape[1:]), array.dtype) for array, _ in copies
    ]
    aliases = {}
    for array, incoming, first in sums:
        aliases[len(args)] = len(out_shape)
        args += [array, incoming]
        in_specs += [spec(array, first), spec(incoming, 0)]
        out_specs.append(spec(array, first))
        out_shape.append(jax.ShapeDtypeStruct(array.shape, array.dtype))
    for array in held:
        aliases[len(args)] = len(out_shape)
        args.append(array)
        in_specs.append(anywhere)
        out_specs.append(anywhere)
        out_shape.append(jax.ShapeDtypeStruct(array.shape, array.dtype))
    return pl.pallas_call(
        body,
        grid=(count,),
        in_specs=in_specs + [anywhere] * len(after),
        out_specs=out_specs,
        out_shape=out_shape,
        input_output_aliases=aliases,
        compiler_params=pltpu.CompilerParams(vmem_limit_bytes=VMEM_BYTES),
    )(*args, *after)


def piece_specs(sizes, block, shape):
    specs, first = [], 0
    for size in sizes:
        steps = size // block
        specs.append(
            pl.BlockSpec(
                (block, *shape), lambda i, f=first, n=steps: (jnp.clip(i - f, 0, n - 1), 0, 0)
            )
        )
        first += steps
    return specs


def store_piece(sizes, block, refs, step, value):
    first = 0
    for size, ref in zip(sizes, refs):
        end = first + size // block

        @pl.when((step >= first) & (step < end))
        def _(ref=ref):
            ref[...] = value

        first = end


def sum_and_split(groups, sizes, held, after):
    anywhere = pl.BlockSpec(memory_space=pl.ANY)
    terms, pieces = len(groups[0]), len(sizes)
    shape = groups[0][0].shape
    flat = [array for group in groups for array in group]

    def body(*refs):
        step = pl.program_id(0)
        outs = refs[len(flat) + len(held) + len(after) :]
        for i in range(len(groups)):
            total = narrow_sum(*[ref[...] for ref in refs[i * terms : (i + 1) * terms]])
            store_piece(sizes, 1, outs[i * pieces : (i + 1) * pieces], step, total)

    one = pl.BlockSpec((1, *shape[1:]), lambda i: (i, 0, 0))
    results = pl.pallas_call(
        body,
        grid=(shape[0],),
        in_specs=[one] * len(flat) + [anywhere] * (len(held) + len(after)),
        out_specs=piece_specs(sizes, 1, shape[1:]) * len(groups) + [anywhere] * len(held),
        out_shape=[
            jax.ShapeDtypeStruct((size, *shape[1:]), jnp.bfloat16)
            for _ in groups
            for size in sizes
        ]
        + [jax.ShapeDtypeStruct(array.shape, array.dtype) for array in held],
        input_output_aliases={len(flat) + i: len(groups) * pieces + i for i in range(len(held))},
        compiler_params=pltpu.CompilerParams(vmem_limit_bytes=VMEM_BYTES),
    )(*flat, *held, *after)
    cut = [results[i * pieces : (i + 1) * pieces] for i in range(len(groups))]
    return *cut, list(results[len(groups) * pieces :])


def narrow_sum(*terms):
    return f32_sum(*terms).astype(jnp.bfloat16)


def halves(value):
    half = value.shape[0] // 2
    return value[:half], value[half:]


def quarters(value):
    rows = value.shape[0] // 4
    return [value[i * rows : (i + 1) * rows] for i in range(4)]


def gather_first(block, near, wrap):
    return seq_swap(block, near), seq_swap(block, wrap)


def gather_second(from_near, from_wrap, near, wrap):
    return seq_swap(from_wrap, near), seq_swap(from_near, wrap)


def scatter_first(far, near, wrap):
    low, high = halves(far)
    return seq_swap(low, wrap), seq_swap(high, near)


def scatter_sums(to_near, to_wrap, low, high):
    near_low, near_high = halves(to_near)
    wrap_low, wrap_high = halves(to_wrap)
    return (
        jnp.concatenate([narrow_sum(near_low, low), near_high], axis=0),
        jnp.concatenate([wrap_low, narrow_sum(wrap_high, high)], axis=0),
    )


def swap_half(parts):
    own, other = halves(parts)
    return own, tp_swap(other, CORE)


def half_sums(own, beside):
    kept, sent = halves(own)
    kept_beside, sent_beside = halves(beside)
    return narrow_sum(kept, kept_beside), narrow_sum(sent, sent_beside)


def mask_of(place, y_outer):
    if not y_outer:
        return place
    y, z, x = place // 8, (place // 2) % 4, place % 2
    return z * 8 + y * 2 + x


def norm_kernel(seq_ref, residual_ref, gain_ref, cotangent_ref, normed_ref, turned_ref):
    me = seq_ref[0]
    width = residual_ref.shape[1]
    total = jnp.zeros((residual_ref.shape[0], LANES), jnp.float32)
    for place in range(width // LANES):
        piece = residual_ref[:, place * LANES : (place + 1) * LANES].astype(jnp.float32)
        total = total + piece * piece
    inverse_rms = lax.rsqrt(jnp.sum(total, axis=-1, keepdims=True) / width + EPSILON)
    for place in range(width // LANES):
        here = slice(place * LANES, (place + 1) * LANES)
        there = pl.ds(pl.multiple_of((me ^ mask_of(place, True)) * LANES, LANES), LANES)
        scaled = residual_ref[:, there].astype(jnp.float32) * inverse_rms
        normed_ref[:, here] = (scaled * gain_ref[:, there]).astype(jnp.bfloat16)
        there = pl.ds(pl.multiple_of((me ^ mask_of(place, False)) * LANES, LANES), LANES)
        turned_ref[:, here] = cotangent_ref[:, there]


def output_kernel(seq_ref, residual_ref, kept_ref, across_ref, out_ref):
    me = seq_ref[0]
    for place in range(residual_ref.shape[1] // LANES):
        here = slice(place * LANES, (place + 1) * LANES)
        there = pl.ds(pl.multiple_of((me ^ mask_of(place, False)) * LANES, LANES), LANES)
        mixed = kept_ref[:, here].astype(jnp.float32) + across_ref[:, here].astype(jnp.float32)
        out_ref[:, there] = (residual_ref[:, there].astype(jnp.float32) + mixed).astype(
            jnp.bfloat16
        )


def residual_kernel(
    seq_ref, residual_ref, gain_ref, cotangent_ref, kept_ref, across_ref, out_ref, gained_ref
):
    me = seq_ref[0]
    width = residual_ref.shape[1]
    rows = residual_ref.shape[0]
    square = jnp.zeros((rows, LANES), jnp.float32)
    cross = jnp.zeros((rows, LANES), jnp.float32)
    for place in range(width // LANES):
        here = slice(place * LANES, (place + 1) * LANES)
        there = pl.ds(pl.multiple_of((me ^ mask_of(place, True)) * LANES, LANES), LANES)
        feature = kept_ref[:, here].astype(jnp.float32) + across_ref[:, here].astype(jnp.float32)
        gained = feature * gain_ref[:, there]
        piece = residual_ref[:, there].astype(jnp.float32)
        square = square + piece * piece
        cross = cross + gained * piece
        gained_ref[:, there] = gained
    inverse_rms = lax.rsqrt(jnp.sum(square, axis=-1, keepdims=True) / width + EPSILON)
    mean = jnp.sum(cross, axis=-1, keepdims=True) * inverse_rms / width
    for place in range(width // LANES):
        here = slice(place * LANES, (place + 1) * LANES)
        scaled = residual_ref[:, here].astype(jnp.float32) * inverse_rms
        out_ref[:, here] = (
            inverse_rms * (gained_ref[:, here] - scaled * mean)
            + cotangent_ref[:, here].astype(jnp.float32)
        ).astype(jnp.bfloat16)


def compact_kernel(seq_ref, *refs):
    me = seq_ref[0]
    out_ref, keys, values = refs[-3:]
    count, _, width = keys.shape
    pieces = (len(refs) - 3) // 2
    for joined, sources in ((keys, refs[:pieces]), (values, refs[pieces : 2 * pieces])):
        first = 0
        for source in sources:
            joined[first : first + source.shape[0]] = source[...]
            first += source.shape[0]
    rows = out_ref.shape[0] // count
    for part in range(count):
        here = slice(part * rows, (part + 1) * rows)
        out_ref[here, :width] = keys[mask_of(me ^ part, True), :rows, :]
        out_ref[here, width:] = values[mask_of(me ^ part, False), :rows, :]


def compact(seq_index, query_pieces, output_pieces, first_row, rows):
    pieces = [*query_pieces, *output_pieces]
    _, all_rows, width = pieces[0].shape
    padded = all_rows - first_row
    count = sum(piece.shape[0] for piece in query_pieces)
    extra = lambda *_: (0, first_row // padded, 0)
    return pl.pallas_call(
        compact_kernel,
        grid_spec=pltpu.PrefetchScalarGridSpec(
            num_scalar_prefetch=1,
            grid=(1,),
            in_specs=[pl.BlockSpec((piece.shape[0], padded, width), extra) for piece in pieces],
            out_specs=whole((count * rows, 2 * width)),
            scratch_shapes=[pltpu.VMEM((count, padded, width), jnp.bfloat16)] * 2,
        ),
        out_shape=jax.ShapeDtypeStruct((count * rows, 2 * width), jnp.bfloat16),
        compiler_params=pltpu.CompilerParams(vmem_limit_bytes=MOST_VMEM_BYTES),
    )(seq_index, *pieces)


def spread_kernel(seq_ref, keyval_ref, keys_ref, values_ref):
    me = seq_ref[0]
    count, padded, width = keys_ref.shape
    rows = keyval_ref.shape[0] // count
    rest = jnp.zeros((padded - rows, width), jnp.bfloat16)
    for part in range(count):
        here = slice(part * rows, (part + 1) * rows)
        keys_ref[mask_of(me ^ part, True)] = jnp.concatenate([keyval_ref[here, :width], rest], axis=0)
        values_ref[mask_of(me ^ part, False)] = jnp.concatenate(
            [keyval_ref[here, width:], rest], axis=0
        )


def whole(shape):
    return pl.BlockSpec(shape, lambda *_: (0,) * len(shape))


def row_call(kernel, seq_index, args, outs, scratch=()):
    return pl.pallas_call(
        kernel,
        grid_spec=pltpu.PrefetchScalarGridSpec(
            num_scalar_prefetch=1,
            grid=(1,),
            in_specs=[whole(arg.shape) for arg in args],
            out_specs=[whole(out.shape) for out in outs],
            scratch_shapes=list(scratch),
        ),
        out_shape=outs,
        compiler_params=pltpu.CompilerParams(vmem_limit_bytes=VMEM_BYTES),
    )(seq_index, *args)


def dot(left, right, left_dim, right_dim):
    return lax.dot_general(
        left, right, (((left_dim,), (right_dim,)), ((), ())), preferred_element_type=jnp.float32
    )


def weight_kernel(starts, parts, *refs):
    pieces_end = parts + len(starts) - 1
    tokens, pieces, before = refs[:parts], refs[parts:pieces_end], refs[pieces_end:-3]
    product_ref, full_ref, total = refs[-3:]
    step = pl.program_id(0)
    count = pieces[0].shape[0]
    rows, width = full_ref.shape[0] // count, full_ref.shape[1]
    for piece, first, end in zip(pieces, starts, starts[1:]):

        @pl.when((step >= first) & (step < end))
        def _(piece=piece):
            full_ref[...] = piece[...].reshape(count * rows, width)

    @pl.when(step == 0)
    def _():
        total[...] = before[0][...] if before else jnp.zeros_like(total)

    total[...] += dot(jnp.concatenate([ref[...] for ref in tokens]), full_ref[...], 1, 0)

    @pl.when(step == pl.num_programs(0) - 1)
    def _():
        product_ref[...] = total[...].astype(product_ref.dtype)


def weight_call(tokens, pieces, rows, shards, place, out_type, before=()):
    width = pieces[0].shape[2]
    starts = [0]
    for piece in pieces:
        starts.append(starts[-1] + piece.shape[0] // shards)
    token_rows, features = tokens[0].shape
    product_shape = (token_rows * len(tokens), width)
    inputs = len(tokens) + len(pieces)
    before_specs = [whole(product_shape), pl.BlockSpec(memory_space=pl.ANY)] if before else []
    return pl.pallas_call(
        functools.partial(weight_kernel, tuple(starts), len(tokens)),
        grid=(starts[-1],),
        in_specs=[pl.BlockSpec((token_rows, shards * rows), lambda i: (0, place(i)))] * len(tokens)
        + piece_specs([piece.shape[0] for piece in pieces], shards, (rows, width))
        + before_specs,
        out_specs=[
            whole(product_shape),
            pl.BlockSpec((shards * rows, width), lambda i: (place(i), 0)),
        ],
        out_shape=[
            jax.ShapeDtypeStruct(product_shape, out_type),
            jax.ShapeDtypeStruct((features, width), jnp.bfloat16),
        ],
        input_output_aliases={inputs + 1: 1} if before else {},
        scratch_shapes=[pltpu.VMEM(product_shape, jnp.float32)],
        cost_estimate=pl.CostEstimate(
            flops=2 * product_shape[0] * starts[-1] * shards * rows * width,
            bytes_accessed=8 * starts[-1] * shards * rows * width,
            transcendentals=0,
        ),
        compiler_params=pltpu.CompilerParams(vmem_limit_bytes=MOST_VMEM_BYTES),
    )(*tokens, *pieces, *before)


def grad_kernel(sizes, parts, *refs):
    tokens, (back_ref, extra_ref), pieces = refs[:parts], refs[parts : parts + 2], refs[parts + 2 :]
    joined = jnp.concatenate([ref[...] for ref in tokens])
    product = dot(joined, back_ref[...], 0, 0)
    count, _, width = extra_ref.shape
    shards = product.astype(jnp.bfloat16).reshape(count, product.shape[0] // count, width)
    value = jnp.concatenate([shards, extra_ref[...]], axis=1)
    store_piece(sizes, count, pieces, pl.program_id(0), value)


def grad_call(tokens, back, extra, sizes):
    shards = min(sizes)
    count, padded, width = extra.shape
    features = tokens[0].shape[1]
    columns = features // count * shards
    rows = features // count + padded
    return pl.pallas_call(
        functools.partial(grad_kernel, tuple(sizes), len(tokens)),
        grid=(count // shards,),
        in_specs=[pl.BlockSpec((tokens[0].shape[0], columns), lambda i: (0, i))] * len(tokens)
        + [whole(back.shape), pl.BlockSpec((shards, padded, width), lambda i: (i, 0, 0))],
        out_specs=piece_specs(sizes, shards, (rows, width)),
        out_shape=[jax.ShapeDtypeStruct((size, rows, width), jnp.bfloat16) for size in sizes],
        cost_estimate=pl.CostEstimate(
            flops=2 * back.shape[0] * features * width,
            bytes_accessed=8 * features * width,
            transcendentals=0,
        ),
        compiler_params=pltpu.CompilerParams(vmem_limit_bytes=MOST_VMEM_BYTES),
    )(*tokens, back, extra)


def column_kernel(parts, *refs):
    tokens, feature_ref, out_ref = refs[:parts], refs[parts], refs[parts + 1]
    joined = jnp.concatenate([ref[...] for ref in tokens]).astype(jnp.float32)
    product = joined * feature_ref[...].astype(jnp.float32)
    rows, columns = product.shape
    out_ref[...] = jnp.sum(product.reshape(rows // 8, 8, columns), axis=0)


def column_sums(tokens, feature):
    rows, features = feature.shape
    columns = features // 8
    return pl.pallas_call(
        functools.partial(column_kernel, len(tokens)),
        grid=(8,),
        in_specs=[pl.BlockSpec((tokens[0].shape[0], columns), lambda i: (0, i))] * len(tokens)
        + [pl.BlockSpec((rows, columns), lambda i: (0, i))],
        out_specs=pl.BlockSpec((8, columns), lambda i: (0, i)),
        out_shape=jax.ShapeDtypeStruct((8, features), jnp.float32),
        compiler_params=pltpu.CompilerParams(vmem_limit_bytes=VMEM_BYTES),
    )(*tokens, feature)


def attention_kernel(
    place_ref,
    query_ref,
    up_ref,
    next_ref,
    keyval_ref,
    attended_ref,
    query_back_ref,
    keyval_back_ref,
    end_ref,
    attended_carry,
    query_carry,
):
    span = pl.program_id(0)
    last = pl.num_programs(0) - 1
    width = query_ref.shape[1]
    rows = lax.broadcasted_iota(jnp.int32, (SPAN, width), 0)
    here = pl.ds(pl.multiple_of(place_ref[span] * SPAN, SPAN), SPAN)
    after = pl.ds(pl.multiple_of(place_ref[span + 1] * SPAN, SPAN), SPAN)

    @pl.when(span == 0)
    def _():
        attended_carry[...] = jnp.zeros_like(attended_carry)
        query_carry[...] = jnp.zeros_like(query_carry)

    def shifted(ref, part):
        first = ref[here, :].astype(jnp.float32)
        following = next_ref[part * SPAN : (part + 1) * SPAN, :]
        second = jnp.where(span == last, following, ref[after, :]).astype(jnp.float32)
        joined = jnp.where(rows == SPAN - 1, first, second)
        return pltpu.roll(joined, 1, 0).astype(jnp.bfloat16)

    query = shifted(query_ref, 0)
    up = shifted(up_ref, 1)
    factor = 1.0 / math.sqrt(HEAD_DIM)
    heads = [slice(first, first + HEAD_DIM) for first in range(0, width, HEAD_DIM)]
    value_heads = [slice(width + head.start, width + head.stop) for head in heads]
    queries, ups = [query[:, head] for head in heads], [up[:, head] for head in heads]
    keys = [keyval_ref[:, head] for head in heads]
    values = [keyval_ref[:, head] for head in value_heads]
    scores = [dot(q, k, 1, 1) * factor for q, k in zip(queries, keys)]
    weight_grads = [dot(u, v, 1, 1) for u, v in zip(ups, values)]
    exponents = [jnp.exp(score - jnp.max(score, axis=-1, keepdims=True)) for score in scores]
    probabilities = [e * (1.0 / jnp.sum(e, axis=-1, keepdims=True)) for e in exponents]
    weights = [p.astype(jnp.bfloat16) for p in probabilities]
    inners = [
        jnp.sum(grad * p, axis=-1, keepdims=True) for grad, p in zip(weight_grads, probabilities)
    ]
    score_grads = [
        (p * (grad - inner) * factor).astype(jnp.bfloat16)
        for p, grad, inner in zip(probabilities, weight_grads, inners)
    ]
    attended_parts = [dot(w, v, 1, 0) for w, v in zip(weights, values)]
    query_parts = [dot(g, k, 1, 0) for g, k in zip(score_grads, keys)]
    key_grads = [dot(g, q, 0, 0).astype(jnp.bfloat16) for g, q in zip(score_grads, queries)]
    value_grads = [dot(w, u, 0, 0).astype(jnp.bfloat16) for w, u in zip(weights, ups)]
    for head, value_head, key_grad, value_grad in zip(heads, value_heads, key_grads, value_grads):
        keyval_back_ref[:, head] = key_grad
        keyval_back_ref[:, value_head] = value_grad
    for part, (parts, carry, out_ref) in enumerate(
        (
            (attended_parts, attended_carry, attended_ref),
            (query_parts, query_carry, query_back_ref),
        )
    ):
        turned = pltpu.roll(jnp.concatenate(parts, axis=1), SPAN - 1, 0)
        out_ref[...] = jnp.where(rows == SPAN - 1, turned, carry[...]).astype(jnp.bfloat16)
        carry[...] = turned
        end_ref[part * SPAN : (part + 1) * SPAN, :] = jnp.where(
            rows == SPAN - 1, 0.0, turned
        ).astype(jnp.bfloat16)


def attention(places, query, up, following, keyvals):
    tokens, width = query.shape
    spans = tokens // SPAN
    span_rows = keyvals.shape[0] // spans
    by_place = lambda i, places: (places[i], 0)
    like = lambda array: jax.ShapeDtypeStruct(array.shape, jnp.bfloat16)
    return pl.pallas_call(
        attention_kernel,
        grid_spec=pltpu.PrefetchScalarGridSpec(
            num_scalar_prefetch=1,
            grid=(spans,),
            in_specs=[
                whole(query.shape),
                whole(up.shape),
                whole(following.shape),
                pl.BlockSpec((span_rows, keyvals.shape[1]), by_place),
            ],
            out_specs=[
                pl.BlockSpec((SPAN, width), by_place),
                pl.BlockSpec((SPAN, width), by_place),
                pl.BlockSpec((span_rows, keyvals.shape[1]), by_place),
                whole(following.shape),
            ],
            scratch_shapes=[
                pltpu.VMEM((SPAN, width), jnp.float32),
                pltpu.VMEM((SPAN, width), jnp.float32),
            ],
        ),
        out_shape=[
            like(query),
            like(query),
            like(keyvals),
            like(following),
        ],
        compiler_params=pltpu.CompilerParams(vmem_limit_bytes=VMEM_BYTES),
    )(places, query, up, following, keyvals)


def per_device(
    residual, norm_gain, query_weight, keyval_weight, output_weight, neighbours, cotangent
):
    me, seq_count = lax.axis_index("seq"), lax.axis_size("seq")
    column, tp_count = lax.axis_index("tp"), lax.axis_size("tp")
    tokens_here, features = residual.shape
    local_width = query_weight.shape[1]
    neighbour_count, _, enc_width = neighbours.shape
    enc_rows = keyval_weight.shape[0]
    group_tokens = tokens_here * tp_count
    spans = group_tokens // SPAN
    seq_index = me.astype(jnp.int32).reshape(1)
    gain_row = norm_gain.reshape(1, features)
    token_shape = jax.ShapeDtypeStruct(residual.shape, jnp.bfloat16)

    weight_rows = query_weight.shape[0]
    padded = -(-enc_rows // 16) * 16
    padding = ((0, padded - enc_rows), (0, 0))
    query_shard = jnp.concatenate([query_weight, jnp.pad(keyval_weight[:, 0], padding)])[None]
    output_shard = jnp.concatenate([output_weight, jnp.pad(keyval_weight[:, 1], padding)])[None]
    flat_neighbours = neighbours.reshape(neighbour_count * R, enc_width)
    normed, turned = row_call(
        norm_kernel, seq_index, (residual, gain_row, cotangent), [token_shape, token_shape]
    )

    neighbours_beside = tp_swap(flat_neighbours, CORE)
    normed_beside, turned_beside = tp_swap(normed, CORE), tp_swap(turned, CORE)
    queries = jnp.concatenate([query_shard, seq_swap(query_shard, X_HIGH)])
    outputs = jnp.concatenate([output_shard, seq_swap(output_shard, X_HIGH)])
    queries, outputs, flat_neighbours = fence(
        [queries, outputs, flat_neighbours], [neighbours_beside, normed_beside, turned_beside]
    )
    neighbours_across = tp_swap(flat_neighbours, X_LOW)
    queries_near, queries_wrap = gather_first(queries, Z_NEAR, Z_WRAP)
    outputs_near, outputs_wrap = gather_first(outputs, Y_NEAR, Y_WRAP)
    queries_far = gather_second(
        halves(queries_near)[1], halves(queries_wrap)[0], Z_NEAR, Z_WRAP
    )
    outputs_far = gather_second(
        halves(outputs_near)[1], halves(outputs_wrap)[0], Y_NEAR, Y_WRAP
    )
    queries = jnp.concatenate([queries, queries_near, *queries_far, queries_wrap])
    outputs = jnp.concatenate([outputs, outputs_near, *outputs_far, outputs_wrap])

    neighbours_both = tp_swap(neighbours_across, CORE)
    queries, outputs, normed = fence([queries, outputs, normed], [neighbours_both])
    normed_across = tp_swap(normed, X_LOW)
    queries_near, queries_wrap = gather_first(queries, Y_NEAR, Y_WRAP)
    outputs_near, outputs_wrap = gather_first(outputs, Z_NEAR, Z_WRAP)

    group_neighbours = jnp.concatenate(
        [flat_neighbours, neighbours_across, neighbours_beside, neighbours_both]
    )
    normed_both = tp_swap(normed_across, CORE)
    group_normed = [normed, normed_across, normed_beside, normed_both]
    half = queries.shape[0] // 2
    *far, turned = block_steps(
        half,
        [(queries_wrap, 0), (queries_near, half), (outputs_wrap, 0), (outputs_near, half)],
        [],
        [turned],
        [normed_both, group_neighbours],
    )
    turned_across = tp_swap(turned, X_LOW)
    query_pieces = [
        queries,
        queries_near,
        seq_swap(far[0], Y_NEAR),
        seq_swap(far[1], Y_WRAP),
        queries_wrap,
    ]
    output_pieces = [
        outputs,
        outputs_near,
        seq_swap(far[2], Z_NEAR),
        seq_swap(far[3], Z_WRAP),
        outputs_wrap,
    ]
    (turned_across,) = fence([turned_across], [*query_pieces[2:4], *output_pieces[2:4]])
    turned_both = tp_swap(turned_across, CORE)
    group_cotangent = [turned, turned_across, turned_beside, turned_both]
    full_keyval = compact(seq_index, query_pieces, output_pieces, weight_rows, enc_rows)
    keyvals = dot(group_neighbours, full_keyval, 1, 0).astype(jnp.bfloat16)
    early = weight_call(
        group_normed,
        [queries, queries_near, queries_wrap],
        weight_rows,
        half,
        lambda i: jnp.where(i < 4, i, i + 2),
        jnp.float32,
    )
    query, full_query = weight_call(
        group_normed, query_pieces[2:4], weight_rows, half, lambda i: i + 4, jnp.bfloat16, early
    )
    attended_grad, full_output = weight_call(
        group_cotangent, output_pieces, weight_rows, half, lambda i: i, jnp.bfloat16
    )

    block = jnp.arange(spans, dtype=jnp.int32)
    mask = (block // (spans // tp_count)) ^ column.astype(jnp.int32)
    place = ((mask % 2) * 2 + mask // 2) * (spans // tp_count) + block % (spans // tp_count)
    places = jnp.concatenate([place, place[:1]])
    groups = LENGTH // group_tokens
    inside = [i for i in range(seq_count) if i % groups]
    first_row = place[0] * SPAN

    def first_block(value):
        return lax.dynamic_slice(value, (first_row, 0), (SPAN, local_width))

    following = lax.ppermute(
        jnp.concatenate([first_block(query), first_block(attended_grad)]),
        "seq",
        [(i, i - 1) for i in inside],
    )
    attended, query_back, keyval_back, ends = attention(
        places, query, attended_grad, following, keyvals
    )
    arrived = lax.ppermute(ends, "seq", [(i - 1, i) for i in inside])

    def with_previous(value, part):
        block = first_block(value) + arrived[part * SPAN : (part + 1) * SPAN]
        return lax.dynamic_update_slice(value, block, (first_row, 0))

    attended, query_back = with_previous(attended, 0), with_previous(query_back, 1)

    feature_part = dot(query_back, full_query, 1, 1).astype(jnp.bfloat16)
    feature_own, feature_beside = swap_half(feature_part)
    where_from = mask_of(jnp.arange(seq_count, dtype=jnp.int32) ^ me, True)
    gain_total = jnp.sum(column_sums(group_normed, feature_part), axis=0)
    gain_total = jnp.take(
        gain_total.reshape(seq_count, features // seq_count), where_from, axis=0
    )

    keyval_part = dot(group_neighbours, keyval_back, 0, 0).astype(jnp.bfloat16)
    mixed_part = dot(attended, full_output, 1, 1).astype(jnp.bfloat16)
    mixed_own, mixed_beside = swap_half(mixed_part)
    neighbour_part = dot(keyval_back, full_keyval, 1, 1).astype(jnp.bfloat16)
    neighbour_kept, neighbour_sent = half_sums(*swap_half(neighbour_part))
    extra_shape = jax.ShapeDtypeStruct((seq_count, padded, local_width), jnp.bfloat16)
    key_part, value_part = row_call(
        spread_kernel, seq_index, (keyval_part,), [extra_shape, extra_shape]
    )

    eighth = seq_count // 8
    sizes = [2 * eighth, 2 * eighth, eighth, eighth, 2 * eighth]
    query_own, query_near, query_low, query_high, query_wrap = grad_call(
        group_normed, query_back, key_part, sizes
    )
    output_own, output_near, output_low, output_high, output_wrap = grad_call(
        group_cotangent, attended, value_part, sizes
    )
    for swap, mask in (
        (tp_swap, CORE),
        (tp_swap, X_LOW),
        (seq_swap, X_HIGH),
        (seq_swap, Y_NEAR),
        (seq_swap, Y_WRAP),
        (seq_swap, Z_NEAR),
        (seq_swap, Z_WRAP),
    ):
        gain_total = gain_total + swap(gain_total, mask)
    gain_grad = gain_total.reshape(features) / norm_gain

    query_low, query_high, output_low, output_high, neighbour_sent = fence(
        [query_low, query_high, output_low, output_high, neighbour_sent],
        [gain_grad, mixed_beside, feature_beside],
    )
    mixed_kept, mixed_sent = half_sums(mixed_own, mixed_beside)
    feature_kept, feature_sent = half_sums(feature_own, feature_beside)
    query_low, query_high = seq_swap(query_low, Y_WRAP), seq_swap(query_high, Y_NEAR)
    output_low, output_high = seq_swap(output_low, Z_WRAP), seq_swap(output_high, Z_NEAR)
    neighbour_across = tp_swap(neighbour_sent, X_LOW)
    query_near, query_wrap, output_near, output_wrap, mixed_sent = block_steps(
        eighth,
        [],
        [
            (query_near, query_low, 0),
            (query_wrap, query_high, eighth),
            (output_near, output_low, 0),
            (output_wrap, output_high, eighth),
        ],
        [mixed_sent],
        [neighbour_across],
    )
    mixed_across = tp_swap(mixed_sent, X_LOW)
    feature_first, feature_last = halves(feature_sent)
    query_cut, output_cut, (feature_first, feature_last) = sum_and_split(
        [
            [query_own, seq_swap(query_near, Y_NEAR), seq_swap(query_wrap, Y_WRAP)],
            [output_own, seq_swap(output_near, Z_NEAR), seq_swap(output_wrap, Z_WRAP)],
        ],
        [2, 2, 2, 2],
        [feature_first, feature_last],
        [mixed_across],
    )
    query_own, query_near, query_far, query_wrap = query_cut
    output_own, output_near, output_far, output_wrap = output_cut
    feature_first = tp_swap(feature_first, X_LOW)
    query_wrap, output_wrap, feature_last = block_steps(
        2,
        [],
        [
            (query_wrap, seq_swap(query_far, Z_NEAR), 0),
            (output_wrap, seq_swap(output_far, Y_NEAR), 0),
        ],
        [feature_last],
        [feature_first],
    )
    feature_last = tp_swap(feature_last, X_LOW)
    feature_across = jnp.concatenate([feature_first, feature_last])
    queries = narrow_sum(query_own, seq_swap(query_near, Z_NEAR), seq_swap(query_wrap, Z_WRAP))
    outputs = narrow_sum(
        output_own, seq_swap(output_near, Y_NEAR), seq_swap(output_wrap, Y_WRAP)
    )
    outputs, queries = fence([outputs, queries], [feature_last])
    output_total = f32_sum(outputs[0], seq_swap(outputs[1], X_HIGH))
    query_total = f32_sum(queries[0], seq_swap(queries[1], X_HIGH))
    output_grad, query_grad = output_total[:weight_rows], query_total[:weight_rows]
    keyval_grad = jnp.stack(
        [
            query_total[weight_rows : weight_rows + enc_rows],
            output_total[weight_rows : weight_rows + enc_rows],
        ],
        axis=1,
    )

    (layer_output,) = row_call(
        output_kernel, seq_index, (residual, mixed_kept, mixed_across), [token_shape]
    )
    (residual_grad,) = row_call(
        residual_kernel,
        seq_index,
        (residual, gain_row, cotangent, feature_kept, feature_across),
        [token_shape],
        [pltpu.VMEM(residual.shape, jnp.float32)],
    )
    neighbour_grad = (
        f32_sum(neighbour_kept, neighbour_across).astype(jnp.bfloat16).reshape(neighbours.shape)
    )
    return (
        layer_output,
        residual_grad,
        neighbour_grad,
        gain_grad,
        query_grad,
        keyval_grad,
        output_grad,
    )


def solution(mesh):
    in_specs = (
        P(("seq", "tp"), None),
        P(),
        P("seq", "tp"),
        P("seq", None, "tp"),
        P("seq", "tp"),
        P(("seq", "tp"), None, None),
        P(("seq", "tp"), None),
    )
    out_specs = (
        P(("seq", "tp"), None),
        P(("seq", "tp"), None),
        P(("seq", "tp"), None, None),
        P(),
        P("seq", "tp"),
        P("seq", None, "tp"),
        P("seq", "tp"),
    )
    return jax.shard_map(
        per_device, mesh=mesh, in_specs=in_specs, out_specs=out_specs, check_vma=False
    )
```

```python
import functools
import math

import jax
import jax.numpy as jnp
from jax import lax
from jax.experimental import pallas as pl
from jax.experimental.pallas import tpu as pltpu
from jax.sharding import PartitionSpec as P

HEAD_DIM = 128
SPAN = 64
K_NB = 2
R = 128
LENGTH = 2048
EPSILON = 1e-06
LANES = 128
VMEM_BYTES = 40 * 1024 * 1024
MOST_VMEM_BYTES = 56 * 1024 * 1024

Z_NEAR, Z_WRAP = 8, 24
Y_NEAR, Y_WRAP = 2, 6
X_HIGH = 1
X_LOW, CORE = 2, 1


def seq_swap(value, mask):
    count = lax.axis_size("seq")
    return lax.ppermute(value, "seq", [(i, i ^ mask) for i in range(count)])


def tp_swap(value, mask):
    count = lax.axis_size("tp")
    return lax.ppermute(value, "tp", [(i, i ^ mask) for i in range(count)])


def f32_sum(*terms):
    total = terms[0].astype(jnp.float32)
    for term in terms[1:]:
        total = total + term.astype(jnp.float32)
    return total


def fence(values, after):
    count = len(values)
    anywhere = pl.BlockSpec(memory_space=pl.ANY)
    return pl.pallas_call(
        lambda *refs: None,
        in_specs=[anywhere] * (count + len(after)),
        out_specs=[anywhere] * count,
        out_shape=[jax.ShapeDtypeStruct(value.shape, value.dtype) for value in values],
        input_output_aliases={i: i for i in range(count)},
    )(*values, *after)


def block_steps(count, copies, sums, held, after):
    anywhere = pl.BlockSpec(memory_space=pl.ANY)

    def spec(array, first):
        return pl.BlockSpec((1, *array.shape[1:]), lambda i: (i + first, 0, 0))

    copied, summed = len(copies), len(sums)

    def body(*refs):
        for source, out in zip(refs[:copied], refs[-copied - summed - len(held) :]):
            out[...] = source[...]
        sources = refs[copied : copied + 2 * summed]
        for i in range(summed):
            out = refs[len(refs) - summed - len(held) + i]
            out[...] = narrow_sum(sources[2 * i][...], sources[2 * i + 1][...])

    args = [array for array, _ in copies]
    in_specs = [spec(array, first) for array, first in copies]
    out_specs = [spec(array, 0) for array, _ in copies]
    out_shape = [
        jax.ShapeDtypeStruct((count, *array.shape[1:]), array.dtype) for array, _ in copies
    ]
    aliases = {}
    for array, incoming, first in sums:
        aliases[len(args)] = len(out_shape)
        args += [array, incoming]
        in_specs += [spec(array, first), spec(incoming, 0)]
        out_specs.append(spec(array, first))
        out_shape.append(jax.ShapeDtypeStruct(array.shape, array.dtype))
    for array in held:
        aliases[len(args)] = len(out_shape)
        args.append(array)
        in_specs.append(anywhere)
        out_specs.append(anywhere)
        out_shape.append(jax.ShapeDtypeStruct(array.shape, array.dtype))
    return pl.pallas_call(
        body,
        grid=(count,),
        in_specs=in_specs + [anywhere] * len(after),
        out_specs=out_specs,
        out_shape=out_shape,
        input_output_aliases=aliases,
        compiler_params=pltpu.CompilerParams(vmem_limit_bytes=VMEM_BYTES),
    )(*args, *after)


def piece_specs(sizes, block, shape):
    specs, first = [], 0
    for size in sizes:
        steps = size // block
        specs.append(
            pl.BlockSpec(
                (block, *shape), lambda i, f=first, n=steps: (jnp.clip(i - f, 0, n - 1), 0, 0)
            )
        )
        first += steps
    return specs


def store_piece(sizes, block, refs, step, value):
    first = 0
    for size, ref in zip(sizes, refs):
        end = first + size // block

        @pl.when((step >= first) & (step < end))
        def _(ref=ref):
            ref[...] = value

        first = end


def sum_and_split(groups, sizes, held, after):
    anywhere = pl.BlockSpec(memory_space=pl.ANY)
    terms, pieces = len(groups[0]), len(sizes)
    shape = groups[0][0].shape
    flat = [array for group in groups for array in group]

    def body(*refs):
        step = pl.program_id(0)
        outs = refs[len(flat) + len(held) + len(after) :]
        for i in range(len(groups)):
            total = narrow_sum(*[ref[...] for ref in refs[i * terms : (i + 1) * terms]])
            store_piece(sizes, 1, outs[i * pieces : (i + 1) * pieces], step, total)

    one = pl.BlockSpec((1, *shape[1:]), lambda i: (i, 0, 0))
    results = pl.pallas_call(
        body,
        grid=(shape[0],),
        in_specs=[one] * len(flat) + [anywhere] * (len(held) + len(after)),
        out_specs=piece_specs(sizes, 1, shape[1:]) * len(groups) + [anywhere] * len(held),
        out_shape=[
            jax.ShapeDtypeStruct((size, *shape[1:]), jnp.bfloat16)
            for _ in groups
            for size in sizes
        ]
        + [jax.ShapeDtypeStruct(array.shape, array.dtype) for array in held],
        input_output_aliases={len(flat) + i: len(groups) * pieces + i for i in range(len(held))},
        compiler_params=pltpu.CompilerParams(vmem_limit_bytes=VMEM_BYTES),
    )(*flat, *held, *after)
    cut = [results[i * pieces : (i + 1) * pieces] for i in range(len(groups))]
    return *cut, list(results[len(groups) * pieces :])


def narrow_sum(*terms):
    return f32_sum(*terms).astype(jnp.bfloat16)


def halves(value):
    half = value.shape[0] // 2
    return value[:half], value[half:]


def quarters(value):
    rows = value.shape[0] // 4
    return [value[i * rows : (i + 1) * rows] for i in range(4)]


def gather_first(block, near, wrap):
    return seq_swap(block, near), seq_swap(block, wrap)


def gather_second(from_near, from_wrap, near, wrap):
    return seq_swap(from_wrap, near), seq_swap(from_near, wrap)


def scatter_first(far, near, wrap):
    low, high = halves(far)
    return seq_swap(low, wrap), seq_swap(high, near)


def scatter_sums(to_near, to_wrap, low, high):
    near_low, near_high = halves(to_near)
    wrap_low, wrap_high = halves(to_wrap)
    return (
        jnp.concatenate([narrow_sum(near_low, low), near_high], axis=0),
        jnp.concatenate([wrap_low, narrow_sum(wrap_high, high)], axis=0),
    )


def swap_half(parts):
    own, other = halves(parts)
    return own, tp_swap(other, CORE)


def half_sums(own, beside):
    kept, sent = halves(own)
    kept_beside, sent_beside = halves(beside)
    return narrow_sum(kept, kept_beside), narrow_sum(sent, sent_beside)


def mask_of(place, y_outer):
    if not y_outer:
        return place
    y, z, x = place // 8, (place // 2) % 4, place % 2
    return z * 8 + y * 2 + x


def norm_kernel(seq_ref, residual_ref, gain_ref, cotangent_ref, normed_ref, turned_ref):
    me = seq_ref[0]
    width = residual_ref.shape[1]
    total = jnp.zeros((residual_ref.shape[0], LANES), jnp.float32)
    for place in range(width // LANES):
        piece = residual_ref[:, place * LANES : (place + 1) * LANES].astype(jnp.float32)
        total = total + piece * piece
    inverse_rms = lax.rsqrt(jnp.sum(total, axis=-1, keepdims=True) / width + EPSILON)
    for place in range(width // LANES):
        here = slice(place * LANES, (place + 1) * LANES)
        there = pl.ds(pl.multiple_of((me ^ mask_of(place, True)) * LANES, LANES), LANES)
        scaled = residual_ref[:, there].astype(jnp.float32) * inverse_rms
        normed_ref[:, here] = (scaled * gain_ref[:, there]).astype(jnp.bfloat16)
        there = pl.ds(pl.multiple_of((me ^ mask_of(place, False)) * LANES, LANES), LANES)
        turned_ref[:, here] = cotangent_ref[:, there]


def output_kernel(seq_ref, residual_ref, kept_ref, across_ref, out_ref):
    me = seq_ref[0]
    for place in range(residual_ref.shape[1] // LANES):
        here = slice(place * LANES, (place + 1) * LANES)
        there = pl.ds(pl.multiple_of((me ^ mask_of(place, False)) * LANES, LANES), LANES)
        mixed = kept_ref[:, here].astype(jnp.float32) + across_ref[:, here].astype(jnp.float32)
        out_ref[:, there] = (residual_ref[:, there].astype(jnp.float32) + mixed).astype(
            jnp.bfloat16
        )


def residual_kernel(
    seq_ref, residual_ref, gain_ref, cotangent_ref, kept_ref, across_ref, out_ref, gained_ref
):
    me = seq_ref[0]
    width = residual_ref.shape[1]
    rows = residual_ref.shape[0]
    square = jnp.zeros((rows, LANES), jnp.float32)
    cross = jnp.zeros((rows, LANES), jnp.float32)
    for place in range(width // LANES):
        here = slice(place * LANES, (place + 1) * LANES)
        there = pl.ds(pl.multiple_of((me ^ mask_of(place, True)) * LANES, LANES), LANES)
        feature = kept_ref[:, here].astype(jnp.float32) + across_ref[:, here].astype(jnp.float32)
        gained = feature * gain_ref[:, there]
        piece = residual_ref[:, there].astype(jnp.float32)
        square = square + piece * piece
        cross = cross + gained * piece
        gained_ref[:, there] = gained
    inverse_rms = lax.rsqrt(jnp.sum(square, axis=-1, keepdims=True) / width + EPSILON)
    mean = jnp.sum(cross, axis=-1, keepdims=True) * inverse_rms / width
    for place in range(width // LANES):
        here = slice(place * LANES, (place + 1) * LANES)
        scaled = residual_ref[:, here].astype(jnp.float32) * inverse_rms
        out_ref[:, here] = (
            inverse_rms * (gained_ref[:, here] - scaled * mean)
            + cotangent_ref[:, here].astype(jnp.float32)
        ).astype(jnp.bfloat16)


def compact_kernel(seq_ref, *refs):
    me = seq_ref[0]
    out_ref, keys, values = refs[-3:]
    count, _, width = keys.shape
    pieces = (len(refs) - 3) // 2
    for joined, sources in ((keys, refs[:pieces]), (values, refs[pieces : 2 * pieces])):
        first = 0
        for source in sources:
            joined[first : first + source.shape[0]] = source[...]
            first += source.shape[0]
    rows = out_ref.shape[0] // count
    for part in range(count):
        here = slice(part * rows, (part + 1) * rows)
        out_ref[here, :width] = keys[mask_of(me ^ part, True), :rows, :]
        out_ref[here, width:] = values[mask_of(me ^ part, False), :rows, :]


def compact(seq_index, query_pieces, output_pieces, first_row, rows):
    pieces = [*query_pieces, *output_pieces]
    _, all_rows, width = pieces[0].shape
    padded = all_rows - first_row
    count = sum(piece.shape[0] for piece in query_pieces)
    extra = lambda *_: (0, first_row // padded, 0)
    return pl.pallas_call(
        compact_kernel,
        grid_spec=pltpu.PrefetchScalarGridSpec(
            num_scalar_prefetch=1,
            grid=(1,),
            in_specs=[pl.BlockSpec((piece.shape[0], padded, width), extra) for piece in pieces],
            out_specs=whole((count * rows, 2 * width)),
            scratch_shapes=[pltpu.VMEM((count, padded, width), jnp.bfloat16)] * 2,
        ),
        out_shape=jax.ShapeDtypeStruct((count * rows, 2 * width), jnp.bfloat16),
        compiler_params=pltpu.CompilerParams(vmem_limit_bytes=MOST_VMEM_BYTES),
    )(seq_index, *pieces)


def spread_kernel(seq_ref, keyval_ref, keys_ref, values_ref):
    me = seq_ref[0]
    count, padded, width = keys_ref.shape
    rows = keyval_ref.shape[0] // count
    rest = jnp.zeros((padded - rows, width), jnp.bfloat16)
    for part in range(count):
        here = slice(part * rows, (part + 1) * rows)
        keys_ref[mask_of(me ^ part, True)] = jnp.concatenate([keyval_ref[here, :width], rest], axis=0)
        values_ref[mask_of(me ^ part, False)] = jnp.concatenate(
            [keyval_ref[here, width:], rest], axis=0
        )


def whole(shape):
    return pl.BlockSpec(shape, lambda *_: (0,) * len(shape))


def row_call(kernel, seq_index, args, outs, scratch=()):
    return pl.pallas_call(
        kernel,
        grid_spec=pltpu.PrefetchScalarGridSpec(
            num_scalar_prefetch=1,
            grid=(1,),
            in_specs=[whole(arg.shape) for arg in args],
            out_specs=[whole(out.shape) for out in outs],
            scratch_shapes=list(scratch),
        ),
        out_shape=outs,
        compiler_params=pltpu.CompilerParams(vmem_limit_bytes=VMEM_BYTES),
    )(seq_index, *args)


def dot(left, right, left_dim, right_dim):
    return lax.dot_general(
        left, right, (((left_dim,), (right_dim,)), ((), ())), preferred_element_type=jnp.float32
    )


def weight_kernel(starts, parts, *refs):
    pieces_end = parts + len(starts) - 1
    tokens, pieces, before = refs[:parts], refs[parts:pieces_end], refs[pieces_end:-3]
    product_ref, full_ref, total = refs[-3:]
    step = pl.program_id(0)
    count = pieces[0].shape[0]
    rows, width = full_ref.shape[0] // count, full_ref.shape[1]
    for piece, first, end in zip(pieces, starts, starts[1:]):

        @pl.when((step >= first) & (step < end))
        def _(piece=piece):
            full_ref[...] = piece[...].reshape(count * rows, width)

    @pl.when(step == 0)
    def _():
        total[...] = before[0][...] if before else jnp.zeros_like(total)

    total[...] += dot(jnp.concatenate([ref[...] for ref in tokens]), full_ref[...], 1, 0)

    @pl.when(step == pl.num_programs(0) - 1)
    def _():
        product_ref[...] = total[...].astype(product_ref.dtype)


def weight_call(tokens, pieces, rows, shards, place, out_type, before=()):
    width = pieces[0].shape[2]
    starts = [0]
    for piece in pieces:
        starts.append(starts[-1] + piece.shape[0] // shards)
    token_rows, features = tokens[0].shape
    product_shape = (token_rows * len(tokens), width)
    inputs = len(tokens) + len(pieces)
    before_specs = [whole(product_shape), pl.BlockSpec(memory_space=pl.ANY)] if before else []
    return pl.pallas_call(
        functools.partial(weight_kernel, tuple(starts), len(tokens)),
        grid=(starts[-1],),
        in_specs=[pl.BlockSpec((token_rows, shards * rows), lambda i: (0, place(i)))] * len(tokens)
        + piece_specs([piece.shape[0] for piece in pieces], shards, (rows, width))
        + before_specs,
        out_specs=[
            whole(product_shape),
            pl.BlockSpec((shards * rows, width), lambda i: (place(i), 0)),
        ],
        out_shape=[
            jax.ShapeDtypeStruct(product_shape, out_type),
            jax.ShapeDtypeStruct((features, width), jnp.bfloat16),
        ],
        input_output_aliases={inputs + 1: 1} if before else {},
        scratch_shapes=[pltpu.VMEM(product_shape, jnp.float32)],
        cost_estimate=pl.CostEstimate(
            flops=2 * product_shape[0] * starts[-1] * shards * rows * width,
            bytes_accessed=8 * starts[-1] * shards * rows * width,
            transcendentals=0,
        ),
        compiler_params=pltpu.CompilerParams(vmem_limit_bytes=MOST_VMEM_BYTES),
    )(*tokens, *pieces, *before)


def grad_kernel(sizes, parts, *refs):
    tokens, (back_ref, extra_ref), pieces = refs[:parts], refs[parts : parts + 2], refs[parts + 2 :]
    joined = jnp.concatenate([ref[...] for ref in tokens])
    product = dot(joined, back_ref[...], 0, 0)
    count, _, width = extra_ref.shape
    shards = product.astype(jnp.bfloat16).reshape(count, product.shape[0] // count, width)
    value = jnp.concatenate([shards, extra_ref[...]], axis=1)
    store_piece(sizes, count, pieces, pl.program_id(0), value)


def grad_call(tokens, back, extra, sizes):
    shards = min(sizes)
    count, padded, width = extra.shape
    features = tokens[0].shape[1]
    columns = features // count * shards
    rows = features // count + padded
    return pl.pallas_call(
        functools.partial(grad_kernel, tuple(sizes), len(tokens)),
        grid=(count // shards,),
        in_specs=[pl.BlockSpec((tokens[0].shape[0], columns), lambda i: (0, i))] * len(tokens)
        + [whole(back.shape), pl.BlockSpec((shards, padded, width), lambda i: (i, 0, 0))],
        out_specs=piece_specs(sizes, shards, (rows, width)),
        out_shape=[jax.ShapeDtypeStruct((size, rows, width), jnp.bfloat16) for size in sizes],
        cost_estimate=pl.CostEstimate(
            flops=2 * back.shape[0] * features * width,
            bytes_accessed=8 * features * width,
            transcendentals=0,
        ),
        compiler_params=pltpu.CompilerParams(vmem_limit_bytes=MOST_VMEM_BYTES),
    )(*tokens, back, extra)


def column_kernel(parts, *refs):
    tokens, feature_ref, out_ref = refs[:parts], refs[parts], refs[parts + 1]
    joined = jnp.concatenate([ref[...] for ref in tokens]).astype(jnp.float32)
    product = joined * feature_ref[...].astype(jnp.float32)
    rows, columns = product.shape
    out_ref[...] = jnp.sum(product.reshape(rows // 8, 8, columns), axis=0)


def column_sums(tokens, feature):
    rows, features = feature.shape
    columns = features // 8
    return pl.pallas_call(
        functools.partial(column_kernel, len(tokens)),
        grid=(8,),
        in_specs=[pl.BlockSpec((tokens[0].shape[0], columns), lambda i: (0, i))] * len(tokens)
        + [pl.BlockSpec((rows, columns), lambda i: (0, i))],
        out_specs=pl.BlockSpec((8, columns), lambda i: (0, i)),
        out_shape=jax.ShapeDtypeStruct((8, features), jnp.float32),
        compiler_params=pltpu.CompilerParams(vmem_limit_bytes=VMEM_BYTES),
    )(*tokens, feature)


def attention_kernel(
    place_ref,
    query_ref,
    up_ref,
    next_ref,
    keyval_ref,
    attended_ref,
    query_back_ref,
    keyval_back_ref,
    end_ref,
    attended_carry,
    query_carry,
):
    span = pl.program_id(0)
    last = pl.num_programs(0) - 1
    width = query_ref.shape[1]
    rows = lax.broadcasted_iota(jnp.int32, (SPAN, width), 0)
    here = pl.ds(pl.multiple_of(place_ref[span] * SPAN, SPAN), SPAN)
    after = pl.ds(pl.multiple_of(place_ref[span + 1] * SPAN, SPAN), SPAN)

    @pl.when(span == 0)
    def _():
        attended_carry[...] = jnp.zeros_like(attended_carry)
        query_carry[...] = jnp.zeros_like(query_carry)

    def shifted(ref, part):
        first = ref[here, :].astype(jnp.float32)
        following = next_ref[part * SPAN : (part + 1) * SPAN, :]
        second = jnp.where(span == last, following, ref[after, :]).astype(jnp.float32)
        joined = jnp.where(rows == SPAN - 1, first, second)
        return pltpu.roll(joined, 1, 0).astype(jnp.bfloat16)

    query = shifted(query_ref, 0)
    up = shifted(up_ref, 1)
    factor = 1.0 / math.sqrt(HEAD_DIM)
    heads = [slice(first, first + HEAD_DIM) for first in range(0, width, HEAD_DIM)]
    value_heads = [slice(width + head.start, width + head.stop) for head in heads]
    queries, ups = [query[:, head] for head in heads], [up[:, head] for head in heads]
    keys = [keyval_ref[:, head] for head in heads]
    values = [keyval_ref[:, head] for head in value_heads]
    scores = [dot(q, k, 1, 1) * factor for q, k in zip(queries, keys)]
    weight_grads = [dot(u, v, 1, 1) for u, v in zip(ups, values)]
    exponents = [jnp.exp(score - jnp.max(score, axis=-1, keepdims=True)) for score in scores]
    probabilities = [e * (1.0 / jnp.sum(e, axis=-1, keepdims=True)) for e in exponents]
    weights = [p.astype(jnp.bfloat16) for p in probabilities]
    inners = [
        jnp.sum(grad * p, axis=-1, keepdims=True) for grad, p in zip(weight_grads, probabilities)
    ]
    score_grads = [
        (p * (grad - inner) * factor).astype(jnp.bfloat16)
        for p, grad, inner in zip(probabilities, weight_grads, inners)
    ]
    attended_parts = [dot(w, v, 1, 0) for w, v in zip(weights, values)]
    query_parts = [dot(g, k, 1, 0) for g, k in zip(score_grads, keys)]
    key_grads = [dot(g, q, 0, 0).astype(jnp.bfloat16) for g, q in zip(score_grads, queries)]
    value_grads = [dot(w, u, 0, 0).astype(jnp.bfloat16) for w, u in zip(weights, ups)]
    for head, value_head, key_grad, value_grad in zip(heads, value_heads, key_grads, value_grads):
        keyval_back_ref[:, head] = key_grad
        keyval_back_ref[:, value_head] = value_grad
    for part, (parts, carry, out_ref) in enumerate(
        (
            (attended_parts, attended_carry, attended_ref),
            (query_parts, query_carry, query_back_ref),
        )
    ):
        turned = pltpu.roll(jnp.concatenate(parts, axis=1), SPAN - 1, 0)
        out_ref[...] = jnp.where(rows == SPAN - 1, turned, carry[...]).astype(jnp.bfloat16)
        carry[...] = turned
        end_ref[part * SPAN : (part + 1) * SPAN, :] = jnp.where(
            rows == SPAN - 1, 0.0, turned
        ).astype(jnp.bfloat16)


def attention(places, query, up, following, keyvals):
    tokens, width = query.shape
    spans = tokens // SPAN
    span_rows = keyvals.shape[0] // spans
    by_place = lambda i, places: (places[i], 0)
    like = lambda array: jax.ShapeDtypeStruct(array.shape, jnp.bfloat16)
    return pl.pallas_call(
        attention_kernel,
        grid_spec=pltpu.PrefetchScalarGridSpec(
            num_scalar_prefetch=1,
            grid=(spans,),
            in_specs=[
                whole(query.shape),
                whole(up.shape),
                whole(following.shape),
                pl.BlockSpec((span_rows, keyvals.shape[1]), by_place),
            ],
            out_specs=[
                pl.BlockSpec((SPAN, width), by_place),
                pl.BlockSpec((SPAN, width), by_place),
                pl.BlockSpec((span_rows, keyvals.shape[1]), by_place),
                whole(following.shape),
            ],
            scratch_shapes=[
                pltpu.VMEM((SPAN, width), jnp.float32),
                pltpu.VMEM((SPAN, width), jnp.float32),
            ],
        ),
        out_shape=[
            like(query),
            like(query),
            like(keyvals),
            like(following),
        ],
        compiler_params=pltpu.CompilerParams(vmem_limit_bytes=VMEM_BYTES),
    )(places, query, up, following, keyvals)


def per_device(
    residual, norm_gain, query_weight, keyval_weight, output_weight, neighbours, cotangent
):
    me, seq_count = lax.axis_index("seq"), lax.axis_size("seq")
    column, tp_count = lax.axis_index("tp"), lax.axis_size("tp")
    tokens_here, features = residual.shape
    local_width = query_weight.shape[1]
    neighbour_count, _, enc_width = neighbours.shape
    enc_rows = keyval_weight.shape[0]
    group_tokens = tokens_here * tp_count
    spans = group_tokens // SPAN
    seq_index = me.astype(jnp.int32).reshape(1)
    gain_row = norm_gain.reshape(1, features)
    token_shape = jax.ShapeDtypeStruct(residual.shape, jnp.bfloat16)

    weight_rows = query_weight.shape[0]
    padded = -(-enc_rows // 16) * 16
    padding = ((0, padded - enc_rows), (0, 0))
    query_shard = jnp.concatenate([query_weight, jnp.pad(keyval_weight[:, 0], padding)])[None]
    output_shard = jnp.concatenate([output_weight, jnp.pad(keyval_weight[:, 1], padding)])[None]
    flat_neighbours = neighbours.reshape(neighbour_count * R, enc_width)
    normed, turned = row_call(
        norm_kernel, seq_index, (residual, gain_row, cotangent), [token_shape, token_shape]
    )

    neighbours_beside = tp_swap(flat_neighbours, CORE)
    normed_beside, turned_beside = tp_swap(normed, CORE), tp_swap(turned, CORE)
    queries = jnp.concatenate([query_shard, seq_swap(query_shard, X_HIGH)])
    outputs = jnp.concatenate([output_shard, seq_swap(output_shard, X_HIGH)])
    queries, outputs, flat_neighbours = fence(
        [queries, outputs, flat_neighbours], [neighbours_beside, normed_beside, turned_beside]
    )
    neighbours_across = tp_swap(flat_neighbours, X_LOW)
    queries_near, queries_wrap = gather_first(queries, Z_NEAR, Z_WRAP)
    outputs_near, outputs_wrap = gather_first(outputs, Y_NEAR, Y_WRAP)
    queries_far = gather_second(
        halves(queries_near)[1], halves(queries_wrap)[0], Z_NEAR, Z_WRAP
    )
    outputs_far = gather_second(
        halves(outputs_near)[1], halves(outputs_wrap)[0], Y_NEAR, Y_WRAP
    )
    queries = jnp.concatenate([queries, queries_near, *queries_far, queries_wrap])
    outputs = jnp.concatenate([outputs, outputs_near, *outputs_far, outputs_wrap])

    neighbours_both = tp_swap(neighbours_across, CORE)
    queries, outputs, normed = fence([queries, outputs, normed], [neighbours_both])
    normed_across = tp_swap(normed, X_LOW)
    queries_near, queries_wrap = gather_first(queries, Y_NEAR, Y_WRAP)
    outputs_near, outputs_wrap = gather_first(outputs, Z_NEAR, Z_WRAP)

    group_neighbours = jnp.concatenate(
        [flat_neighbours, neighbours_across, neighbours_beside, neighbours_both]
    )
    normed_both = tp_swap(normed_across, CORE)
    group_normed = [normed, normed_across, normed_beside, normed_both]
    half = queries.shape[0] // 2
    *far, turned = block_steps(
        half,
        [(queries_wrap, 0), (queries_near, half), (outputs_wrap, 0), (outputs_near, half)],
        [],
        [turned],
        [normed_both, group_neighbours],
    )
    turned_across = tp_swap(turned, X_LOW)
    query_pieces = [
        queries,
        queries_near,
        seq_swap(far[0], Y_NEAR),
        seq_swap(far[1], Y_WRAP),
        queries_wrap,
    ]
    output_pieces = [
        outputs,
        outputs_near,
        seq_swap(far[2], Z_NEAR),
        seq_swap(far[3], Z_WRAP),
        outputs_wrap,
    ]
    early = weight_call(
        group_normed,
        [queries, queries_near, queries_wrap],
        weight_rows,
        half,
        lambda i: jnp.where(i < 4, i, i + 2),
        jnp.float32,
    )
    (turned_across,) = fence(
        [turned_across], [*query_pieces[2:4], *output_pieces[2:4], early[0]]
    )
    turned_both = tp_swap(turned_across, CORE)
    group_cotangent = [turned, turned_across, turned_beside, turned_both]
    full_keyval = compact(seq_index, query_pieces, output_pieces, weight_rows, enc_rows)
    keyvals = dot(group_neighbours, full_keyval, 1, 0).astype(jnp.bfloat16)
    query, full_query = weight_call(
        group_normed, query_pieces[2:4], weight_rows, half, lambda i: i + 4, jnp.bfloat16, early
    )
    attended_grad, full_output = weight_call(
        group_cotangent, output_pieces, weight_rows, half, lambda i: i, jnp.bfloat16
    )

    block = jnp.arange(spans, dtype=jnp.int32)
    mask = (block // (spans // tp_count)) ^ column.astype(jnp.int32)
    place = ((mask % 2) * 2 + mask // 2) * (spans // tp_count) + block % (spans // tp_count)
    places = jnp.concatenate([place, place[:1]])
    groups = LENGTH // group_tokens
    inside = [i for i in range(seq_count) if i % groups]
    first_row = place[0] * SPAN

    def first_block(value):
        return lax.dynamic_slice(value, (first_row, 0), (SPAN, local_width))

    following = lax.ppermute(
        jnp.concatenate([first_block(query), first_block(attended_grad)]),
        "seq",
        [(i, i - 1) for i in inside],
    )
    attended, query_back, keyval_back, ends = attention(
        places, query, attended_grad, following, keyvals
    )
    arrived = lax.ppermute(ends, "seq", [(i - 1, i) for i in inside])

    def with_previous(value, part):
        block = first_block(value) + arrived[part * SPAN : (part + 1) * SPAN]
        return lax.dynamic_update_slice(value, block, (first_row, 0))

    attended, query_back = with_previous(attended, 0), with_previous(query_back, 1)

    feature_part = dot(query_back, full_query, 1, 1).astype(jnp.bfloat16)
    feature_own, feature_beside = swap_half(feature_part)
    where_from = mask_of(jnp.arange(seq_count, dtype=jnp.int32) ^ me, True)
    gain_total = jnp.sum(column_sums(group_normed, feature_part), axis=0)
    gain_total = jnp.take(
        gain_total.reshape(seq_count, features // seq_count), where_from, axis=0
    )

    keyval_part = dot(group_neighbours, keyval_back, 0, 0).astype(jnp.bfloat16)
    mixed_part = dot(attended, full_output, 1, 1).astype(jnp.bfloat16)
    mixed_own, mixed_beside = swap_half(mixed_part)
    neighbour_part = dot(keyval_back, full_keyval, 1, 1).astype(jnp.bfloat16)
    neighbour_kept, neighbour_sent = half_sums(*swap_half(neighbour_part))
    extra_shape = jax.ShapeDtypeStruct((seq_count, padded, local_width), jnp.bfloat16)
    key_part, value_part = row_call(
        spread_kernel, seq_index, (keyval_part,), [extra_shape, extra_shape]
    )

    eighth = seq_count // 8
    sizes = [2 * eighth, 2 * eighth, eighth, eighth, 2 * eighth]
    query_own, query_near, query_low, query_high, query_wrap = grad_call(
        group_normed, query_back, key_part, sizes
    )
    output_own, output_near, output_low, output_high, output_wrap = grad_call(
        group_cotangent, attended, value_part, sizes
    )
    for swap, mask in (
        (tp_swap, CORE),
        (tp_swap, X_LOW),
        (seq_swap, X_HIGH),
        (seq_swap, Y_NEAR),
        (seq_swap, Y_WRAP),
        (seq_swap, Z_NEAR),
        (seq_swap, Z_WRAP),
    ):
        gain_total = gain_total + swap(gain_total, mask)
    gain_grad = gain_total.reshape(features) / norm_gain

    query_low, query_high, output_low, output_high, neighbour_sent = fence(
        [query_low, query_high, output_low, output_high, neighbour_sent],
        [gain_grad, mixed_beside, feature_beside],
    )
    mixed_kept, mixed_sent = half_sums(mixed_own, mixed_beside)
    feature_kept, feature_sent = half_sums(feature_own, feature_beside)
    query_low, query_high = seq_swap(query_low, Y_WRAP), seq_swap(query_high, Y_NEAR)
    output_low, output_high = seq_swap(output_low, Z_WRAP), seq_swap(output_high, Z_NEAR)
    neighbour_across = tp_swap(neighbour_sent, X_LOW)
    query_near, query_wrap, output_near, output_wrap, mixed_sent = block_steps(
        eighth,
        [],
        [
            (query_near, query_low, 0),
            (query_wrap, query_high, eighth),
            (output_near, output_low, 0),
            (output_wrap, output_high, eighth),
        ],
        [mixed_sent],
        [neighbour_across],
    )
    mixed_across = tp_swap(mixed_sent, X_LOW)
    feature_first, feature_last = halves(feature_sent)
    query_cut, output_cut, (feature_first, feature_last) = sum_and_split(
        [
            [query_own, seq_swap(query_near, Y_NEAR), seq_swap(query_wrap, Y_WRAP)],
            [output_own, seq_swap(output_near, Z_NEAR), seq_swap(output_wrap, Z_WRAP)],
        ],
        [2, 2, 2, 2],
        [feature_first, feature_last],
        [mixed_across],
    )
    query_own, query_near, query_far, query_wrap = query_cut
    output_own, output_near, output_far, output_wrap = output_cut
    feature_first = tp_swap(feature_first, X_LOW)
    query_wrap, output_wrap, feature_last = block_steps(
        2,
        [],
        [
            (query_wrap, seq_swap(query_far, Z_NEAR), 0),
            (output_wrap, seq_swap(output_far, Y_NEAR), 0),
        ],
        [feature_last],
        [feature_first],
    )
    feature_last = tp_swap(feature_last, X_LOW)
    feature_across = jnp.concatenate([feature_first, feature_last])
    queries = narrow_sum(query_own, seq_swap(query_near, Z_NEAR), seq_swap(query_wrap, Z_WRAP))
    outputs = narrow_sum(
        output_own, seq_swap(output_near, Y_NEAR), seq_swap(output_wrap, Y_WRAP)
    )
    outputs, queries = fence([outputs, queries], [feature_last])
    output_total = f32_sum(outputs[0], seq_swap(outputs[1], X_HIGH))
    query_total = f32_sum(queries[0], seq_swap(queries[1], X_HIGH))
    output_grad, query_grad = output_total[:weight_rows], query_total[:weight_rows]
    keyval_grad = jnp.stack(
        [
            query_total[weight_rows : weight_rows + enc_rows],
            output_total[weight_rows : weight_rows + enc_rows],
        ],
        axis=1,
    )

    (layer_output,) = row_call(
        output_kernel, seq_index, (residual, mixed_kept, mixed_across), [token_shape]
    )
    (residual_grad,) = row_call(
        residual_kernel,
        seq_index,
        (residual, gain_row, cotangent, feature_kept, feature_across),
        [token_shape],
        [pltpu.VMEM(residual.shape, jnp.float32)],
    )
    neighbour_grad = (
        f32_sum(neighbour_kept, neighbour_across).astype(jnp.bfloat16).reshape(neighbours.shape)
    )
    return (
        layer_output,
        residual_grad,
        neighbour_grad,
        gain_grad,
        query_grad,
        keyval_grad,
        output_grad,
    )


def solution(mesh):
    in_specs = (
        P(("seq", "tp"), None),
        P(),
        P("seq", "tp"),
        P("seq", None, "tp"),
        P("seq", "tp"),
        P(("seq", "tp"), None, None),
        P(("seq", "tp"), None),
    )
    out_specs = (
        P(("seq", "tp"), None),
        P(("seq", "tp"), None),
        P(("seq", "tp"), None, None),
        P(),
        P("seq", "tp"),
        P("seq", None, "tp"),
        P("seq", "tp"),
    )
    return jax.shard_map(
        per_device, mesh=mesh, in_specs=in_specs, out_specs=out_specs, check_vma=False
    )
```
